256 devices in a mesh: rows: 32 (over z, y_lo, core), pairs: 8 (over y_hi, x).
Axes of the slice: x: 4, y: 4 (y_hi: 2, y_lo: 2; y = y_hi * 2 + y_lo), z: 8, core: 2. Of those that a mesh axis runs over, the one named last changes fastest.
Arguments:
- sample: float32 [8192, 4096], P('rows', 'pairs'), may hold values from -6 to 6
- column_scale: float32 [4096], P('pairs'), may hold values from 0.3 to 3
- inner_order: int32 [4, 256], replicated, may hold values from 0 to 255, each once within a row
Outputs:
- rotated: float32 [8192, 4096], P('rows', 'pairs')
- basis: float32 [4096, 4096], P('rows', 'pairs')
The draws below stay inside these ranges and needn't reach their ends.
Inputs may be any that keep to these rules, and one draw needn't show every extreme that they name: `inner_order`: each row is a permutation of 0 to 255.
All inputs are finite; a program needn't handle non-finite values.
Results may differ from the reference program's by a relative error of at most 0.0003.
Values sent between devices are 32-bit elements; how exact they have to be, the bound alone decides.
No kernel may reach another device: no remote copies, remote signals or barrier semaphores. Data moves between devices by JAX's collectives and lax.ppermute only.
A program may use at most 64 MiB of HBM per device.

```python
import math
import jax
import jax.numpy as jnp
import numpy as np
from jax import lax

BLOCK = 128
W = 4096
PAIRS = 16
TOTAL_ROWS = 8192
STEPS = 4
ROUNDS = 8


def levels(key, shape, pieces, low, largest):
    def one(dim, blocks):
        steps = jax.random.uniform(jax.random.fold_in(jax.random.fold_in(key, 6), dim), (blocks,), jnp.float32, low / len(pieces), largest / len(pieces))
        return jnp.repeat(jnp.exp(steps), shape[dim] // blocks).reshape((-1,) + (1,) * (len(shape) - dim - 1))

    gain = one(*pieces[0])
    for cut in pieces[1:]:
        gain = gain * one(*cut)
    return gain


def normal_values(stream_key, dims, scale, bound, split=(), kind=jnp.bfloat16):
    result = scale * jax.random.normal(stream_key, dims, jnp.float32)
    if split:
        result = result * levels(stream_key, dims, split, -0.22, 0.18)
    return jnp.clip(result, -bound, bound).astype(kind)


def setup_inputs(seed: int = 0) -> dict:
    streams_of = jax.random.split(jax.random.key(seed), 4)
    sample = normal_values(streams_of[0], (TOTAL_ROWS, W), 1.0, 6.0, ((0, 32), (1, 8)), jnp.float32)
    column_scale = jnp.clip(jnp.exp(math.log(3.0) - 2.3025851 * jax.random.uniform(streams_of[1], (W,), jnp.float32) ** levels(streams_of[1], (W,), ((0, 8),), -0.2, 0.2)), 0.3, 3.0)
    inner_order = jax.vmap(lambda own: jax.random.permutation(own, 2 * BLOCK))(jax.random.split(streams_of[2], STEPS)).reshape((STEPS, 2 * BLOCK)).astype(jnp.int32)
    return dict(sample=sample, column_scale=column_scale, inner_order=inner_order)


def pair_tables(n, count):
    m = n - 1
    partner = np.zeros((count, n), np.int32)
    slot = np.zeros((count, n), np.int32)
    role = np.zeros((count, n), np.float32)
    firsts = np.zeros((count, n // 2), np.int32)
    seconds = np.zeros((count, n // 2), np.int32)
    for r in range(count):
        left_ids = [m] + [(r + i) % m for i in range(1, n // 2)]
        right_ids = [r] + [(r - i) % m for i in range(1, n // 2)]
        for k in range(n // 2):
            a = left_ids[k]
            b = right_ids[k]
            partner[r, a] = b
            partner[r, b] = a
            slot[r, a] = k
            slot[r, b] = k
            role[r, a] = -1.0
            role[r, b] = 1.0
            firsts[r, k] = a
            seconds[r, k] = b
    return (partner, slot, role, firsts, seconds)

def jacobi(gram_mat, ordering, count):
    n = gram_mat.shape[0]
    partner, slot, role, firsts, seconds = pair_tables(n, count)
    partner = jnp.asarray(partner)
    slot = jnp.asarray(slot)
    role = jnp.asarray(role).astype(gram_mat.dtype)
    firsts = jnp.asarray(firsts)
    seconds = jnp.asarray(seconds)
    ordering = ordering.astype(jnp.int32)
    state_g = gram_mat[ordering][:, ordering]
    state_q = jnp.eye(n, dtype=gram_mat.dtype)

    def round_fn(r, state):
        g, q = state
        across = partner[r]
        first = firsts[r]
        second = seconds[r]
        diagonal = jnp.diagonal(g)
        gpp = diagonal[first]
        gqq = diagonal[second]
        cross = g[first, second]
        d = gqq - gpp
        root = jnp.sqrt(d * d + 4.0 * cross * cross)
        t = 2.0 * cross * d / ((jnp.abs(d) + root) * root + 1e-06 * (gpp + gqq) * (gpp + gqq))
        c = 1.0 / jnp.sqrt(1.0 + t * t)
        s = t * c
        c_col = c[slot[r]]
        s_col = s[slot[r]] * role[r]
        g = c_col[None, :] * g + s_col[None, :] * g[:, across]
        g = c_col[:, None] * g + s_col[:, None] * g[across, :]
        q = c_col[None, :] * q + s_col[None, :] * q[:, across]
        return (g, q)
    state_g, state_q = lax.fori_loop(0, count, round_fn, (state_g, state_q))
    restore = jnp.zeros((n,), jnp.int32).at[ordering].set(jnp.arange(n, dtype=jnp.int32))
    return (state_g[restore][:, restore], state_q[restore][:, restore])

def reference(sample, column_scale, inner_order):
    data = sample * column_scale[None, :]
    width = data.shape[1]
    basis = jnp.eye(width, dtype=data.dtype)
    joined = data.reshape(TOTAL_ROWS, PAIRS, 2 * BLOCK)
    basis_join = basis.reshape(width, PAIRS, 2 * BLOCK)
    for section in range(STEPS):
        if section > 0:
            joined = jnp.concatenate([jnp.roll(joined[..., :BLOCK], 1, axis=1), jnp.roll(joined[..., BLOCK:], -1, axis=1)], -1)
            basis_join = jnp.concatenate([jnp.roll(basis_join[..., :BLOCK], 1, axis=1), jnp.roll(basis_join[..., BLOCK:], -1, axis=1)], -1)
        gram = jnp.einsum('rpi,rpj->pij', joined, joined, precision=lax.Precision.HIGHEST)
        rotations = jax.vmap(lambda g: jacobi(g, inner_order[section], ROUNDS)[1])(gram)
        joined = jnp.einsum('rpi,pij->rpj', joined, rotations, precision=lax.Precision.HIGHEST)
        basis_join = jnp.einsum('rpi,pij->rpj', basis_join, rotations, precision=lax.Precision.HIGHEST)
    return (joined.reshape(TOTAL_ROWS, width), basis_join.reshape(width, width))
```

```python
import functools

import jax
import jax.numpy as jnp
import numpy as np
from jax import lax
from jax.experimental import pallas as pl
from jax.experimental.pallas import tpu as pltpu
from jax.sharding import PartitionSpec as P

BLOCK = 128
N = 2 * BLOCK
W = 4096
STEPS = 4
ROUNDS = 8
HIGHEST = lax.Precision.HIGHEST


def arrangement(r):
    m = N - 1
    first = [m] + [(r + i) % m for i in range(1, BLOCK)]
    second = [r % m] + [(r - i) % m for i in range(1, BLOCK)]
    return np.array(first + second)


def exact_dot(left, right):
    return jnp.dot(left, right, precision=HIGHEST, preferred_element_type=jnp.float32)


def turn(p, q, c, s):
    return c * p - s * q, s * p + c * q


def advance(p, q, axis):
    at = lax.broadcasted_iota(jnp.int32, p.shape, axis)
    p_back = pltpu.roll(p, BLOCK - 1, axis)
    q_on = pltpu.roll(q, 1, axis)
    new_p = jnp.where(at == 0, p, jnp.where(at == BLOCK - 1, q, p_back))
    new_q = jnp.where(at == 0, p_back, q_on)
    return new_p, new_q


def solve_kernel(g00, g01, g11, rows_ref, cols_ref, x0, x1, y0, y1, q_out, a, b, c_, d_, qp, qq):
    lane = lax.broadcasted_iota(jnp.int32, (N, N), 1).astype(jnp.float32)
    sub = lax.broadcasted_iota(jnp.int32, (N, N), 0).astype(jnp.float32)
    take = jnp.where(sub == rows_ref[0:1, :], 1.0, 0.0).astype(jnp.float32)
    take_t = jnp.where(lane == cols_ref[:, 0:1], 1.0, 0.0).astype(jnp.float32)
    back_t = jnp.where(lane == cols_ref[:, 1:2], 1.0, 0.0).astype(jnp.float32)
    cross = g01[...]
    gram = jnp.concatenate(
        [
            jnp.concatenate([g00[...], cross], axis=1),
            jnp.concatenate([cross.T, g11[...]], axis=1),
        ],
        axis=0,
    )
    placed = exact_dot(take_t, exact_dot(gram, take))
    a[...] = placed[:BLOCK, :BLOCK]
    b[...] = placed[:BLOCK, BLOCK:]
    c_[...] = placed[BLOCK:, :BLOCK]
    d_[...] = placed[BLOCK:, BLOCK:]
    qp[...] = take[:, :BLOCK]
    qq[...] = take[:, BLOCK:]
    i0 = lax.broadcasted_iota(jnp.int32, (BLOCK, BLOCK), 0)
    i1 = lax.broadcasted_iota(jnp.int32, (BLOCK, BLOCK), 1)

    def round_fn(r, carry):
        on = i0 == i1
        ga, gb, gc, gd = a[...], b[...], c_[...], d_[...]

        def diagonal(m):
            return jnp.sum(jnp.where(on, m, 0.0), axis=0, keepdims=True)

        gpp, cr, gqq = diagonal(ga), diagonal(gb), diagonal(gd)
        d = gqq - gpp
        root = jnp.sqrt(d * d + 4.0 * cr * cr)
        t = 2.0 * cr * d / ((jnp.abs(d) + root) * root + 1e-06 * (gpp + gqq) * (gpp + gqq))
        c = 1.0 / jnp.sqrt(1.0 + t * t)
        s = t * c
        c_col = jnp.sum(jnp.where(on, c, 0.0), axis=1, keepdims=True)
        s_col = jnp.sum(jnp.where(on, s, 0.0), axis=1, keepdims=True)
        ga, gb = advance(*turn(ga, gb, c, s), 1)
        gc, gd = advance(*turn(gc, gd, c, s), 1)
        ga, gc = advance(*turn(ga, gc, c_col, s_col), 0)
        gb, gd = advance(*turn(gb, gd, c_col, s_col), 0)
        a[...], b[...], c_[...], d_[...] = ga, gb, gc, gd
        qp[...], qq[...] = advance(*turn(qp[...], qq[...], c, s), 1)
        return carry

    lax.fori_loop(0, ROUNDS, round_fn, 0)
    q = exact_dot(jnp.concatenate([qp[...], qq[...]], axis=1), back_t)
    q_out[...] = q
    x = jnp.concatenate([x0[...], x1[...]], axis=1)
    y = exact_dot(x, q)
    y0[...] = y[:, :BLOCK]
    y1[...] = y[:, BLOCK:]


def solve(g00, g01, g11, rows, cols, x0, x1):
    half = jax.ShapeDtypeStruct(x0.shape, jnp.float32)
    block = pltpu.VMEM((BLOCK, BLOCK), jnp.float32)
    tall = pltpu.VMEM((N, BLOCK), jnp.float32)
    vmem = pl.BlockSpec(memory_space=pltpu.VMEM)
    return pl.pallas_call(
        solve_kernel,
        out_shape=(half, half, jax.ShapeDtypeStruct((N, N), jnp.float32)),
        in_specs=[vmem] * 7,
        out_specs=(vmem,) * 3,
        scratch_shapes=[block] * 4 + [tall] * 2,
        compiler_params=pltpu.CompilerParams(vmem_limit_bytes=32 * 2**20),
    )(g00, g01, g11, rows, cols, x0, x1)


def chip_groups(size):
    return [list(range(core, size, 2)) for core in range(2)]


def sum_over_chips(part):
    groups = chip_groups(lax.axis_size("rows"))
    n = len(groups[0])
    slices = part.reshape(n, -1, BLOCK)
    mine = lax.all_to_all(slices, "rows", 0, 0, axis_index_groups=groups).sum(0)
    spread = jnp.broadcast_to(mine[None], (n,) + mine.shape)
    whole = lax.all_to_all(spread, "rows", 0, 0, axis_index_groups=groups)
    return whole.reshape(part.shape)


def other_core(x):
    return lax.ppermute(x, "rows", [(i, i ^ 1) for i in range(lax.axis_size("rows"))])


def along_pairs(x, sign):
    n_rows, n_pairs = lax.axis_size("rows"), lax.axis_size("pairs")
    route = []
    for r in range(n_rows):
        step = sign if r % 2 else -sign
        for p in range(n_pairs):
            route.append((r * n_pairs + p, r * n_pairs + (p + step) % n_pairs))
    return lax.ppermute(x, ("rows", "pairs"), route)


def body(sample, column_scale, inner_order):
    row, col = lax.axis_index("rows"), lax.axis_index("pairs")
    core = row % 2
    first = core == 0
    data = sample * column_scale[None, :]
    rows = data.shape[0]
    left, right = data[:, :N], data[:, N:]
    own = jnp.where(first, left, right)
    joined = jnp.concatenate([own, other_core(jnp.where(first, right, left))], axis=0)
    height = W // lax.axis_size("rows")
    ids = jnp.arange(height, dtype=jnp.int32)
    row_ids = jnp.concatenate([ids + row * height, ids + (row ^ 1) * height])[:, None]
    col_ids = jnp.arange(BLOCK, dtype=jnp.int32)[None, :] + (2 * col + core) * N
    shift = core * BLOCK
    x0 = jnp.concatenate(
        [
            jnp.where(first, joined[:, :BLOCK], joined[:, BLOCK:]),
            jnp.where(row_ids == col_ids + shift, 1.0, 0.0).astype(jnp.float32),
        ]
    )
    x1 = jnp.concatenate(
        [
            jnp.where(first, joined[:, BLOCK:], joined[:, :BLOCK]),
            jnp.where(row_ids == col_ids + (BLOCK - shift), 1.0, 0.0).astype(jnp.float32),
        ]
    )
    order = ((inner_order + shift) % N).astype(jnp.float32)
    table = np.concatenate([np.eye(N)[:, arrangement(0)], np.eye(N)[:, arrangement(ROUNDS)]], 1)
    table = jnp.asarray(table.astype(np.float32))
    along = exact_dot(order, table).reshape(STEPS, 2, N)
    down = lax.dot_general(
        table, order, (((0,), (1,)), ((), ())), precision=HIGHEST
    ).reshape(2, N, STEPS)
    data_rows = 2 * rows
    for step in range(STEPS):
        d0, d1 = x0[:data_rows], x1[:data_rows]
        dot_t = functools.partial(
            lax.dot_general, dimension_numbers=(((0,), (0,)), ((), ())), precision=HIGHEST
        )
        if step == 0:
            sums = sum_over_chips(jnp.concatenate([dot_t(d0, d0), dot_t(d0, d1), dot_t(d1, d1)]))
            g00, g01, g11 = sums[:BLOCK], sums[BLOCK : 2 * BLOCK], sums[2 * BLOCK :]
        else:
            g01 = sum_over_chips(dot_t(d0, d1))
        y0, y1, q = solve(g00, g01, g11, along[step], down[:, :, step].T, x0, x1)
        x0, x1 = y0, y1
        if step == STEPS - 1:
            break
        gram = jnp.concatenate(
            [jnp.concatenate([g00, g01], 1), jnp.concatenate([g01.T, g11], 1)], 0
        )
        half = exact_dot(gram, q)
        g00 = dot_t(q[:, :BLOCK], half[:, :BLOCK])
        g11 = dot_t(q[:, BLOCK:], half[:, BLOCK:])
        if step % 2 == 0:
            x1 = jnp.concatenate(
                [along_pairs(x1[:data_rows], 1), along_pairs(x1[data_rows:], 1)]
            )
            g11 = along_pairs(g11, 1)
        else:
            x0 = jnp.concatenate(
                [along_pairs(x0[:data_rows], -1), along_pairs(x0[data_rows:], -1)]
            )
            g00 = along_pairs(g00, -1)
    mine0 = jnp.concatenate([x0[:rows], x0[data_rows : data_rows + height]])
    mine1 = jnp.concatenate([x1[:rows], x1[data_rows : data_rows + height]])
    theirs = jnp.concatenate(
        [x0[rows:data_rows], x0[data_rows + height :], x1[rows:data_rows], x1[data_rows + height :]]
    )
    got = other_core(theirs)
    got0, got1 = got[: rows + height], got[rows + height :]
    whole = jnp.where(
        first,
        jnp.concatenate([got1, got0, mine0, mine1], 1),
        jnp.concatenate([mine1, mine0, got0, got1], 1),
    )
    return whole[:rows], whole[rows:]


def solution(mesh):
    return jax.shard_map(
        body,
        mesh=mesh,
        in_specs=(P("rows", "pairs"), P("pairs"), P()),
        out_specs=(P("rows", "pairs"), P("rows", "pairs")),
        check_vma=False,
    )
```

```python
import functools

import jax
import jax.numpy as jnp
import numpy as np
from jax import lax
from jax.experimental import pallas as pl
from jax.experimental.pallas import tpu as pltpu
from jax.sharding import PartitionSpec as P

BLOCK = 128
N = 2 * BLOCK
W = 4096
STEPS = 4
ROUNDS = 8
HIGHEST = lax.Precision.HIGHEST
VMEM = pl.BlockSpec(memory_space=pltpu.VMEM)


def arrangement(r):
    m = N - 1
    first = [m] + [(r + i) % m for i in range(1, BLOCK)]
    second = [r % m] + [(r - i) % m for i in range(1, BLOCK)]
    return np.array(first + second)


def shape(*dims):
    return jax.ShapeDtypeStruct(dims, jnp.float32)


def call(kernel, out_shape, scratch, *operands):
    return pl.pallas_call(
        kernel,
        out_shape=out_shape,
        in_specs=[VMEM] * len(operands),
        out_specs=jax.tree.map(lambda _: VMEM, out_shape),
        scratch_shapes=scratch,
        compiler_params=pltpu.CompilerParams(vmem_limit_bytes=40 * 2**20),
    )(*operands)


def solve_scratch(count):
    block = pltpu.VMEM((count, BLOCK, BLOCK), jnp.float32)
    tall = pltpu.VMEM((count, N, BLOCK), jnp.float32)
    return [block] * 4 + [tall] * 2


def dot(left, right):
    return jnp.dot(left, right, precision=HIGHEST, preferred_element_type=jnp.float32)


def dot_t(left, right):
    return lax.dot_general(
        left,
        right,
        (((0,), (0,)), ((), ())),
        precision=HIGHEST,
        preferred_element_type=jnp.float32,
    )


def beside(*parts):
    return jnp.concatenate(parts, axis=1)


def joined(g00, g01, g11):
    return jnp.concatenate([beside(g00, g01), beside(g01.T, g11)], axis=0)


def turn(p, q, c, s):
    return c * p - s * q, s * p + c * q


def advance(p, q, axis):
    at = lax.broadcasted_iota(jnp.int32, p.shape, axis)
    p_back = pltpu.roll(p, BLOCK - 1, axis)
    q_on = pltpu.roll(q, 1, axis)
    new_p = jnp.where(at == 0, p, jnp.where(at == BLOCK - 1, q, p_back))
    new_q = jnp.where(at == 0, p_back, q_on)
    return new_p, new_q


def solves(grams, along, down, scratch):
    a, b, c_, d_, qp, qq = scratch
    lane = lax.broadcasted_iota(jnp.int32, (N, N), 1).astype(jnp.float32)
    sub = lax.broadcasted_iota(jnp.int32, (N, N), 0).astype(jnp.float32)
    take = jnp.where(sub == along[0:1, :], 1.0, 0.0).astype(jnp.float32)
    take_t = jnp.where(lane == down[:, 0:1], 1.0, 0.0).astype(jnp.float32)
    back_t = jnp.where(lane == down[:, 1:2], 1.0, 0.0).astype(jnp.float32)
    for k, gram in enumerate(grams):
        placed = dot(take_t, dot(gram, take))
        a[k] = placed[:BLOCK, :BLOCK]
        b[k] = placed[:BLOCK, BLOCK:]
        c_[k] = placed[BLOCK:, :BLOCK]
        d_[k] = placed[BLOCK:, BLOCK:]
        qp[k] = take[:, :BLOCK]
        qq[k] = take[:, BLOCK:]
    i0 = lax.broadcasted_iota(jnp.int32, (BLOCK, BLOCK), 0)
    i1 = lax.broadcasted_iota(jnp.int32, (BLOCK, BLOCK), 1)

    def round_fn(r, carry):
        on = i0 == i1

        def diagonal(m):
            return jnp.sum(jnp.where(on, m, 0.0), axis=0, keepdims=True)

        for k in range(len(grams)):
            ga, gb, gc, gd = a[k], b[k], c_[k], d_[k]
            gpp, cr, gqq = diagonal(ga), diagonal(gb), diagonal(gd)
            d = gqq - gpp
            root = jnp.sqrt(d * d + 4.0 * cr * cr)
            t = 2.0 * cr * d / ((jnp.abs(d) + root) * root + 1e-06 * (gpp + gqq) * (gpp + gqq))
            c = 1.0 / jnp.sqrt(1.0 + t * t)
            s = t * c
            c_col = jnp.sum(jnp.where(on, c, 0.0), axis=1, keepdims=True)
            s_col = jnp.sum(jnp.where(on, s, 0.0), axis=1, keepdims=True)
            ga, gb = advance(*turn(ga, gb, c, s), 1)
            gc, gd = advance(*turn(gc, gd, c, s), 1)
            ga, gc = advance(*turn(ga, gc, c_col, s_col), 0)
            gb, gd = advance(*turn(gb, gd, c_col, s_col), 0)
            a[k], b[k], c_[k], d_[k] = ga, gb, gc, gd
            qp[k], qq[k] = advance(*turn(qp[k], qq[k], c, s), 1)
        return carry

    lax.fori_loop(0, ROUNDS, round_fn, 0)
    return [dot(beside(qp[k], qq[k]), back_t) for k in range(len(grams))]


def gram_kernel(own, other, out):
    x = jnp.concatenate([own[...], other[...]], axis=0)
    x0, x1 = x[:, :BLOCK], x[:, BLOCK:]
    out[0], out[1], out[2] = dot_t(x0, x0), dot_t(x0, x1), dot_t(x1, x1)


def mixed_kernel(x, near, out):
    out[...] = dot_t(x[...], near[...])


def first_kernel(sums, along, down, q_out, ship, *scratch):
    gram = joined(sums[0], sums[1], sums[2])
    (q,) = solves([gram], along[...], down[...], scratch)
    q_out[...] = q
    q1 = q[:, BLOCK:]
    ship[:N] = q1
    ship[N:] = dot_t(q1, dot(gram, q1))


def keep_kernel(sums, q, x, g00, kept):
    q0 = q[:, :BLOCK]
    kept[...] = dot(x[...], q0)
    g00[...] = dot_t(q0, dot(joined(sums[0], sums[1], sums[2]), q0))


def second_kernel(mixed, q, ship, g00, kept, near, along, down, x0, x1, gram_out, q_out, *scratch):
    q1 = ship[:N]
    cross = dot_t(q[:, :BLOCK], dot(mixed[...], q1))
    gram = joined(g00[...], cross, ship[N:])
    gram_out[...] = gram
    (turned,) = solves([gram], along[...], down[...], scratch)
    q_out[...] = turned
    y = dot(beside(kept[...], dot(near[...], q1)), turned)
    x0[...] = y[:, :BLOCK]
    x1[...] = y[:, BLOCK:]


def turned_kernel(gram, q, out):
    g = dot_t(q[...], dot(gram[...], q[...]))
    out[0], out[1], out[2] = g[:BLOCK, :BLOCK], g[:BLOCK, BLOCK:], g[BLOCK:, BLOCK:]


def cross_kernel(far0, x0, x1, near1, out):
    f0, s0, s1, n1 = far0[...], x0[...], x1[...], near1[...]
    out[0] = dot_t(f0, s1)
    out[1] = dot_t(s0, n1)
    out[2] = dot_t(f0, s0)
    out[3] = dot_t(f0, n1)
    out[4] = dot_t(s1, n1)


def last_kernel(
    sums, inner, far00, near11, far0, x0, x1, near1, along2, down2, along3, down3, out, *scratch
):
    gram_a = joined(far00[...], sums[0], inner[2])
    gram_b = joined(inner[0], sums[1], near11[...])
    qa, qb = solves([gram_a, gram_b], along2[...], down2[...], scratch)
    qa, qb = qa[:, :BLOCK], qb[:, BLOCK:]
    mixed = jnp.concatenate([beside(sums[2], sums[3]), beside(inner[1].T, sums[4])], axis=0)
    gram = joined(
        dot_t(qa, dot(gram_a, qa)), dot_t(qa, dot(mixed, qb)), dot_t(qb, dot(gram_b, qb))
    )
    (q,) = solves([gram], along3[...], down3[...], scratch)
    ya = dot(beside(far0[...], x1[...]), qa)
    yb = dot(beside(x0[...], near1[...]), qb)
    out[...] = dot(beside(ya, yb), q)


def chip_groups(size):
    return [list(range(core, size, 2)) for core in range(2)]


def sum_slices(part):
    groups = chip_groups(lax.axis_size("rows"))
    n = len(groups[0])
    return lax.all_to_all(
        part.reshape(n, -1, part.shape[-1]), "rows", 0, 0, axis_index_groups=groups
    ).sum(0)


def all_slices(mine, dims):
    groups = chip_groups(lax.axis_size("rows"))
    spread = jnp.broadcast_to(mine[None], (len(groups[0]),) + mine.shape)
    return lax.all_to_all(spread, "rows", 0, 0, axis_index_groups=groups).reshape(dims)


def other_core(x):
    return lax.ppermute(x, "rows", [(i, i ^ 1) for i in range(lax.axis_size("rows"))])


def along_pairs(x, sign):
    n_rows, n_pairs = lax.axis_size("rows"), lax.axis_size("pairs")
    route = []
    for r in range(n_rows):
        step = sign if r % 2 else -sign
        for p in range(n_pairs):
            route.append((r * n_pairs + p, r * n_pairs + (p + step) % n_pairs))
    return lax.ppermute(x, ("rows", "pairs"), route)


def body(sample, column_scale, inner_order):
    row, col = lax.axis_index("rows"), lax.axis_index("pairs")
    core = row % 2
    first = core == 0
    n_pairs = lax.axis_size("pairs")
    data = sample * column_scale[None, :]
    rows = data.shape[0]
    left, right = data[:, :N], data[:, N:]
    own = jnp.where(first, left, beside(right[:, BLOCK:], right[:, :BLOCK]))
    send = jnp.where(first, beside(right[:, BLOCK:], right[:, :BLOCK]), left)
    got = other_core(send)
    x = jnp.concatenate([own, got], axis=0)
    near = along_pairs(x, 1)
    near_col = (col + jnp.where(first, 1, -1)) % n_pairs

    height = W // lax.axis_size("rows")
    ids = jnp.arange(height, dtype=jnp.int32)
    row_ids = jnp.concatenate([ids + row * height, ids + (row ^ 1) * height])[:, None]
    places = (jnp.arange(N, dtype=jnp.int32)[None, :] + core * BLOCK) % N + core * N

    def with_basis(values, at):
        unit = jnp.where(row_ids == places + 2 * N * at, 1.0, 0.0).astype(jnp.float32)
        return jnp.concatenate([values, unit])

    order = ((inner_order + core * BLOCK) % N).astype(jnp.float32)
    table = np.concatenate([np.eye(N)[:, arrangement(0)], np.eye(N)[:, arrangement(ROUNDS)]], 1)
    table = jnp.asarray(table.astype(np.float32))
    along = dot(order, table).reshape(STEPS, 2, N)
    down = dot_t(table, order.T).reshape(2, N, STEPS)
    down = [down[:, :, s].T for s in range(STEPS)]

    blocks = (3, BLOCK, BLOCK)
    sums = sum_slices(call(gram_kernel, shape(*blocks), [], own, got).reshape(-1, BLOCK))
    mixed = call(mixed_kernel, shape(N, N), [], x, near)
    mixed = sum_slices(mixed)
    sums = all_slices(sums, blocks)
    mixed = all_slices(mixed, (N, N))

    x, near = with_basis(x, col), with_basis(near, near_col)
    total = x.shape[0]
    q, ship = call(
        first_kernel,
        (shape(N, N), shape(N + BLOCK, BLOCK)),
        solve_scratch(1),
        sums,
        along[0],
        down[0],
    )
    ship = along_pairs(ship, 1)
    g00, kept = call(keep_kernel, (shape(BLOCK, BLOCK), shape(total, BLOCK)), [], sums, q, x)
    half = shape(total, BLOCK)
    x0, x1, gram, q = call(
        second_kernel,
        (half, half, shape(N, N), shape(N, N)),
        solve_scratch(1),
        mixed,
        q,
        ship,
        g00,
        kept,
        near,
        along[1],
        down[1],
    )

    both = 2 * rows
    far0, near1 = along_pairs(x0[:both], -1), along_pairs(x1[:both], 1)
    cross = call(
        cross_kernel, shape(5, BLOCK, BLOCK), [], far0, x0[:both], x1[:both], near1
    )
    sums = sum_slices(cross.reshape(-1, BLOCK))
    inner = call(turned_kernel, shape(3, BLOCK, BLOCK), [], gram, q)
    far_rest = along_pairs(jnp.concatenate([x0[both:], inner[0]]), -1)
    near_rest = along_pairs(jnp.concatenate([x1[both:], inner[2]]), 1)
    sums = all_slices(sums, (5, BLOCK, BLOCK))
    cut = 2 * height
    far0 = jnp.concatenate([far0, far_rest[:cut]])
    near1 = jnp.concatenate([near1, near_rest[:cut]])
    y = call(
        last_kernel,
        shape(total, N),
        solve_scratch(2),
        sums,
        inner,
        far_rest[cut:],
        near_rest[cut:],
        far0,
        x0,
        x1,
        near1,
        along[2],
        down[2],
        along[3],
        down[3],
    )
    mine = jnp.concatenate([y[:rows], y[both : both + height]])
    theirs = jnp.concatenate([y[rows:both], y[both + height :]])
    got = other_core(theirs)

    def ordered(part, swapped):
        return jnp.where(swapped, beside(part[:, BLOCK:], part[:, :BLOCK]), part)

    mine, got = ordered(mine, core == 1), ordered(got, core == 0)
    whole = jnp.where(first, beside(got, mine), beside(mine, got))
    return whole[:rows], whole[rows:]


def solution(mesh):
    return jax.shard_map(
        body,
        mesh=mesh,
        in_specs=(P("rows", "pairs"), P("pairs"), P()),
        out_specs=(P("rows", "pairs"), P("rows", "pairs")),
        check_vma=False,
    )
```

```python
import functools

import jax
import jax.numpy as jnp
import numpy as np
from jax import lax
from jax.experimental import pallas as pl
from jax.experimental.pallas import tpu as pltpu
from jax.sharding import PartitionSpec as P

BLOCK = 128
N = 2 * BLOCK
W = 4096
STEPS = 4
ROUNDS = 8
HIGHEST = lax.Precision.HIGHEST
VMEM = pl.BlockSpec(memory_space=pltpu.VMEM)


def arrangement(r):
    m = N - 1
    first = [m] + [(r + i) % m for i in range(1, BLOCK)]
    second = [r % m] + [(r - i) % m for i in range(1, BLOCK)]
    return np.array(first + second)


def shape(*dims):
    return jax.ShapeDtypeStruct(dims, jnp.float32)


def call(kernel, out_shape, scratch, *operands):
    return pl.pallas_call(
        kernel,
        out_shape=out_shape,
        in_specs=[VMEM] * len(operands),
        out_specs=jax.tree.map(lambda _: VMEM, out_shape),
        scratch_shapes=scratch,
        compiler_params=pltpu.CompilerParams(vmem_limit_bytes=40 * 2**20),
    )(*operands)


def solve_scratch(count):
    block = pltpu.VMEM((2, count, BLOCK + 16, BLOCK), jnp.float32)
    return [block] * 8


def dot(left, right):
    return jnp.dot(left, right, precision=HIGHEST, preferred_element_type=jnp.float32)


def dot_t(left, right):
    return lax.dot_general(
        left,
        right,
        (((0,), (0,)), ((), ())),
        precision=HIGHEST,
        preferred_element_type=jnp.float32,
    )


def beside(*parts):
    return jnp.concatenate(parts, axis=1)


def joined(g00, g01, g11):
    return jnp.concatenate([beside(g00, g01), beside(g01.T, g11)], axis=0)


def thirds(x):
    high = x.astype(jnp.bfloat16)
    rest = x - high.astype(jnp.float32)
    middle = rest.astype(jnp.bfloat16)
    return high, middle, (rest - middle.astype(jnp.float32)).astype(jnp.bfloat16)


def dot_16(left, right):
    return jnp.dot(left, right, preferred_element_type=jnp.float32)


def pick_columns(x, units):
    high, middle, low = thirds(x)
    return dot_16(high, units) + (dot_16(middle, units) + dot_16(low, units))


def pick_rows(units, x):
    high, middle, low = thirds(x)
    return dot_16(units, high) + (dot_16(units, middle) + dot_16(units, low))


def turn(p, q, c, s):
    return c * p - s * q, s * p + c * q


def advance(p, q):
    at = lax.broadcasted_iota(jnp.int32, p.shape, 1)
    p_back = pltpu.roll(p, BLOCK - 1, 1)
    q_on = pltpu.roll(q, 1, 1)
    new_p = jnp.where(at == 0, p, jnp.where(at == BLOCK - 1, q, p_back))
    new_q = jnp.where(at == 0, p_back, q_on)
    return new_p, new_q


def angles(gpp, cross, gqq):
    d = gqq - gpp
    root = jnp.sqrt(d * d + 4.0 * cross * cross)
    t = 2.0 * cross * d / ((jnp.abs(d) + root) * root + 1e-06 * (gpp + gqq) * (gpp + gqq))
    w = 1.0 + t * t
    c = lax.rsqrt(w)
    c = c * (1.5 - 0.5 * w * c * c)
    return c, t * c


def solves(grams, along, down, scratch):
    ga, gb, gc, gd, qa, qb, qc, qd = scratch
    count = len(grams)
    lane = lax.broadcasted_iota(jnp.int32, (N, N), 1).astype(jnp.float32)
    sub = lax.broadcasted_iota(jnp.int32, (N, N), 0).astype(jnp.float32)
    take = jnp.where(sub == along[0:1, :], 1.0, 0.0).astype(jnp.bfloat16)
    take_t = jnp.where(lane == down[:, 0:1], 1.0, 0.0)
    back_t = jnp.where(lane == down[:, 1:2], 1.0, 0.0).astype(jnp.bfloat16)
    i0 = lax.broadcasted_iota(jnp.int32, (BLOCK, BLOCK), 0)
    i1 = lax.broadcasted_iota(jnp.int32, (BLOCK, BLOCK), 1)
    at = lax.broadcasted_iota(jnp.int32, (1, BLOCK), 1)
    body = pl.ds(8, BLOCK)
    state = []
    for k, gram in enumerate(grams):
        placed = pick_rows(take_t.astype(jnp.bfloat16), pick_columns(gram, take))
        a, b = placed[:BLOCK, :BLOCK], placed[:BLOCK, BLOCK:]
        c_, d_ = placed[BLOCK:, :BLOCK], placed[BLOCK:, BLOCK:]
        ga[0, k, body], gb[0, k, body], gc[0, k, body], gd[0, k, body] = a, b, c_, d_
        qa[0, k, body], qb[0, k, body] = take_t[:BLOCK, :BLOCK], take_t[:BLOCK, BLOCK:]
        qc[0, k, body], qd[0, k, body] = take_t[BLOCK:, :BLOCK], take_t[BLOCK:, BLOCK:]
        on = i0 == i1

        def diagonal(m):
            return jnp.sum(jnp.where(on, m, 0.0), axis=0, keepdims=True)

        state.append((diagonal(a), diagonal(b), diagonal(d_)))

    def one_round(old, new, k, gpp, cross, gqq):
        c, s = angles(gpp, cross, gqq)
        a, b, c_, d_ = ga[old, k, body], gb[old, k, body], gc[old, k, body], gd[old, k, body]
        on = i0 == i1
        c_col = jnp.sum(jnp.where(on, c, 0.0), axis=1, keepdims=True)
        s_col = jnp.sum(jnp.where(on, s, 0.0), axis=1, keepdims=True)
        low = c * gpp - s * cross
        new_pp = c * low - s * (c * cross - s * gqq)
        new_qq = s * (s * gpp + c * cross) + c * (s * cross + c * gqq)
        new_pp, new_qq = advance(new_pp, new_qq)
        off = (i0 == i1 + 2) | ((i0 == BLOCK - 1) & (i1 == BLOCK - 2))

        def beyond(m):
            return jnp.sum(jnp.where(off, m, 0.0), axis=0, keepdims=True)

        ea, eb, ec, ed = (pltpu.roll(beyond(m), 1, 1) for m in (a, b, c_, d_))
        ra, rb, rc, rd = (pltpu.roll(m[0:1], BLOCK - 1, 1) for m in (a, b, c_, d_))
        end, start = at == BLOCK - 1, at == 0
        cl, sl = pltpu.roll(c, 1, 1), pltpu.roll(s, 1, 1)
        cr, sr = pltpu.roll(c, BLOCK - 1, 1), pltpu.roll(s, BLOCK - 1, 1)
        cu, su = jnp.where(end, s, cr), jnp.where(end, -c, sr)
        main = cu * (sl * ea + cl * eb) - su * (sl * ec + cl * ed)
        tip = c * (cr * ra - sr * rb) - s * (cr * rc - sr * rd)
        new_cross = jnp.where(start, tip, main)
        a, b = advance(*turn(a, b, c, s))
        c_, d_ = advance(*turn(c_, d_, c, s))
        qs = [x[old, k, body] for x in (qa, qc, qb, qd)]
        for first, second, top, bottom in (
            (a, c_, ga, gc),
            (b, d_, gb, gd),
            (qs[0], qs[1], qa, qc),
            (qs[2], qs[3], qb, qd),
        ):
            up, under = turn(first, second, c_col, s_col)
            top[new, k, pl.ds(7, BLOCK)] = up
            top[new, k, pl.ds(8, 1)] = up[0:1]
            top[new, k, pl.ds(BLOCK + 7, 1)] = under[BLOCK - 1 :]
            bottom[new, k, pl.ds(9, BLOCK)] = under
            bottom[new, k, pl.ds(8, 1)] = up[1:2]
        return new_pp, new_cross, new_qq

    def two_rounds(_, state):
        state = [one_round(0, 1, k, *state[k]) for k in range(count)]
        return [one_round(1, 0, k, *state[k]) for k in range(count)]

    if count == 1:
        lax.fori_loop(0, ROUNDS // 2, two_rounds, state)
    else:
        for pair in range(ROUNDS // 2):
            state = two_rounds(pair, state)
    turned = [
        [jnp.concatenate([top[0, k, body], bottom[0, k, body]], axis=0).T for k in range(count)]
        for top, bottom in ((qa, qc), (qb, qd))
    ]
    return [
        pick_columns(jnp.concatenate([turned[0][k], turned[1][k]], axis=0), back_t)
        for k in range(count)
    ]


def gram_kernel(own, other, out):
    x = jnp.concatenate([own[...], other[...]], axis=0)
    x0, x1 = x[:, :BLOCK], x[:, BLOCK:]
    out[0], out[1], out[2] = dot_t(x0, x0), dot_t(x0, x1), dot_t(x1, x1)


def mixed_kernel(x, near, out):
    mixed = dot_t(x[...], near[...])
    out[0], out[1] = mixed[:, :BLOCK], mixed[:, BLOCK:]


def spread_kernel(parts, mixed, out):
    n, m = parts.shape[0], parts.shape[1]
    total = parts[0]
    for k in range(1, n):
        total = total + parts[k]
    for k in range(n):
        out[k, :m] = total
    out[:, m:] = mixed[...]


def first_gram(landed, m):
    sums = landed[:, :m].reshape(3, BLOCK, BLOCK)
    return joined(sums[0], sums[1], sums[2])


def first_kernel(landed, along, down, q_out, ship, *scratch):
    gram = first_gram(landed, 3 * BLOCK // landed.shape[0])
    (q,) = solves([gram], along[...], down[...], scratch)
    q_out[...] = q
    q1 = q[:, BLOCK:]
    ship[:N] = q1
    ship[N:] = dot_t(q1, dot(gram, q1))


def keep_kernel(landed, q, x, g00, kept):
    q0 = q[:, :BLOCK]
    kept[...] = dot(x[...], q0)
    g00[...] = dot_t(q0, dot(first_gram(landed, 3 * BLOCK // landed.shape[0]), q0))


def second_kernel(mixed, q, ship, g00, kept, near, along, down, x0, x1, gram_out, q_out, *scratch):
    q1 = ship[:N]
    cross = dot_t(q[:, :BLOCK], dot(beside(mixed[0], mixed[1]), q1))
    gram = joined(g00[...], cross, ship[N:])
    gram_out[...] = gram
    (turned,) = solves([gram], along[...], down[...], scratch)
    q_out[...] = turned
    y = dot(beside(kept[...], dot(near[...], q1)), turned)
    x0[...] = y[:, :BLOCK]
    x1[...] = y[:, BLOCK:]


def turned_kernel(gram, q, out):
    g = dot_t(q[...], dot(gram[...], q[...]))
    out[0], out[1], out[2] = g[:BLOCK, :BLOCK], g[:BLOCK, BLOCK:], g[BLOCK:, BLOCK:]


def cross_kernel(far0, x0, x1, near1, out):
    f0, s0, s1, n1 = far0[...], x0[...], x1[...], near1[...]
    out[0] = dot_t(f0, s1)
    out[1] = dot_t(s0, n1)
    out[2] = dot_t(f0, s0)
    out[3] = dot_t(f0, n1)
    out[4] = dot_t(s1, n1)


def last_kernel(
    sums,
    inner,
    far00,
    near11,
    far0,
    x0,
    x1,
    near1,
    along2,
    down2,
    along3,
    down3,
    swapped,
    mine_data,
    mine_basis,
    theirs,
    *scratch,
):
    gram_a = joined(far00[...], sums[0], inner[2])
    gram_b = joined(inner[0], sums[1], near11[...])
    qa, qb = solves([gram_a, gram_b], along2[...], down2[...], scratch)
    qa, qb = qa[:, :BLOCK], qb[:, BLOCK:]
    mixed = jnp.concatenate([beside(sums[2], sums[3]), beside(inner[1].T, sums[4])], axis=0)
    gram = joined(
        dot_t(qa, dot(gram_a, qa)), dot_t(qa, dot(mixed, qb)), dot_t(qb, dot(gram_b, qb))
    )
    (q,) = solves([gram], along3[...], down3[...], scratch)
    ya = dot(beside(far0[...], x1[...]), qa)
    yb = dot(beside(x0[...], near1[...]), qb)
    y = dot(beside(ya, yb), q)
    swap = swapped[...] > 0.0
    y = beside(
        jnp.where(swap, y[:, BLOCK:], y[:, :BLOCK]), jnp.where(swap, y[:, :BLOCK], y[:, BLOCK:])
    )
    rows, height = mine_data.shape[0], mine_basis.shape[0]
    mine_data[...] = y[:rows]
    theirs[:rows] = y[rows : 2 * rows]
    mine_basis[...] = y[2 * rows : 2 * rows + height]
    theirs[rows:] = y[2 * rows + height :]


def chip_groups(size):
    return [list(range(core, size, 2)) for core in range(2)]


def trade(parts):
    groups = chip_groups(lax.axis_size("rows"))
    return lax.all_to_all(parts, "rows", 0, 0, axis_index_groups=groups)


def all_slices(mine, n):
    return trade(jnp.broadcast_to(mine[None], (n,) + mine.shape))


def other_core(x):
    return lax.ppermute(x, "rows", [(i, i ^ 1) for i in range(lax.axis_size("rows"))])


def along_pairs(x, sign):
    n_rows, n_pairs = lax.axis_size("rows"), lax.axis_size("pairs")
    route = []
    for r in range(n_rows):
        step = sign if r % 2 else -sign
        for p in range(n_pairs):
            route.append((r * n_pairs + p, r * n_pairs + (p + step) % n_pairs))
    return lax.ppermute(x, ("rows", "pairs"), route)


def body(sample, column_scale, inner_order):
    row, col = lax.axis_index("rows"), lax.axis_index("pairs")
    core = row % 2
    first = core == 0
    n_pairs = lax.axis_size("pairs")
    data = sample * column_scale[None, :]
    rows = data.shape[0]
    left, right = data[:, :N], data[:, N:]
    own = jnp.where(first, left, beside(right[:, BLOCK:], right[:, :BLOCK]))
    send = jnp.where(first, beside(right[:, BLOCK:], right[:, :BLOCK]), left)
    got = other_core(send)
    x = jnp.concatenate([own, got], axis=0)
    near = along_pairs(x, 1)
    near_col = (col + jnp.where(first, 1, -1)) % n_pairs

    height = W // lax.axis_size("rows")
    ids = jnp.arange(height, dtype=jnp.int32)
    row_ids = jnp.concatenate([ids + row * height, ids + (row ^ 1) * height])[:, None]
    places = (jnp.arange(N, dtype=jnp.int32)[None, :] + core * BLOCK) % N + core * N

    def with_basis(values, at):
        unit = jnp.where(row_ids == places + 2 * N * at, 1.0, 0.0).astype(jnp.float32)
        return jnp.concatenate([values, unit])

    order = ((inner_order + core * BLOCK) % N).astype(jnp.float32)
    table = np.concatenate([np.eye(N)[:, arrangement(0)], np.eye(N)[:, arrangement(ROUNDS)]], 1)
    table = jnp.asarray(table.astype(np.float32))
    along = dot(order, table).reshape(STEPS, 2, N)
    down = dot_t(table, order.T).reshape(2, N, STEPS)
    down = [down[:, :, s].T for s in range(STEPS)]

    chips = lax.axis_size("rows") // 2
    gram_rows, mixed_rows = 3 * BLOCK // chips, 2 * N // chips
    parts = trade(call(gram_kernel, shape(3, BLOCK, BLOCK), [], own, got).reshape(chips, -1, BLOCK))
    mixed = call(mixed_kernel, shape(2, N, BLOCK), [], x, near).reshape(chips, -1, BLOCK)
    landed = trade(
        call(spread_kernel, shape(chips, gram_rows + mixed_rows, BLOCK), [], parts, mixed)
    )
    mixed = all_slices(landed[:, gram_rows:].sum(0), chips).reshape(2, N, BLOCK)

    x, near = with_basis(x, col), with_basis(near, near_col)
    total = x.shape[0]
    q, ship = call(
        first_kernel,
        (shape(N, N), shape(N + BLOCK, BLOCK)),
        solve_scratch(1),
        landed,
        along[0],
        down[0],
    )
    ship = along_pairs(ship, 1)
    g00, kept = call(keep_kernel, (shape(BLOCK, BLOCK), shape(total, BLOCK)), [], landed, q, x)
    half = shape(total, BLOCK)
    x0, x1, gram, q = call(
        second_kernel,
        (half, half, shape(N, N), shape(N, N)),
        solve_scratch(1),
        mixed,
        q,
        ship,
        g00,
        kept,
        near,
        along[1],
        down[1],
    )

    both = 2 * rows
    far0, near1 = along_pairs(x0[:both], -1), along_pairs(x1[:both], 1)
    cross = call(
        cross_kernel, shape(5, BLOCK, BLOCK), [], far0, x0[:both], x1[:both], near1
    )
    sums = trade(cross.reshape(chips, -1, BLOCK)).sum(0)
    inner = call(turned_kernel, shape(3, BLOCK, BLOCK), [], gram, q)
    far_rest = along_pairs(jnp.concatenate([x0[both:], inner[0]]), -1)
    near_rest = along_pairs(jnp.concatenate([x1[both:], inner[2]]), 1)
    sums = all_slices(sums, chips).reshape(5, BLOCK, BLOCK)
    cut = 2 * height
    far0 = jnp.concatenate([far0, far_rest[:cut]])
    near1 = jnp.concatenate([near1, near_rest[:cut]])
    mine_data, mine_basis, theirs = call(
        last_kernel,
        (shape(rows, N), shape(height, N), shape(rows + height, N)),
        solve_scratch(2),
        sums,
        inner,
        far_rest[cut:],
        near_rest[cut:],
        far0,
        x0,
        x1,
        near1,
        along[2],
        down[2],
        along[3],
        down[3],
        jnp.full((1, BLOCK), core, jnp.float32),
    )
    got = other_core(theirs)

    def placed(got, mine):
        return jnp.where(first, beside(got, mine), beside(mine, got))

    return placed(got[:rows], mine_data), placed(got[rows:], mine_basis)


def solution(mesh):
    return jax.shard_map(
        body,
        mesh=mesh,
        in_specs=(P("rows", "pairs"), P("pairs"), P()),
        out_specs=(P("rows", "pairs"), P("rows", "pairs")),
        check_vma=False,
    )
```

```python
import functools

import jax
import jax.numpy as jnp
import numpy as np
from jax import lax
from jax.experimental import pallas as pl
from jax.experimental.pallas import tpu as pltpu
from jax.sharding import PartitionSpec as P

BLOCK = 128
N = 2 * BLOCK
W = 4096
STEPS = 4
ROUNDS = 8
HIGHEST = lax.Precision.HIGHEST
VMEM = pl.BlockSpec(memory_space=pltpu.VMEM)


def arrangement(r):
    m = N - 1
    first = [m] + [(r + i) % m for i in range(1, BLOCK)]
    second = [r % m] + [(r - i) % m for i in range(1, BLOCK)]
    return np.array(first + second)


def shape(*dims):
    return jax.ShapeDtypeStruct(dims, jnp.float32)


def call(kernel, out_shape, scratch, *operands):
    return pl.pallas_call(
        kernel,
        out_shape=out_shape,
        in_specs=[VMEM] * len(operands),
        out_specs=jax.tree.map(lambda _: VMEM, out_shape),
        scratch_shapes=scratch,
        compiler_params=pltpu.CompilerParams(vmem_limit_bytes=40 * 2**20),
    )(*operands)


def solve_scratch(count):
    block = pltpu.VMEM((2, count, BLOCK + 16, BLOCK), jnp.float32)
    return [block] * 8


def dot(left, right):
    return jnp.dot(left, right, precision=HIGHEST, preferred_element_type=jnp.float32)


def dot_t(left, right):
    return lax.dot_general(
        left,
        right,
        (((0,), (0,)), ((), ())),
        precision=HIGHEST,
        preferred_element_type=jnp.float32,
    )


def beside(*parts):
    return jnp.concatenate(parts, axis=1)


def joined(g00, g01, g11):
    return jnp.concatenate([beside(g00, g01), beside(g01.T, g11)], axis=0)


def thirds(x):
    high = x.astype(jnp.bfloat16)
    rest = x - high.astype(jnp.float32)
    middle = rest.astype(jnp.bfloat16)
    return high, middle, (rest - middle.astype(jnp.float32)).astype(jnp.bfloat16)


def dot_16(left, right):
    return jnp.dot(left, right, preferred_element_type=jnp.float32)


def pick_columns(x, units):
    high, middle, low = thirds(x)
    return dot_16(high, units) + (dot_16(middle, units) + dot_16(low, units))


def pick_rows(units, x):
    high, middle, low = thirds(x)
    return dot_16(units, high) + (dot_16(units, middle) + dot_16(units, low))


def dot_3(left, right):
    l_high, l_low, _ = thirds(left)
    r_high, r_low, _ = thirds(right)
    return dot_16(l_high, r_high) + (dot_16(l_high, r_low) + dot_16(l_low, r_high))


def turn(p, q, c, s):
    return c * p - s * q, s * p + c * q


def advance(p, q):
    at = lax.broadcasted_iota(jnp.int32, p.shape, 1)
    p_back = pltpu.roll(p, BLOCK - 1, 1)
    q_on = pltpu.roll(q, 1, 1)
    new_p = jnp.where(at == 0, p, jnp.where(at == BLOCK - 1, q, p_back))
    new_q = jnp.where(at == 0, p_back, q_on)
    return new_p, new_q


def angles(gpp, cross, gqq):
    d = gqq - gpp
    root = jnp.sqrt(d * d + 4.0 * cross * cross)
    t = 2.0 * cross * d / ((jnp.abs(d) + root) * root + 1e-06 * (gpp + gqq) * (gpp + gqq))
    w = 1.0 + t * t
    c = lax.rsqrt(w)
    c = c * (1.5 - 0.5 * w * c * c)
    return c, t * c


def solves(grams, along, down, scratch):
    ga, gb, gc, gd, qa, qb, qc, qd = scratch
    count = len(grams)
    lane = lax.broadcasted_iota(jnp.int32, (N, N), 1).astype(jnp.float32)
    sub = lax.broadcasted_iota(jnp.int32, (N, N), 0).astype(jnp.float32)
    take = jnp.where(sub == along[0:1, :], 1.0, 0.0).astype(jnp.bfloat16)
    take_t = jnp.where(lane == down[:, 0:1], 1.0, 0.0)
    back_t = jnp.where(lane == down[:, 1:2], 1.0, 0.0).astype(jnp.bfloat16)
    i0 = lax.broadcasted_iota(jnp.int32, (BLOCK, BLOCK), 0)
    i1 = lax.broadcasted_iota(jnp.int32, (BLOCK, BLOCK), 1)
    at = lax.broadcasted_iota(jnp.int32, (1, BLOCK), 1)
    body = pl.ds(8, BLOCK)
    state = []
    for k, gram in enumerate(grams):
        placed = pick_rows(take_t.astype(jnp.bfloat16), pick_columns(gram, take))
        a, b = placed[:BLOCK, :BLOCK], placed[:BLOCK, BLOCK:]
        c_, d_ = placed[BLOCK:, :BLOCK], placed[BLOCK:, BLOCK:]
        ga[0, k, body], gb[0, k, body], gc[0, k, body], gd[0, k, body] = a, b, c_, d_
        qa[0, k, body], qb[0, k, body] = take_t[:BLOCK, :BLOCK], take_t[:BLOCK, BLOCK:]
        qc[0, k, body], qd[0, k, body] = take_t[BLOCK:, :BLOCK], take_t[BLOCK:, BLOCK:]
        on = i0 == i1

        def diagonal(m):
            return jnp.sum(jnp.where(on, m, 0.0), axis=0, keepdims=True)

        state.append((diagonal(a), diagonal(b), diagonal(d_)))

    def one_round(old, new, k, gpp, cross, gqq):
        c, s = angles(gpp, cross, gqq)
        a, b, c_, d_ = ga[old, k, body], gb[old, k, body], gc[old, k, body], gd[old, k, body]
        on = i0 == i1
        c_col = jnp.sum(jnp.where(on, c, 0.0), axis=1, keepdims=True)
        s_col = jnp.sum(jnp.where(on, s, 0.0), axis=1, keepdims=True)
        low = c * gpp - s * cross
        new_pp = c * low - s * (c * cross - s * gqq)
        new_qq = s * (s * gpp + c * cross) + c * (s * cross + c * gqq)
        new_pp, new_qq = advance(new_pp, new_qq)
        off = (i0 == i1 + 2) | ((i0 == BLOCK - 1) & (i1 == BLOCK - 2))

        def beyond(m):
            return jnp.sum(jnp.where(off, m, 0.0), axis=0, keepdims=True)

        ea, eb, ec, ed = (pltpu.roll(beyond(m), 1, 1) for m in (a, b, c_, d_))
        ra, rb, rc, rd = (pltpu.roll(m[0:1], BLOCK - 1, 1) for m in (a, b, c_, d_))
        end, start = at == BLOCK - 1, at == 0
        cl, sl = pltpu.roll(c, 1, 1), pltpu.roll(s, 1, 1)
        cr, sr = pltpu.roll(c, BLOCK - 1, 1), pltpu.roll(s, BLOCK - 1, 1)
        cu, su = jnp.where(end, s, cr), jnp.where(end, -c, sr)
        main = cu * (sl * ea + cl * eb) - su * (sl * ec + cl * ed)
        tip = c * (cr * ra - sr * rb) - s * (cr * rc - sr * rd)
        new_cross = jnp.where(start, tip, main)
        a, b = advance(*turn(a, b, c, s))
        c_, d_ = advance(*turn(c_, d_, c, s))
        qs = [x[old, k, body] for x in (qa, qc, qb, qd)]
        for first, second, top, bottom in (
            (a, c_, ga, gc),
            (b, d_, gb, gd),
            (qs[0], qs[1], qa, qc),
            (qs[2], qs[3], qb, qd),
        ):
            up, under = turn(first, second, c_col, s_col)
            top[new, k, pl.ds(7, BLOCK)] = up
            top[new, k, pl.ds(8, 1)] = up[0:1]
            top[new, k, pl.ds(BLOCK + 7, 1)] = under[BLOCK - 1 :]
            bottom[new, k, pl.ds(9, BLOCK)] = under
            bottom[new, k, pl.ds(8, 1)] = up[1:2]
        return new_pp, new_cross, new_qq

    def two_rounds(_, state):
        state = [one_round(0, 1, k, *state[k]) for k in range(count)]
        return [one_round(1, 0, k, *state[k]) for k in range(count)]

    lax.fori_loop(0, ROUNDS // 2, two_rounds, state)
    turned = [
        [jnp.concatenate([top[0, k, body], bottom[0, k, body]], axis=0).T for k in range(count)]
        for top, bottom in ((qa, qc), (qb, qd))
    ]
    return [
        pick_columns(jnp.concatenate([turned[0][k], turned[1][k]], axis=0), back_t)
        for k in range(count)
    ]


def start_kernel(sample, scale, swapped, own, send):
    x = sample[...] * scale[...]
    blocks = [x[:, k * BLOCK : (k + 1) * BLOCK] for k in range(4)]
    swap = swapped[...] > 0.0
    for k, far in ((0, 3), (1, 2)):
        at = slice(k * BLOCK, (k + 1) * BLOCK)
        own[:, at] = jnp.where(swap, blocks[far], blocks[k])
        send[:, at] = jnp.where(swap, blocks[k], blocks[far])


def gram_kernel(own, other, out):
    x = jnp.concatenate([own[...], other[...]], axis=0)
    gram = dot_t(x, x)
    out[0], out[1], out[2] = gram[:BLOCK, :BLOCK], gram[:BLOCK, BLOCK:], gram[BLOCK:, BLOCK:]


def mixed_kernel(own, other, near, out):
    x = jnp.concatenate([own[...], other[...]], axis=0)
    mixed = dot_t(x, near[...])
    out[0], out[1] = mixed[:, :BLOCK], mixed[:, BLOCK:]


def spread_kernel(parts, mixed, out):
    n, m = parts.shape[0], parts.shape[1]
    total = parts[0]
    for k in range(1, n):
        total = total + parts[k]
    for k in range(n):
        out[k, :m] = total
    out[:, m:] = mixed[...]


def first_gram(landed, m):
    sums = landed[:, :m].reshape(3, BLOCK, BLOCK)
    return joined(sums[0], sums[1], sums[2])


def first_kernel(landed, along, down, q_out, ship, *scratch):
    gram = first_gram(landed, 3 * BLOCK // landed.shape[0])
    (q,) = solves([gram], along[...], down[...], scratch)
    q_out[...] = q
    q1 = q[:, BLOCK:]
    ship[:N] = q1
    ship[N:] = dot_t(q1, dot(gram, q1))


def keep_kernel(landed, q, own, other, unit, g00, kept, kept_basis):
    q0 = q[:, :BLOCK]
    kept[...] = dot(jnp.concatenate([own[...], other[...]], axis=0), q0)
    kept_basis[...] = dot(unit[...], q0)
    g00[...] = dot_t(q0, dot(first_gram(landed, 3 * BLOCK // landed.shape[0]), q0))


def second_kernel(mixed, q, ship, g00, kept, near, along, down, x0, x1, gram_out, q_out, *scratch):
    q1 = ship[:N]
    cross = dot(q[:, :BLOCK].T, dot(beside(mixed[0], mixed[1]), q1))
    gram = joined(g00[...], cross, ship[N:])
    gram_out[...] = gram
    (turned,) = solves([gram], along[...], down[...], scratch)
    q_out[...] = turned
    y = dot(beside(kept[...], dot(near[...], q1)), turned)
    x0[...] = y[:, :BLOCK]
    x1[...] = y[:, BLOCK:]


def basis_kernel(kept, unit, ship, q, gram, far, near, out):
    y = dot(beside(kept[...], dot(unit[...], ship[:N])), q[...])
    g = dot_t(q[...], dot(gram[...], q[...]))
    rows = y.shape[0]
    far[:rows], near[:rows] = y[:, :BLOCK], y[:, BLOCK:]
    far[rows:], near[rows:] = g[:BLOCK, :BLOCK], g[BLOCK:, BLOCK:]
    out[...] = g[:BLOCK, BLOCK:]


def cross_kernel(far0, x0, x1, near1, out):
    f0, n1 = far0[...], near1[...]
    both = dot_t(beside(f0, n1), beside(x1[...], x0[...]))
    out[0] = both[:BLOCK, :BLOCK]
    out[1] = both[BLOCK:, BLOCK:]
    out[2] = both[:BLOCK, BLOCK:]
    out[3] = dot_t(f0, n1)
    out[4] = both[BLOCK:, :BLOCK]


def last_kernel(
    sums,
    inner,
    far0,
    x0,
    x1,
    near1,
    far_rest,
    rest0,
    rest1,
    near_rest,
    along2,
    down2,
    along3,
    down3,
    swapped,
    mine_data,
    mine_basis,
    theirs,
    *scratch,
):
    basis_rows = far_rest.shape[0] - BLOCK
    gram_a = joined(far_rest[basis_rows:], sums[0], rest1[basis_rows:])
    gram_b = joined(rest0[basis_rows:], sums[1].T, near_rest[basis_rows:])
    mixed = jnp.concatenate(
        [beside(sums[2], sums[3]), beside(inner[...].T, sums[4].T)], axis=0
    )
    qa, qb = solves([gram_a, gram_b], along2[...], down2[...], scratch)
    qa, qb = qa[:, :BLOCK], qb[:, BLOCK:]
    left = dot(qa.T, beside(gram_a, mixed))
    gram = joined(dot(left[:, :N], qa), dot(left[:, N:], qb), dot(dot(qb.T, gram_b), qb))
    (q,) = solves([gram], along3[...], down3[...], scratch)

    def whole(data, rest):
        return jnp.concatenate([data[...], rest[:basis_rows]], axis=0)

    ya = dot_3(beside(whole(far0, far_rest), whole(x1, rest1)), qa)
    yb = dot_3(beside(whole(x0, rest0), whole(near1, near_rest)), qb)
    y = dot_3(beside(ya, yb), q)
    swap = swapped[...] > 0.0
    y = beside(
        jnp.where(swap, y[:, BLOCK:], y[:, :BLOCK]), jnp.where(swap, y[:, :BLOCK], y[:, BLOCK:])
    )
    rows, height = mine_data.shape[0], mine_basis.shape[0]
    mine_data[...] = y[:rows]
    theirs[:rows] = y[rows : 2 * rows]
    mine_basis[...] = y[2 * rows : 2 * rows + height]
    theirs[rows:] = y[2 * rows + height :]


def place_kernel(got, mine_data, mine_basis, swapped, data, basis):
    swap = swapped[...] > 0.0
    swap = beside(swap, swap)
    rows = mine_data.shape[0]
    for mine, theirs, out in (
        (mine_data[...], got[:rows], data),
        (mine_basis[...], got[rows:], basis),
    ):
        out[:, :N] = jnp.where(swap, mine, theirs)
        out[:, N:] = jnp.where(swap, theirs, mine)


def chip_groups(size):
    return [list(range(core, size, 2)) for core in range(2)]


def trade(parts):
    groups = chip_groups(lax.axis_size("rows"))
    return lax.all_to_all(parts, "rows", 0, 0, axis_index_groups=groups)


def all_slices(mine, n):
    return trade(jnp.broadcast_to(mine[None], (n,) + mine.shape))


def other_core(x):
    return lax.ppermute(x, "rows", [(i, i ^ 1) for i in range(lax.axis_size("rows"))])


def along_pairs(x, sign):
    n_rows, n_pairs = lax.axis_size("rows"), lax.axis_size("pairs")
    route = []
    for r in range(n_rows):
        step = sign if r % 2 else -sign
        for p in range(n_pairs):
            route.append((r * n_pairs + p, r * n_pairs + (p + step) % n_pairs))
    return lax.ppermute(x, ("rows", "pairs"), route)


def body(sample, column_scale, inner_order):
    row, col = lax.axis_index("rows"), lax.axis_index("pairs")
    core = row % 2
    n_pairs = lax.axis_size("pairs")
    rows, width = sample.shape
    height = W // lax.axis_size("rows")
    swapped = jnp.full((1, BLOCK), core, jnp.float32)
    own, send = call(
        start_kernel,
        (shape(rows, N), shape(rows, N)),
        [],
        sample,
        column_scale.reshape(1, width),
        swapped,
    )
    other = other_core(send)
    near = along_pairs(jnp.concatenate([own, other], axis=0), 1)
    near_col = (col + jnp.where(core == 0, 1, -1)) % n_pairs

    ids = jnp.arange(height, dtype=jnp.int32)
    row_ids = jnp.concatenate([ids + row * height, ids + (row ^ 1) * height])[:, None]
    places = (jnp.arange(N, dtype=jnp.int32)[None, :] + core * BLOCK) % N + core * N
    unit = jnp.where(row_ids == places + 2 * N * col, 1.0, 0.0).astype(jnp.float32)
    near_unit = jnp.where(row_ids == places + 2 * N * near_col, 1.0, 0.0).astype(jnp.float32)

    order = ((inner_order + core * BLOCK) % N).astype(jnp.float32)
    table = np.concatenate([np.eye(N)[:, arrangement(0)], np.eye(N)[:, arrangement(ROUNDS)]], 1)
    table = jnp.asarray(table.astype(np.float32))
    along = dot(order, table).reshape(STEPS, 2, N)
    down = dot_t(table, order.T).reshape(2, N, STEPS)
    down = [down[:, :, s].T for s in range(STEPS)]

    chips = lax.axis_size("rows") // 2
    gram_rows, mixed_rows = 3 * BLOCK // chips, 2 * N // chips
    gram = call(gram_kernel, shape(3, BLOCK, BLOCK), [], own, other)
    parts = trade(gram.reshape(chips, -1, BLOCK))
    mixed = call(mixed_kernel, shape(2, N, BLOCK), [], own, other, near)
    landed = trade(
        call(
            spread_kernel,
            shape(chips, gram_rows + mixed_rows, BLOCK),
            [],
            parts,
            mixed.reshape(chips, -1, BLOCK),
        )
    )
    mixed = all_slices(landed[:, gram_rows:].sum(0), chips).reshape(2, N, BLOCK)

    q, ship = call(
        first_kernel,
        (shape(N, N), shape(N + BLOCK, BLOCK)),
        solve_scratch(1),
        landed,
        along[0],
        down[0],
    )
    ship = along_pairs(ship, 1)
    half, half_basis = shape(2 * rows, BLOCK), shape(2 * height, BLOCK)
    g00, kept, kept_basis = call(
        keep_kernel,
        (shape(BLOCK, BLOCK), half, half_basis),
        [],
        landed,
        q,
        own,
        other,
        unit,
    )
    x0, x1, gram, q = call(
        second_kernel,
        (half, half, shape(N, N), shape(N, N)),
        solve_scratch(1),
        mixed,
        q,
        ship,
        g00,
        kept,
        near,
        along[1],
        down[1],
    )

    far0, near1 = along_pairs(x0, -1), along_pairs(x1, 1)
    rest = shape(2 * height + BLOCK, BLOCK)
    rest0, rest1, inner = call(
        basis_kernel,
        (rest, rest, shape(BLOCK, BLOCK)),
        [],
        kept_basis,
        near_unit,
        ship,
        q,
        gram,
    )
    cross = call(cross_kernel, shape(5, BLOCK, BLOCK), [], far0, x0, x1, near1)
    sums = trade(cross.reshape(chips, -1, BLOCK)).sum(0)
    far_rest, near_rest = along_pairs(rest0, -1), along_pairs(rest1, 1)
    sums = all_slices(sums, chips).reshape(5, BLOCK, BLOCK)
    mine_data, mine_basis, theirs = call(
        last_kernel,
        (shape(rows, N), shape(height, N), shape(rows + height, N)),
        solve_scratch(2),
        sums,
        inner,
        far0,
        x0,
        x1,
        near1,
        far_rest,
        rest0,
        rest1,
        near_rest,
        along[2],
        down[2],
        along[3],
        down[3],
        swapped,
    )
    return call(
        place_kernel,
        (shape(rows, width), shape(height, width)),
        [],
        other_core(theirs),
        mine_data,
        mine_basis,
        swapped,
    )


def solution(mesh):
    return jax.shard_map(
        body,
        mesh=mesh,
        in_specs=(P("rows", "pairs"), P("pairs"), P()),
        out_specs=(P("rows", "pairs"), P("rows", "pairs")),
        check_vma=False,
    )
```

```python
import functools

import jax
import jax.numpy as jnp
import numpy as np
from jax import lax
from jax.experimental import pallas as pl
from jax.experimental.pallas import tpu as pltpu
from jax.sharding import PartitionSpec as P

BLOCK = 128
N = 2 * BLOCK
W = 4096
STEPS = 4
ROUNDS = 8
HIGHEST = lax.Precision.HIGHEST
VMEM = pl.BlockSpec(memory_space=pltpu.VMEM)


def arrangement(r):
    m = N - 1
    first = [m] + [(r + i) % m for i in range(1, BLOCK)]
    second = [r % m] + [(r - i) % m for i in range(1, BLOCK)]
    return np.array(first + second)


def shape(*dims):
    return jax.ShapeDtypeStruct(dims, jnp.float32)


def call(kernel, out_shape, scratch, *operands):
    return pl.pallas_call(
        kernel,
        out_shape=out_shape,
        in_specs=[VMEM] * len(operands),
        out_specs=jax.tree.map(lambda _: VMEM, out_shape),
        scratch_shapes=scratch,
        compiler_params=pltpu.CompilerParams(vmem_limit_bytes=40 * 2**20),
    )(*operands)


def solve_scratch(count):
    block = pltpu.VMEM((2, count, BLOCK + 16, BLOCK), jnp.float32)
    return [block] * 8


def dot(left, right):
    return jnp.dot(left, right, precision=HIGHEST, preferred_element_type=jnp.float32)


def dot_t(left, right):
    return lax.dot_general(
        left,
        right,
        (((0,), (0,)), ((), ())),
        precision=HIGHEST,
        preferred_element_type=jnp.float32,
    )


def beside(*parts):
    return jnp.concatenate(parts, axis=1)


def joined(g00, g01, g11):
    return jnp.concatenate([beside(g00, g01), beside(g01.T, g11)], axis=0)


def thirds(x):
    high = x.astype(jnp.bfloat16)
    rest = x - high.astype(jnp.float32)
    middle = rest.astype(jnp.bfloat16)
    return high, middle, (rest - middle.astype(jnp.float32)).astype(jnp.bfloat16)


def dot_16(left, right):
    return jnp.dot(left, right, preferred_element_type=jnp.float32)


def pick_columns(x, units):
    high, middle, low = thirds(x)
    return dot_16(high, units) + (dot_16(middle, units) + dot_16(low, units))


def pick_rows(units, x):
    high, middle, low = thirds(x)
    return dot_16(units, high) + (dot_16(units, middle) + dot_16(units, low))


def dot_3(left, right):
    l_high, l_low, _ = thirds(left)
    r_high, r_low, _ = thirds(right)
    return dot_16(l_high, r_high) + (dot_16(l_high, r_low) + dot_16(l_low, r_high))


def turn(p, q, c, s):
    return c * p - s * q, s * p + c * q


def advance(p, q):
    at = lax.broadcasted_iota(jnp.int32, p.shape, 1)
    p_back = pltpu.roll(p, BLOCK - 1, 1)
    q_on = pltpu.roll(q, 1, 1)
    new_p = jnp.where(at == 0, p, jnp.where(at == BLOCK - 1, q, p_back))
    new_q = jnp.where(at == 0, p_back, q_on)
    return new_p, new_q


def angles(gpp, cross, gqq):
    d = gqq - gpp
    root = jnp.sqrt(d * d + 4.0 * cross * cross)
    t = 2.0 * cross * d / ((jnp.abs(d) + root) * root + 1e-06 * (gpp + gqq) * (gpp + gqq))
    w = 1.0 + t * t
    c = lax.rsqrt(w)
    c = c * (1.5 - 0.5 * w * c * c)
    return c, t * c


def solves(grams, step, along_ref, down_ref, scratch):
    along = along_ref[2 * step : 2 * step + 1]
    down = down_ref[:, 2 * step : 2 * step + 2]
    ga, gb, gc, gd, qa, qb, qc, qd = scratch
    count = len(grams)
    lane = lax.broadcasted_iota(jnp.int32, (N, N), 1).astype(jnp.float32)
    sub = lax.broadcasted_iota(jnp.int32, (N, N), 0).astype(jnp.float32)
    take = jnp.where(sub == along, 1.0, 0.0).astype(jnp.bfloat16)
    take_t = jnp.where(lane == down[:, 0:1], 1.0, 0.0)
    back_t = jnp.where(lane == down[:, 1:2], 1.0, 0.0).astype(jnp.bfloat16)
    i0 = lax.broadcasted_iota(jnp.int32, (BLOCK, BLOCK), 0)
    i1 = lax.broadcasted_iota(jnp.int32, (BLOCK, BLOCK), 1)
    at = lax.broadcasted_iota(jnp.int32, (1, BLOCK), 1)
    body = pl.ds(8, BLOCK)
    state = []
    for k, gram in enumerate(grams):
        placed = pick_rows(take_t.astype(jnp.bfloat16), pick_columns(gram, take))
        a, b = placed[:BLOCK, :BLOCK], placed[:BLOCK, BLOCK:]
        c_, d_ = placed[BLOCK:, :BLOCK], placed[BLOCK:, BLOCK:]
        ga[0, k, body], gb[0, k, body], gc[0, k, body], gd[0, k, body] = a, b, c_, d_
        qa[0, k, body], qb[0, k, body] = take_t[:BLOCK, :BLOCK], take_t[:BLOCK, BLOCK:]
        qc[0, k, body], qd[0, k, body] = take_t[BLOCK:, :BLOCK], take_t[BLOCK:, BLOCK:]
        on = i0 == i1

        def diagonal(m):
            return jnp.sum(jnp.where(on, m, 0.0), axis=0, keepdims=True)

        state.append((diagonal(a), diagonal(b), diagonal(d_)))

    def one_round(old, new, k, gpp, cross, gqq):
        c, s = angles(gpp, cross, gqq)
        a, b, c_, d_ = ga[old, k, body], gb[old, k, body], gc[old, k, body], gd[old, k, body]
        on = i0 == i1
        c_col = jnp.sum(jnp.where(on, c, 0.0), axis=1, keepdims=True)
        s_col = jnp.sum(jnp.where(on, s, 0.0), axis=1, keepdims=True)
        low = c * gpp - s * cross
        new_pp = c * low - s * (c * cross - s * gqq)
        new_qq = s * (s * gpp + c * cross) + c * (s * cross + c * gqq)
        new_pp, new_qq = advance(new_pp, new_qq)
        off = (i0 == i1 + 2) | ((i0 == BLOCK - 1) & (i1 == BLOCK - 2))

        def beyond(m):
            return jnp.sum(jnp.where(off, m, 0.0), axis=0, keepdims=True)

        ea, eb, ec, ed = (pltpu.roll(beyond(m), 1, 1) for m in (a, b, c_, d_))
        ra, rb, rc, rd = (pltpu.roll(m[0:1], BLOCK - 1, 1) for m in (a, b, c_, d_))
        end, start = at == BLOCK - 1, at == 0
        cl, sl = pltpu.roll(c, 1, 1), pltpu.roll(s, 1, 1)
        cr, sr = pltpu.roll(c, BLOCK - 1, 1), pltpu.roll(s, BLOCK - 1, 1)
        cu, su = jnp.where(end, s, cr), jnp.where(end, -c, sr)
        main = cu * (sl * ea + cl * eb) - su * (sl * ec + cl * ed)
        tip = c * (cr * ra - sr * rb) - s * (cr * rc - sr * rd)
        new_cross = jnp.where(start, tip, main)
        a, b = advance(*turn(a, b, c, s))
        c_, d_ = advance(*turn(c_, d_, c, s))
        qs = [x[old, k, body] for x in (qa, qc, qb, qd)]
        for first, second, top, bottom in (
            (a, c_, ga, gc),
            (b, d_, gb, gd),
            (qs[0], qs[1], qa, qc),
            (qs[2], qs[3], qb, qd),
        ):
            up, under = turn(first, second, c_col, s_col)
            top[new, k, pl.ds(7, BLOCK)] = up
            top[new, k, pl.ds(8, 1)] = up[0:1]
            top[new, k, pl.ds(BLOCK + 7, 1)] = under[BLOCK - 1 :]
            bottom[new, k, pl.ds(9, BLOCK)] = under
            bottom[new, k, pl.ds(8, 1)] = up[1:2]
        return new_pp, new_cross, new_qq

    def two_rounds(_, state):
        state = [one_round(0, 1, k, *state[k]) for k in range(count)]
        return [one_round(1, 0, k, *state[k]) for k in range(count)]

    lax.fori_loop(0, ROUNDS // 2, two_rounds, state)
    turned = [
        [jnp.concatenate([top[0, k, body], bottom[0, k, body]], axis=0).T for k in range(count)]
        for top, bottom in ((qa, qc), (qb, qd))
    ]
    return [
        pick_columns(jnp.concatenate([turned[0][k], turned[1][k]], axis=0), back_t)
        for k in range(count)
    ]


def start_kernel(sample, scale, swapped, own, send, rows_in, scale_in, sems):
    steps = sems.shape[0] - 1
    size = sample.shape[0] // steps
    copies = [
        pltpu.make_async_copy(
            sample.at[pl.ds(k * size, size)], rows_in.at[pl.ds(k * size, size)], sems.at[k]
        )
        for k in range(steps)
    ]
    scale_copy = pltpu.make_async_copy(scale, scale_in, sems.at[steps])
    scale_copy.start()
    for copy in copies:
        copy.start()
    scale_copy.wait()
    swap = swapped[...] > 0.0
    for k in range(steps):
        copies[k].wait()
        part = pl.ds(k * size, size)
        x = rows_in[part] * scale_in[...]
        blocks = [x[:, b * BLOCK : (b + 1) * BLOCK] for b in range(4)]
        for near, far in ((0, 3), (1, 2)):
            at = slice(near * BLOCK, (near + 1) * BLOCK)
            own[part, at] = jnp.where(swap, blocks[far], blocks[near])
            send[part, at] = jnp.where(swap, blocks[near], blocks[far])


def start(sample, scale, swapped):
    rows, width = sample.shape
    steps = 4
    hbm = pl.BlockSpec(memory_space=pltpu.HBM)
    return pl.pallas_call(
        start_kernel,
        out_shape=(shape(rows, N), shape(rows, N)),
        in_specs=[hbm, hbm, VMEM],
        out_specs=(VMEM, VMEM),
        scratch_shapes=[
            pltpu.VMEM((rows, width), jnp.float32),
            pltpu.VMEM((1, width), jnp.float32),
            pltpu.SemaphoreType.DMA((steps + 1,)),
        ],
    )(sample, scale, swapped)


def gram_kernel(own, other, out):
    x = jnp.concatenate([own[...], other[...]], axis=0)
    gram = dot_t(x, x)
    out[0], out[1], out[2] = gram[:BLOCK, :BLOCK], gram[:BLOCK, BLOCK:], gram[BLOCK:, BLOCK:]


def mixed_kernel(own, other, near, out):
    x = jnp.concatenate([own[...], other[...]], axis=0)
    mixed = dot_t(x, near[...])
    out[0], out[1] = mixed[:, :BLOCK], mixed[:, BLOCK:]


def spread_kernel(parts, mixed, out):
    n, m = parts.shape[0], parts.shape[1]
    total = parts[0]
    for k in range(1, n):
        total = total + parts[k]
    for k in range(n):
        out[k, :m] = total
    out[:, m:] = mixed[...]


def first_gram(landed, m):
    sums = landed[:, :m].reshape(3, BLOCK, BLOCK)
    return joined(sums[0], sums[1], sums[2])


def first_kernel(landed, along, down, q_out, ship, *scratch):
    gram = first_gram(landed, 3 * BLOCK // landed.shape[0])
    (q,) = solves([gram], 0, along, down, scratch)
    q_out[...] = q
    q1 = q[:, BLOCK:]
    ship[:N] = q1
    ship[N:] = dot_t(q1, dot(gram, q1))


def keep_kernel(landed, q, own, other, unit, kept, kept_basis):
    q0 = q[:, :BLOCK]
    rows = kept.shape[0] - BLOCK
    kept[:rows] = dot(jnp.concatenate([own[...], other[...]], axis=0), q0)
    kept[rows:] = dot_t(q0, dot(first_gram(landed, 3 * BLOCK // landed.shape[0]), q0))
    kept_basis[...] = dot(unit[...], q0)


def second_kernel(mixed, q, ship, kept, near, along, down, x0, x1, gram_out, q_out, *scratch):
    q1 = ship[:N]
    cross = dot(q[:, :BLOCK].T, dot(beside(mixed[0], mixed[1]), q1))
    rows = near.shape[0]
    gram = joined(kept[rows:], cross, ship[N:])
    gram_out[...] = gram
    (turned,) = solves([gram], 1, along, down, scratch)
    q_out[...] = turned
    y = dot(beside(kept[:rows], dot(near[...], q1)), turned)
    x0[...] = y[:, :BLOCK]
    x1[...] = y[:, BLOCK:]


def basis_kernel(kept, unit, ship, q, gram, far, near, out):
    y = dot(beside(kept[...], dot(unit[...], ship[:N])), q[...])
    g = dot_t(q[...], dot(gram[...], q[...]))
    rows = y.shape[0]
    far[:rows], near[:rows] = y[:, :BLOCK], y[:, BLOCK:]
    far[rows:], near[rows:] = g[:BLOCK, :BLOCK], g[BLOCK:, BLOCK:]
    out[...] = g[:BLOCK, BLOCK:]


def cross_kernel(far0, x0, x1, near1, out):
    f0, n1 = far0[...], near1[...]
    both = dot_t(beside(f0, n1), beside(x1[...], x0[...]))
    out[0] = both[:BLOCK, :BLOCK]
    out[1] = both[BLOCK:, BLOCK:]
    out[2] = both[:BLOCK, BLOCK:]
    out[3] = dot_t(f0, n1)
    out[4] = both[BLOCK:, :BLOCK]


def last_kernel(
    sums,
    inner,
    far0,
    x0,
    x1,
    near1,
    far_rest,
    rest0,
    rest1,
    near_rest,
    along,
    down,
    swapped,
    mine_data,
    mine_basis,
    theirs,
    *scratch,
):
    basis_rows = far_rest.shape[0] - BLOCK
    gram_a = joined(far_rest[basis_rows:], sums[0], rest1[basis_rows:])
    gram_b = joined(rest0[basis_rows:], sums[1].T, near_rest[basis_rows:])
    mixed = jnp.concatenate(
        [beside(sums[2], sums[3]), beside(inner[...].T, sums[4].T)], axis=0
    )
    qa, qb = solves([gram_a, gram_b], 2, along, down, scratch)
    qa, qb = qa[:, :BLOCK], qb[:, BLOCK:]
    left = dot(qa.T, beside(gram_a, mixed))
    gram = joined(dot(left[:, :N], qa), dot(left[:, N:], qb), dot(dot(qb.T, gram_b), qb))
    (q,) = solves([gram], 3, along, down, scratch)

    def whole(data, rest):
        return jnp.concatenate([data[...], rest[:basis_rows]], axis=0)

    ya = dot_3(beside(whole(far0, far_rest), whole(x1, rest1)), qa)
    yb = dot_3(beside(whole(x0, rest0), whole(near1, near_rest)), qb)
    y = dot_3(beside(ya, yb), q)
    swap = swapped[...] > 0.0
    y = beside(
        jnp.where(swap, y[:, BLOCK:], y[:, :BLOCK]), jnp.where(swap, y[:, :BLOCK], y[:, BLOCK:])
    )
    rows, height = mine_data.shape[0], mine_basis.shape[0]
    mine_data[...] = y[:rows]
    theirs[:rows] = y[rows : 2 * rows]
    mine_basis[...] = y[2 * rows : 2 * rows + height]
    theirs[rows:] = y[2 * rows + height :]


def place_kernel(got, mine_data, mine_basis, swapped, data, basis):
    swap = swapped[...] > 0.0
    swap = beside(swap, swap)
    rows = mine_data.shape[0]
    for mine, theirs, out in (
        (mine_data[...], got[:rows], data),
        (mine_basis[...], got[rows:], basis),
    ):
        out[:, :N] = jnp.where(swap, mine, theirs)
        out[:, N:] = jnp.where(swap, theirs, mine)


def chip_groups(size):
    return [list(range(core, size, 2)) for core in range(2)]


def trade(parts):
    groups = chip_groups(lax.axis_size("rows"))
    return lax.all_to_all(parts, "rows", 0, 0, axis_index_groups=groups)


def all_slices(mine, n):
    return trade(jnp.broadcast_to(mine[None], (n,) + mine.shape))


def other_core(x):
    return lax.ppermute(x, "rows", [(i, i ^ 1) for i in range(lax.axis_size("rows"))])


def along_pairs(x, sign):
    n_rows, n_pairs = lax.axis_size("rows"), lax.axis_size("pairs")
    route = []
    for r in range(n_rows):
        step = sign if r % 2 else -sign
        for p in range(n_pairs):
            route.append((r * n_pairs + p, r * n_pairs + (p + step) % n_pairs))
    return lax.ppermute(x, ("rows", "pairs"), route)


def body(sample, column_scale, inner_order):
    row, col = lax.axis_index("rows"), lax.axis_index("pairs")
    core = row % 2
    n_pairs = lax.axis_size("pairs")
    rows, width = sample.shape
    height = W // lax.axis_size("rows")
    swapped = jnp.full((1, BLOCK), core, jnp.float32)
    own, send = start(sample, column_scale.reshape(1, width), swapped)
    other = other_core(send)
    near = along_pairs(jnp.concatenate([own, other], axis=0), 1)
    near_col = (col + jnp.where(core == 0, 1, -1)) % n_pairs

    ids = jnp.arange(height, dtype=jnp.int32)
    row_ids = jnp.concatenate([ids + row * height, ids + (row ^ 1) * height])[:, None]
    places = (jnp.arange(N, dtype=jnp.int32)[None, :] + core * BLOCK) % N + core * N
    unit = jnp.where(row_ids == places + 2 * N * col, 1.0, 0.0).astype(jnp.float32)
    near_unit = jnp.where(row_ids == places + 2 * N * near_col, 1.0, 0.0).astype(jnp.float32)

    order = ((inner_order + core * BLOCK) % N).astype(jnp.float32)
    table = np.eye(N)[:, np.concatenate([arrangement(0), arrangement(ROUNDS)])]
    table = jnp.asarray(table.astype(np.float32))
    along = dot(order, table).reshape(2 * STEPS, N)
    down = along.T

    chips = lax.axis_size("rows") // 2
    gram_rows, mixed_rows = 3 * BLOCK // chips, 2 * N // chips
    gram = call(gram_kernel, shape(3, BLOCK, BLOCK), [], own, other)
    parts = trade(gram.reshape(chips, -1, BLOCK))
    mixed = call(mixed_kernel, shape(2, N, BLOCK), [], own, other, near)
    landed = trade(
        call(
            spread_kernel,
            shape(chips, gram_rows + mixed_rows, BLOCK),
            [],
            parts,
            mixed.reshape(chips, -1, BLOCK),
        )
    )
    mixed = all_slices(landed[:, gram_rows:].sum(0), chips).reshape(2, N, BLOCK)

    q, ship = call(
        first_kernel,
        (shape(N, N), shape(N + BLOCK, BLOCK)),
        solve_scratch(1),
        landed,
        along,
        down,
    )
    ship = along_pairs(ship, 1)
    half, half_basis = shape(2 * rows, BLOCK), shape(2 * height, BLOCK)
    kept, kept_basis = call(
        keep_kernel,
        (shape(2 * rows + BLOCK, BLOCK), half_basis),
        [],
        landed,
        q,
        own,
        other,
        unit,
    )
    x0, x1, gram, q = call(
        second_kernel,
        (half, half, shape(N, N), shape(N, N)),
        solve_scratch(1),
        mixed,
        q,
        ship,
        kept,
        near,
        along,
        down,
    )

    far0, near1 = along_pairs(x0, -1), along_pairs(x1, 1)
    rest = shape(2 * height + BLOCK, BLOCK)
    rest0, rest1, inner = call(
        basis_kernel,
        (rest, rest, shape(BLOCK, BLOCK)),
        [],
        kept_basis,
        near_unit,
        ship,
        q,
        gram,
    )
    far0, near1, rest0, rest1 = lax.optimization_barrier((far0, near1, rest0, rest1))
    far_rest, near_rest = along_pairs(rest0, -1), along_pairs(rest1, 1)
    cross = call(cross_kernel, shape(5, BLOCK, BLOCK), [], far0, x0, x1, near1)
    sums = trade(cross.reshape(chips, -1, BLOCK)).sum(0)
    sums, far_rest, near_rest = lax.optimization_barrier((sums, far_rest, near_rest))
    sums = all_slices(sums, chips).reshape(5, BLOCK, BLOCK)
    mine_data, mine_basis, theirs = call(
        last_kernel,
        (shape(rows, N), shape(height, N), shape(rows + height, N)),
        solve_scratch(2),
        sums,
        inner,
        far0,
        x0,
        x1,
        near1,
        far_rest,
        rest0,
        rest1,
        near_rest,
        along,
        down,
        swapped,
    )
    return call(
        place_kernel,
        (shape(rows, width), shape(height, width)),
        [],
        other_core(theirs),
        mine_data,
        mine_basis,
        swapped,
    )


def solution(mesh):
    return jax.shard_map(
        body,
        mesh=mesh,
        in_specs=(P("rows", "pairs"), P("pairs"), P()),
        out_specs=(P("rows", "pairs"), P("rows", "pairs")),
        check_vma=False,
    )
```

```python
import functools

import jax
import jax.numpy as jnp
import numpy as np
from jax import lax
from jax.experimental import pallas as pl
from jax.experimental.pallas import tpu as pltpu
from jax.sharding import PartitionSpec as P

BLOCK = 128
N = 2 * BLOCK
W = 4096
STEPS = 4
ROUNDS = 8
HIGHEST = lax.Precision.HIGHEST
VMEM = pl.BlockSpec(memory_space=pltpu.VMEM)


def arrangement(r):
    m = N - 1
    first = [m] + [(r + i) % m for i in range(1, BLOCK)]
    second = [r % m] + [(r - i) % m for i in range(1, BLOCK)]
    return np.array(first + second)


def shape(*dims):
    return jax.ShapeDtypeStruct(dims, jnp.float32)


def call(kernel, out_shape, scratch, *operands):
    return pl.pallas_call(
        kernel,
        out_shape=out_shape,
        in_specs=[VMEM] * len(operands),
        out_specs=jax.tree.map(lambda _: VMEM, out_shape),
        scratch_shapes=scratch,
        compiler_params=pltpu.CompilerParams(vmem_limit_bytes=40 * 2**20),
    )(*operands)


def solve_scratch(count):
    block = pltpu.VMEM((2, count, BLOCK + 16, BLOCK), jnp.float32)
    return [block] * 8


def dot(left, right):
    return jnp.dot(left, right, precision=HIGHEST, preferred_element_type=jnp.float32)


def dot_t(left, right):
    return lax.dot_general(
        left,
        right,
        (((0,), (0,)), ((), ())),
        precision=HIGHEST,
        preferred_element_type=jnp.float32,
    )


def beside(*parts):
    return jnp.concatenate(parts, axis=1)


def joined(g00, g01, g11):
    return jnp.concatenate([beside(g00, g01), beside(g01.T, g11)], axis=0)


def thirds(x):
    high = x.astype(jnp.bfloat16)
    rest = x - high.astype(jnp.float32)
    middle = rest.astype(jnp.bfloat16)
    return high, middle, (rest - middle.astype(jnp.float32)).astype(jnp.bfloat16)


def dot_16(left, right):
    return jnp.dot(left, right, preferred_element_type=jnp.float32)


def pick_columns(x, units):
    high, middle, low = thirds(x)
    return dot_16(high, units) + (dot_16(middle, units) + dot_16(low, units))


def pick_rows(units, x):
    high, middle, low = thirds(x)
    return dot_16(units, high) + (dot_16(units, middle) + dot_16(units, low))


def dot_3(left, right):
    l_high, l_low, _ = thirds(left)
    r_high, r_low, _ = thirds(right)
    return dot_16(l_high, r_high) + (dot_16(l_high, r_low) + dot_16(l_low, r_high))


def turn(p, q, c, s):
    return c * p - s * q, s * p + c * q


def advance(p, q):
    at = lax.broadcasted_iota(jnp.int32, p.shape, 1)
    p_back = pltpu.roll(p, BLOCK - 1, 1)
    q_on = pltpu.roll(q, 1, 1)
    new_p = jnp.where(at == 0, p, jnp.where(at == BLOCK - 1, q, p_back))
    new_q = jnp.where(at == 0, p_back, q_on)
    return new_p, new_q


def angles(gpp, cross, gqq):
    d = gqq - gpp
    root = jnp.sqrt(d * d + 4.0 * cross * cross)
    t = 2.0 * cross * d / ((jnp.abs(d) + root) * root + 1e-06 * (gpp + gqq) * (gpp + gqq))
    w = 1.0 + t * t
    c = lax.rsqrt(w)
    c = c * (1.5 - 0.5 * w * c * c)
    return c, t * c


def solves(grams, step, along_ref, down_ref, scratch, beside_rounds=None):
    along = along_ref[2 * step : 2 * step + 1]
    down = down_ref[:, 2 * step : 2 * step + 2]
    ga, gb, gc, gd, qa, qb, qc, qd = scratch
    count = len(grams)
    lane = lax.broadcasted_iota(jnp.int32, (N, N), 1).astype(jnp.float32)
    sub = lax.broadcasted_iota(jnp.int32, (N, N), 0).astype(jnp.float32)
    take = jnp.where(sub == along, 1.0, 0.0).astype(jnp.bfloat16)
    take_t = jnp.where(lane == down[:, 0:1], 1.0, 0.0)
    back_t = jnp.where(lane == down[:, 1:2], 1.0, 0.0).astype(jnp.bfloat16)
    i0 = lax.broadcasted_iota(jnp.int32, (BLOCK, BLOCK), 0)
    i1 = lax.broadcasted_iota(jnp.int32, (BLOCK, BLOCK), 1)
    at = lax.broadcasted_iota(jnp.int32, (1, BLOCK), 1)
    body = pl.ds(8, BLOCK)
    state = []
    for k, gram in enumerate(grams):
        placed = pick_rows(take_t.astype(jnp.bfloat16), pick_columns(gram, take))
        a, b = placed[:BLOCK, :BLOCK], placed[:BLOCK, BLOCK:]
        c_, d_ = placed[BLOCK:, :BLOCK], placed[BLOCK:, BLOCK:]
        ga[0, k, body], gb[0, k, body], gc[0, k, body], gd[0, k, body] = a, b, c_, d_
        qa[0, k, body], qb[0, k, body] = take_t[:BLOCK, :BLOCK], take_t[:BLOCK, BLOCK:]
        qc[0, k, body], qd[0, k, body] = take_t[BLOCK:, :BLOCK], take_t[BLOCK:, BLOCK:]
        on = i0 == i1

        def diagonal(m):
            return jnp.sum(jnp.where(on, m, 0.0), axis=0, keepdims=True)

        state.append((diagonal(a), diagonal(b), diagonal(d_)))

    def one_round(old, new, k, gpp, cross, gqq):
        c, s = angles(gpp, cross, gqq)
        a, b, c_, d_ = ga[old, k, body], gb[old, k, body], gc[old, k, body], gd[old, k, body]
        on = i0 == i1
        c_col = jnp.sum(jnp.where(on, c, 0.0), axis=1, keepdims=True)
        s_col = jnp.sum(jnp.where(on, s, 0.0), axis=1, keepdims=True)
        low = c * gpp - s * cross
        new_pp = c * low - s * (c * cross - s * gqq)
        new_qq = s * (s * gpp + c * cross) + c * (s * cross + c * gqq)
        new_pp, new_qq = advance(new_pp, new_qq)
        off = (i0 == i1 + 2) | ((i0 == BLOCK - 1) & (i1 == BLOCK - 2))

        def beyond(m):
            return jnp.sum(jnp.where(off, m, 0.0), axis=0, keepdims=True)

        ea, eb, ec, ed = (pltpu.roll(beyond(m), 1, 1) for m in (a, b, c_, d_))
        ra, rb, rc, rd = (pltpu.roll(m[0:1], BLOCK - 1, 1) for m in (a, b, c_, d_))
        end, start = at == BLOCK - 1, at == 0
        cl, sl = pltpu.roll(c, 1, 1), pltpu.roll(s, 1, 1)
        cr, sr = pltpu.roll(c, BLOCK - 1, 1), pltpu.roll(s, BLOCK - 1, 1)
        cu, su = jnp.where(end, s, cr), jnp.where(end, -c, sr)
        main = cu * (sl * ea + cl * eb) - su * (sl * ec + cl * ed)
        tip = c * (cr * ra - sr * rb) - s * (cr * rc - sr * rd)
        new_cross = jnp.where(start, tip, main)
        a, b = advance(*turn(a, b, c, s))
        c_, d_ = advance(*turn(c_, d_, c, s))
        qs = [x[old, k, body] for x in (qa, qc, qb, qd)]
        for first, second, top, bottom in (
            (a, c_, ga, gc),
            (b, d_, gb, gd),
            (qs[0], qs[1], qa, qc),
            (qs[2], qs[3], qb, qd),
        ):
            up, under = turn(first, second, c_col, s_col)
            top[new, k, pl.ds(7, BLOCK)] = up
            top[new, k, pl.ds(8, 1)] = up[0:1]
            top[new, k, pl.ds(BLOCK + 7, 1)] = under[BLOCK - 1 :]
            bottom[new, k, pl.ds(9, BLOCK)] = under
            bottom[new, k, pl.ds(8, 1)] = up[1:2]
        return new_pp, new_cross, new_qq

    def two_rounds(i, state):
        if beside_rounds is not None:
            beside_rounds(i)
        state = [one_round(0, 1, k, *state[k]) for k in range(count)]
        return [one_round(1, 0, k, *state[k]) for k in range(count)]

    lax.fori_loop(0, ROUNDS // 2, two_rounds, state)
    turned = [
        [jnp.concatenate([top[0, k, body], bottom[0, k, body]], axis=0).T for k in range(count)]
        for top, bottom in ((qa, qc), (qb, qd))
    ]
    return [
        pick_columns(jnp.concatenate([turned[0][k], turned[1][k]], axis=0), back_t)
        for k in range(count)
    ]


def on_core_1():
    return lax.axis_index("rows") % 2 == 1


def start_kernel(sample, scale, own, send):
    x = sample[...] * scale[...]
    blocks = [x[:, k * BLOCK : (k + 1) * BLOCK] for k in range(4)]
    swap = on_core_1()
    for k, far in ((0, 3), (1, 2)):
        at = slice(k * BLOCK, (k + 1) * BLOCK)
        own[:, at] = jnp.where(swap, blocks[far], blocks[k])
        send[:, at] = jnp.where(swap, blocks[k], blocks[far])


def gram_kernel(own, other, out):
    x = jnp.concatenate([own[...], other[...]], axis=0)
    gram = dot_t(x, x)
    out[0], out[1], out[2] = gram[:BLOCK, :BLOCK], gram[:BLOCK, BLOCK:], gram[BLOCK:, BLOCK:]


def mixed_kernel(own, other, near, out):
    x = jnp.concatenate([own[...], other[...]], axis=0)
    mixed = dot_t(near[...], x)
    out[0], out[1] = mixed[:, :BLOCK], mixed[:, BLOCK:]


def spread_kernel(parts, mixed, out):
    n, m = parts.shape[0], parts.shape[1]
    size = N // n
    total = parts[0]
    for k in range(1, n):
        total = total + parts[k]
    for k in range(n):
        out[k, :m] = total
        for half in range(2):
            at = pl.ds(m + half * size, size)
            out[k, at] = mixed[half, k * size : (k + 1) * size]


def share_kernel(landed, q, out):
    n, m = landed.shape[0], 3 * BLOCK // landed.shape[0]
    size = N // n
    total = landed[0, m:]
    for k in range(1, n):
        total = total + landed[k, m:]
    mine = dot(beside(total[:size], total[size:]), q[:, :BLOCK])
    for k in range(n):
        out[k] = mine


def first_gram(landed, m):
    sums = landed[:, :m].reshape(3, BLOCK, BLOCK)
    return joined(sums[0], sums[1], sums[2])


def first_kernel(landed, along, down, q_out, ship, *scratch):
    gram = first_gram(landed, 3 * BLOCK // landed.shape[0])
    (q,) = solves([gram], 0, along, down, scratch)
    q_out[...] = q
    q1 = q[:, BLOCK:]
    ship[:N] = q1
    ship[N:] = dot_t(q1, dot(gram, q1))


def keep_kernel(landed, q, own, other, unit, kept, kept_basis):
    q0 = q[:, :BLOCK]
    rows = kept.shape[0] - BLOCK
    kept[:rows] = dot(jnp.concatenate([own[...], other[...]], axis=0), q0)
    kept[rows:] = dot_t(q0, dot(first_gram(landed, 3 * BLOCK // landed.shape[0]), q0))
    kept_basis[...] = dot(unit[...], q0)


def second_kernel(mixed, ship, kept, near, along, down, x0, x1, gram_out, q_out, turned1, *scratch):
    q1 = ship[:N]
    cross = dot_t(mixed[...], q1)
    rows = near.shape[0]
    gram = joined(kept[rows:], cross, ship[N:])
    gram_out[...] = gram
    part = rows // (ROUNDS // 2)

    def near_rows(k):
        at = pl.ds(pl.multiple_of(k * part, part), part)
        turned1[at] = dot(near[at], ship[:N])

    (turned,) = solves([gram], 1, along, down, scratch, near_rows)
    q_out[...] = turned
    y = dot(beside(kept[:rows], turned1[...]), turned)
    x0[...] = y[:, :BLOCK]
    x1[...] = y[:, BLOCK:]


def basis_kernel(kept, unit, ship, q, gram, far, near, out):
    y = dot(beside(kept[...], dot(unit[...], ship[:N])), q[...])
    g = dot_t(q[...], dot(gram[...], q[...]))
    rows = y.shape[0]
    far[:rows], near[:rows] = y[:, :BLOCK], y[:, BLOCK:]
    far[rows:], near[rows:] = g[:BLOCK, :BLOCK], g[BLOCK:, BLOCK:]
    out[...] = g[:BLOCK, BLOCK:]


def cross_kernel(far0, x0, x1, near1, out):
    f0, n1 = far0[...], near1[...]
    both = dot_t(beside(f0, n1), beside(x1[...], x0[...]))
    out[0] = both[:BLOCK, :BLOCK]
    out[1] = both[BLOCK:, BLOCK:]
    out[2] = both[:BLOCK, BLOCK:]
    out[3] = dot_t(f0, n1)
    out[4] = both[BLOCK:, :BLOCK]


def last_kernel(
    sums,
    inner,
    far0,
    x0,
    x1,
    near1,
    far_rest,
    rest0,
    rest1,
    near_rest,
    along,
    down,
    mine_data,
    mine_basis,
    theirs,
    ya,
    yb,
    *scratch,
):
    basis_rows = far_rest.shape[0] - BLOCK
    gram_a = joined(far_rest[basis_rows:], sums[0], rest1[basis_rows:])
    gram_b = joined(rest0[basis_rows:], sums[1].T, near_rest[basis_rows:])
    mixed = jnp.concatenate(
        [beside(sums[2], sums[3]), beside(inner[...].T, sums[4].T)], axis=0
    )
    qa, qb = solves([gram_a, gram_b], 2, along, down, scratch)
    qa, qb = qa[:, :BLOCK], qb[:, BLOCK:]
    left = dot(qa.T, beside(gram_a, mixed))
    gram = joined(dot(left[:, :N], qa), dot(left[:, N:], qb), dot(dot(qb.T, gram_b), qb))
    data_rows = far0.shape[0]

    def quarter(k):
        for first, count, pairs in (
            (0, data_rows, ((far0, x1, qa, ya), (x0, near1, qb, yb))),
            (data_rows, basis_rows, ((far_rest, rest1, qa, ya), (rest0, near_rest, qb, yb))),
        ):
            part = count // (ROUNDS // 2)
            at = pl.ds(pl.multiple_of(k * part, part), part)
            to = pl.ds(pl.multiple_of(first + k * part, part), part)
            for left, right, q, out in pairs:
                out[to] = dot_3(beside(left[at], right[at]), q)

    (q,) = solves([gram], 3, along, down, scratch, quarter)
    y = dot_3(beside(ya[...], yb[...]), q)
    swap = on_core_1()
    y = beside(
        jnp.where(swap, y[:, BLOCK:], y[:, :BLOCK]), jnp.where(swap, y[:, :BLOCK], y[:, BLOCK:])
    )
    rows, height = mine_data.shape[0], mine_basis.shape[0]
    mine_data[...] = y[:rows]
    theirs[:rows] = y[rows : 2 * rows]
    mine_basis[...] = y[2 * rows : 2 * rows + height]
    theirs[rows:] = y[2 * rows + height :]


def place_kernel(got, mine_data, mine_basis, data, basis):
    swap = on_core_1()
    rows = mine_data.shape[0]
    for mine, theirs, out in (
        (mine_data[...], got[:rows], data),
        (mine_basis[...], got[rows:], basis),
    ):
        out[:, :N] = jnp.where(swap, mine, theirs)
        out[:, N:] = jnp.where(swap, theirs, mine)


def chip_groups(size):
    return [list(range(core, size, 2)) for core in range(2)]


def trade(parts):
    groups = chip_groups(lax.axis_size("rows"))
    return lax.all_to_all(parts, "rows", 0, 0, axis_index_groups=groups)


def all_slices(mine, n):
    return trade(jnp.broadcast_to(mine[None], (n,) + mine.shape))


def other_core(x):
    return lax.ppermute(x, "rows", [(i, i ^ 1) for i in range(lax.axis_size("rows"))])


def along_pairs(x, sign):
    n_rows, n_pairs = lax.axis_size("rows"), lax.axis_size("pairs")
    route = []
    for r in range(n_rows):
        step = sign if r % 2 else -sign
        for p in range(n_pairs):
            route.append((r * n_pairs + p, r * n_pairs + (p + step) % n_pairs))
    return lax.ppermute(x, ("rows", "pairs"), route)


def body(sample, column_scale, inner_order):
    row, col = lax.axis_index("rows"), lax.axis_index("pairs")
    core = row % 2
    n_pairs = lax.axis_size("pairs")
    rows, width = sample.shape
    height = W // lax.axis_size("rows")
    pair = (shape(rows, N), shape(rows, N))
    own, send = call(start_kernel, pair, [], sample, column_scale.reshape(1, width))
    other = other_core(send)
    near = along_pairs(jnp.concatenate([own, other], axis=0), 1)
    near_col = (col + jnp.where(core == 0, 1, -1)) % n_pairs

    ids = jnp.arange(height, dtype=jnp.int32)
    row_ids = jnp.concatenate([ids + row * height, ids + (row ^ 1) * height])[:, None]
    places = (jnp.arange(N, dtype=jnp.int32)[None, :] + core * BLOCK) % N + core * N
    unit = jnp.where(row_ids == places + 2 * N * col, 1.0, 0.0).astype(jnp.float32)
    near_unit = jnp.where(row_ids == places + 2 * N * near_col, 1.0, 0.0).astype(jnp.float32)

    order = ((inner_order + core * BLOCK) % N).astype(jnp.float32)
    table = np.eye(N)[:, np.concatenate([arrangement(0), arrangement(ROUNDS)])]
    table = jnp.asarray(table.astype(np.float32))
    along = dot(order, table).reshape(2 * STEPS, N)
    down = along.T

    chips = lax.axis_size("rows") // 2
    gram_rows, mixed_rows = 3 * BLOCK // chips, 2 * N // chips
    gram = call(gram_kernel, shape(3, BLOCK, BLOCK), [], own, other)
    parts = trade(gram.reshape(chips, -1, BLOCK))
    mixed = call(mixed_kernel, shape(2, N, BLOCK), [], own, other, near)
    landed = trade(
        call(
            spread_kernel,
            shape(chips, gram_rows + mixed_rows, BLOCK),
            [],
            parts,
            mixed,
        )
    )
    q, ship = call(
        first_kernel,
        (shape(N, N), shape(N + BLOCK, BLOCK)),
        solve_scratch(1),
        landed,
        along,
        down,
    )
    ship = along_pairs(ship, 1)
    mixed = trade(call(share_kernel, shape(chips, N // chips, BLOCK), [], landed, q))
    mixed = mixed.reshape(N, BLOCK)
    half, half_basis = shape(2 * rows, BLOCK), shape(2 * height, BLOCK)
    kept, kept_basis = call(
        keep_kernel,
        (shape(2 * rows + BLOCK, BLOCK), half_basis),
        [],
        landed,
        q,
        own,
        other,
        unit,
    )
    x0, x1, gram, q = call(
        second_kernel,
        (half, half, shape(N, N), shape(N, N)),
        [pltpu.VMEM(half.shape, jnp.float32)] + solve_scratch(1),
        mixed,
        ship,
        kept,
        near,
        along,
        down,
    )

    far0, near1 = along_pairs(x0, -1), along_pairs(x1, 1)
    rest = shape(2 * height + BLOCK, BLOCK)
    rest0, rest1, inner = call(
        basis_kernel,
        (rest, rest, shape(BLOCK, BLOCK)),
        [],
        kept_basis,
        near_unit,
        ship,
        q,
        gram,
    )
    far0, near1, rest0, rest1 = lax.optimization_barrier((far0, near1, rest0, rest1))
    far_rest, near_rest = along_pairs(rest0, -1), along_pairs(rest1, 1)
    cross = call(cross_kernel, shape(5, BLOCK, BLOCK), [], far0, x0, x1, near1)
    sums = trade(cross.reshape(chips, -1, BLOCK)).sum(0)
    sums, far_rest, near_rest = lax.optimization_barrier((sums, far_rest, near_rest))
    sums = all_slices(sums, chips).reshape(5, BLOCK, BLOCK)
    mine_data, mine_basis, theirs = call(
        last_kernel,
        (shape(rows, N), shape(height, N), shape(rows + height, N)),
        [pltpu.VMEM((2 * (rows + height), BLOCK), jnp.float32)] * 2 + solve_scratch(2),
        sums,
        inner,
        far0,
        x0,
        x1,
        near1,
        far_rest,
        rest0,
        rest1,
        near_rest,
        along,
        down,
    )
    return call(
        place_kernel,
        (shape(rows, width), shape(height, width)),
        [],
        other_core(theirs),
        mine_data,
        mine_basis,
    )


def solution(mesh):
    return jax.shard_map(
        body,
        mesh=mesh,
        in_specs=(P("rows", "pairs"), P("pairs"), P()),
        out_specs=(P("rows", "pairs"), P("rows", "pairs")),
        check_vma=False,
    )
```

```python
import functools

import jax
import jax.numpy as jnp
import numpy as np
from jax import lax
from jax.experimental import pallas as pl
from jax.experimental.pallas import tpu as pltpu
from jax.sharding import PartitionSpec as P

BLOCK = 128
N = 2 * BLOCK
W = 4096
STEPS = 4
ROUNDS = 8
HIGHEST = lax.Precision.HIGHEST
VMEM = pl.BlockSpec(memory_space=pltpu.VMEM)


def arrangement(r):
    m = N - 1
    first = [m] + [(r + i) % m for i in range(1, BLOCK)]
    second = [r % m] + [(r - i) % m for i in range(1, BLOCK)]
    return np.array(first + second)


def shape(*dims):
    return jax.ShapeDtypeStruct(dims, jnp.float32)


def call(kernel, out_shape, scratch, *operands):
    return pl.pallas_call(
        kernel,
        out_shape=out_shape,
        in_specs=[VMEM] * len(operands),
        out_specs=jax.tree.map(lambda _: VMEM, out_shape),
        scratch_shapes=scratch,
        compiler_params=pltpu.CompilerParams(vmem_limit_bytes=40 * 2**20),
    )(*operands)


def solve_scratch(count):
    block = pltpu.VMEM((2, count, BLOCK + 16, BLOCK), jnp.float32)
    return [block] * 8


def dot(left, right):
    return jnp.dot(left, right, precision=HIGHEST, preferred_element_type=jnp.float32)


def dot_t(left, right):
    return lax.dot_general(
        left,
        right,
        (((0,), (0,)), ((), ())),
        precision=HIGHEST,
        preferred_element_type=jnp.float32,
    )


def beside(*parts):
    return jnp.concatenate(parts, axis=1)


def joined(g00, g01, g11):
    return jnp.concatenate([beside(g00, g01), beside(g01.T, g11)], axis=0)


def thirds(x):
    high = x.astype(jnp.bfloat16)
    rest = x - high.astype(jnp.float32)
    middle = rest.astype(jnp.bfloat16)
    return high, middle, (rest - middle.astype(jnp.float32)).astype(jnp.bfloat16)


def dot_16(left, right):
    return jnp.dot(left, right, preferred_element_type=jnp.float32)


def pick_columns(x, units):
    high, middle, low = thirds(x)
    return dot_16(high, units) + (dot_16(middle, units) + dot_16(low, units))


def pick_rows(units, x):
    high, middle, low = thirds(x)
    return dot_16(units, high) + (dot_16(units, middle) + dot_16(units, low))


def dot_3(left, right):
    l_high, l_low, _ = thirds(left)
    r_high, r_low, _ = thirds(right)
    return dot_16(l_high, r_high) + (dot_16(l_high, r_low) + dot_16(l_low, r_high))


def turn(p, q, c, s):
    return c * p - s * q, s * p + c * q


def advance(p, q):
    at = lax.broadcasted_iota(jnp.int32, p.shape, 1)
    p_back = pltpu.roll(p, BLOCK - 1, 1)
    q_on = pltpu.roll(q, 1, 1)
    new_p = jnp.where(at == 0, p, jnp.where(at == BLOCK - 1, q, p_back))
    new_q = jnp.where(at == 0, p_back, q_on)
    return new_p, new_q


def angles(gpp, cross, gqq):
    d = gqq - gpp
    root = jnp.sqrt(d * d + 4.0 * cross * cross)
    t = 2.0 * cross * d / ((jnp.abs(d) + root) * root + 1e-06 * (gpp + gqq) * (gpp + gqq))
    w = 1.0 + t * t
    c = lax.rsqrt(w)
    c = c * (1.5 - 0.5 * w * c * c)
    return c, t * c


def solves(grams, step, along_ref, down_ref, scratch, beside_rounds=None):
    along = along_ref[2 * step : 2 * step + 1]
    down = down_ref[:, 2 * step : 2 * step + 2]
    ga, gb, gc, gd, qa, qb, qc, qd = scratch
    count = len(grams)
    lane = lax.broadcasted_iota(jnp.int32, (N, N), 1).astype(jnp.float32)
    sub = lax.broadcasted_iota(jnp.int32, (N, N), 0).astype(jnp.float32)
    take = jnp.where(sub == along, 1.0, 0.0).astype(jnp.bfloat16)
    take_t = jnp.where(lane == down[:, 0:1], 1.0, 0.0)
    back_t = jnp.where(lane == down[:, 1:2], 1.0, 0.0).astype(jnp.bfloat16)
    i0 = lax.broadcasted_iota(jnp.int32, (BLOCK, BLOCK), 0)
    i1 = lax.broadcasted_iota(jnp.int32, (BLOCK, BLOCK), 1)
    at = lax.broadcasted_iota(jnp.int32, (1, BLOCK), 1)
    body = pl.ds(8, BLOCK)
    state = []
    for k, gram in enumerate(grams):
        placed = pick_rows(take_t.astype(jnp.bfloat16), pick_columns(gram, take))
        a, b = placed[:BLOCK, :BLOCK], placed[:BLOCK, BLOCK:]
        c_, d_ = placed[BLOCK:, :BLOCK], placed[BLOCK:, BLOCK:]
        ga[0, k, body], gb[0, k, body], gc[0, k, body], gd[0, k, body] = a, b, c_, d_
        qa[0, k, body], qb[0, k, body] = take_t[:BLOCK, :BLOCK], take_t[:BLOCK, BLOCK:]
        qc[0, k, body], qd[0, k, body] = take_t[BLOCK:, :BLOCK], take_t[BLOCK:, BLOCK:]
        on = i0 == i1

        def diagonal(m):
            return jnp.sum(jnp.where(on, m, 0.0), axis=0, keepdims=True)

        state.append((diagonal(a), diagonal(b), diagonal(d_)))

    def one_round(old, new, k, gpp, cross, gqq):
        c, s = angles(gpp, cross, gqq)
        a, b, c_, d_ = ga[old, k, body], gb[old, k, body], gc[old, k, body], gd[old, k, body]
        on = i0 == i1
        c_col = jnp.sum(jnp.where(on, c, 0.0), axis=1, keepdims=True)
        s_col = jnp.sum(jnp.where(on, s, 0.0), axis=1, keepdims=True)
        low = c * gpp - s * cross
        new_pp = c * low - s * (c * cross - s * gqq)
        new_qq = s * (s * gpp + c * cross) + c * (s * cross + c * gqq)
        new_pp, new_qq = advance(new_pp, new_qq)
        off = (i0 == i1 + 2) | ((i0 == BLOCK - 1) & (i1 == BLOCK - 2))

        def beyond(m):
            return jnp.sum(jnp.where(off, m, 0.0), axis=0, keepdims=True)

        ea, eb, ec, ed = (pltpu.roll(beyond(m), 1, 1) for m in (a, b, c_, d_))
        ra, rb, rc, rd = (pltpu.roll(m[0:1], BLOCK - 1, 1) for m in (a, b, c_, d_))
        end, start = at == BLOCK - 1, at == 0
        cl, sl = pltpu.roll(c, 1, 1), pltpu.roll(s, 1, 1)
        cr, sr = pltpu.roll(c, BLOCK - 1, 1), pltpu.roll(s, BLOCK - 1, 1)
        cu, su = jnp.where(end, s, cr), jnp.where(end, -c, sr)
        main = cu * (sl * ea + cl * eb) - su * (sl * ec + cl * ed)
        tip = c * (cr * ra - sr * rb) - s * (cr * rc - sr * rd)
        new_cross = jnp.where(start, tip, main)
        a, b = advance(*turn(a, b, c, s))
        c_, d_ = advance(*turn(c_, d_, c, s))
        qs = [x[old, k, body] for x in (qa, qc, qb, qd)]
        for first, second, top, bottom in (
            (a, c_, ga, gc),
            (b, d_, gb, gd),
            (qs[0], qs[1], qa, qc),
            (qs[2], qs[3], qb, qd),
        ):
            up, under = turn(first, second, c_col, s_col)
            top[new, k, pl.ds(7, BLOCK)] = up
            top[new, k, pl.ds(8, 1)] = up[0:1]
            top[new, k, pl.ds(BLOCK + 7, 1)] = under[BLOCK - 1 :]
            bottom[new, k, pl.ds(9, BLOCK)] = under
            bottom[new, k, pl.ds(8, 1)] = up[1:2]
        return new_pp, new_cross, new_qq

    def two_rounds(i, state):
        if beside_rounds is not None:
            beside_rounds(i)
        state = [one_round(0, 1, k, *state[k]) for k in range(count)]
        return [one_round(1, 0, k, *state[k]) for k in range(count)]

    lax.fori_loop(0, ROUNDS // 2, two_rounds, state)
    turned = [
        [jnp.concatenate([top[0, k, body], bottom[0, k, body]], axis=0).T for k in range(count)]
        for top, bottom in ((qa, qc), (qb, qd))
    ]
    return [
        pick_columns(jnp.concatenate([turned[0][k], turned[1][k]], axis=0), back_t)
        for k in range(count)
    ]


def on_core_1():
    return lax.axis_index("rows") % 2 == 1


def start_kernel(sample, scale, own, send):
    x = sample[...] * scale[...]
    blocks = [x[:, k * BLOCK : (k + 1) * BLOCK] for k in range(4)]
    swap = on_core_1()
    for k, far in ((0, 3), (1, 2)):
        at = slice(k * BLOCK, (k + 1) * BLOCK)
        own[:, at] = jnp.where(swap, blocks[far], blocks[k])
        send[:, at] = jnp.where(swap, blocks[k], blocks[far])


def gram_kernel(own, other, out):
    x = jnp.concatenate([own[...], other[...]], axis=0)
    gram = dot_t(x, x)
    out[0], out[1], out[2] = gram[:BLOCK, :BLOCK], gram[:BLOCK, BLOCK:], gram[BLOCK:, BLOCK:]


def mixed_kernel(own, other, near, keep, give):
    x = jnp.concatenate([own[...], other[...]], axis=0)
    mixed = dot_t(near[...], x)
    upper = lax.axis_index("rows") // 2 % 2 == 1
    for half in range(2):
        at = slice(half * BLOCK, (half + 1) * BLOCK)
        top, bottom = mixed[:BLOCK, at], mixed[BLOCK:, at]
        keep[half] = jnp.where(upper, bottom, top)
        give[half] = jnp.where(upper, top, bottom)


def spread_kernel(parts, keep, got, out):
    n, m = parts.shape[0], parts.shape[1]
    size = BLOCK // n
    total = parts[0]
    for k in range(1, n):
        total = total + parts[k]
    mixed = [keep[half] + got[half] for half in range(2)]
    for k in range(n):
        out[k, :m] = total
        for half in range(2):
            out[k, pl.ds(m + half * size, size)] = mixed[half][k * size : (k + 1) * size]


def share_kernel(landed, q, out):
    n, m = landed.shape[0], 3 * BLOCK // landed.shape[0]
    size = BLOCK // n
    rows = []
    for upper in range(2):
        total = landed[upper, m:]
        for k in range(upper + 2, n, 2):
            total = total + landed[k, m:]
        rows.append(beside(total[:size], total[size:]))
    mine = dot(jnp.concatenate(rows, axis=0), q[:, :BLOCK])
    for k in range(n):
        out[k] = mine


def first_gram(landed, m):
    sums = landed[:, :m].reshape(3, BLOCK, BLOCK)
    return joined(sums[0], sums[1], sums[2])


def first_kernel(landed, along, down, q_out, ship, *scratch):
    gram = first_gram(landed, 3 * BLOCK // landed.shape[0])
    (q,) = solves([gram], 0, along, down, scratch)
    q_out[...] = q
    q1 = q[:, BLOCK:]
    ship[:N] = q1
    ship[N:] = dot_t(q1, dot(gram, q1))


def keep_kernel(landed, q, own, other, unit, kept, kept_basis):
    q0 = q[:, :BLOCK]
    rows = kept.shape[0] - BLOCK
    kept[:rows] = dot(jnp.concatenate([own[...], other[...]], axis=0), q0)
    kept[rows:] = dot_t(q0, dot(first_gram(landed, 3 * BLOCK // landed.shape[0]), q0))
    kept_basis[...] = dot(unit[...], q0)


def second_kernel(mixed, ship, kept, near, along, down, x0, x1, gram_out, q_out, turned1, *scratch):
    q1 = ship[:N]
    size = mixed.shape[1] // 2
    cross = dot_t(mixed[:, :size].reshape(BLOCK, BLOCK), q1[:BLOCK]) + dot_t(
        mixed[:, size:].reshape(BLOCK, BLOCK), q1[BLOCK:]
    )
    rows = near.shape[0]
    gram = joined(kept[rows:], cross, ship[N:])
    gram_out[...] = gram
    part = rows // (ROUNDS // 2)

    def near_rows(k):
        at = pl.ds(pl.multiple_of(k * part, part), part)
        turned1[at] = dot(near[at], ship[:N])

    (turned,) = solves([gram], 1, along, down, scratch, near_rows)
    q_out[...] = turned
    y = dot(beside(kept[:rows], turned1[...]), turned)
    x0[...] = y[:, :BLOCK]
    x1[...] = y[:, BLOCK:]


def basis_kernel(kept, unit, ship, q, gram, far, near, out):
    y = dot(beside(kept[...], dot(unit[...], ship[:N])), q[...])
    g = dot_t(q[...], dot(gram[...], q[...]))
    rows = y.shape[0]
    far[:rows], near[:rows] = y[:, :BLOCK], y[:, BLOCK:]
    far[rows:], near[rows:] = g[:BLOCK, :BLOCK], g[BLOCK:, BLOCK:]
    out[...] = g[:BLOCK, BLOCK:]


def cross_kernel(far0, x0, x1, near1, out):
    f0, n1 = far0[...], near1[...]
    both = dot_t(beside(f0, n1), beside(x1[...], x0[...]))
    out[0] = both[:BLOCK, :BLOCK]
    out[1] = both[BLOCK:, BLOCK:]
    out[2] = both[:BLOCK, BLOCK:]
    out[3] = dot_t(f0, n1)
    out[4] = both[BLOCK:, :BLOCK]


def last_kernel(
    sums,
    inner,
    far0,
    x0,
    x1,
    near1,
    far_rest,
    rest0,
    rest1,
    near_rest,
    along,
    down,
    theirs,
    ya,
    yb,
    q_out,
    *scratch,
):
    basis_rows = far_rest.shape[0] - BLOCK
    gram_a = joined(far_rest[basis_rows:], sums[0], rest1[basis_rows:])
    gram_b = joined(rest0[basis_rows:], sums[1].T, near_rest[basis_rows:])
    mixed = jnp.concatenate(
        [beside(sums[2], sums[3]), beside(inner[...].T, sums[4].T)], axis=0
    )
    qa, qb = solves([gram_a, gram_b], 2, along, down, scratch)
    qa, qb = qa[:, :BLOCK], qb[:, BLOCK:]
    left = dot(qa.T, beside(gram_a, mixed))
    gram = joined(dot(left[:, :N], qa), dot(left[:, N:], qb), dot(dot(qb.T, gram_b), qb))
    data_rows = far0.shape[0]

    def quarter(k):
        for first, count, pairs in (
            (0, data_rows, ((far0, x1, qa, ya), (x0, near1, qb, yb))),
            (data_rows, basis_rows, ((far_rest, rest1, qa, ya), (rest0, near_rest, qb, yb))),
        ):
            part = count // (ROUNDS // 2)
            at = pl.ds(pl.multiple_of(k * part, part), part)
            to = pl.ds(pl.multiple_of(first + k * part, part), part)
            for left, right, q, out in pairs:
                out[to] = dot_3(beside(left[at], right[at]), q)

    (q,) = solves([gram], 3, along, down, scratch, quarter)
    q_out[...] = q
    half = data_rows // 2
    theirs[:half] = turned_rows(ya, yb, q, half, half)
    theirs[half:] = turned_rows(ya, yb, q, data_rows + basis_rows // 2, basis_rows // 2)


def turned_rows(ya, yb, q, first, count):
    at = pl.ds(first, count)
    y = dot_3(beside(ya[at], yb[at]), q)
    swap = on_core_1()
    return beside(
        jnp.where(swap, y[:, BLOCK:], y[:, :BLOCK]), jnp.where(swap, y[:, :BLOCK], y[:, BLOCK:])
    )


def mine_kernel(ya, yb, q, data, basis):
    rows, height = data.shape[0], basis.shape[0]
    data[...] = turned_rows(ya, yb, q[...], 0, rows)
    basis[...] = turned_rows(ya, yb, q[...], 2 * rows, height)


def place_kernel(got, mine_data, mine_basis, data, basis):
    swap = on_core_1()
    rows = mine_data.shape[0]
    for mine, theirs, out in (
        (mine_data[...], got[:rows], data),
        (mine_basis[...], got[rows:], basis),
    ):
        out[:, :N] = jnp.where(swap, mine, theirs)
        out[:, N:] = jnp.where(swap, theirs, mine)


def chip_groups(size):
    return [list(range(core, size, 2)) for core in range(2)]


def trade(parts):
    groups = chip_groups(lax.axis_size("rows"))
    return lax.all_to_all(parts, "rows", 0, 0, axis_index_groups=groups)


def all_slices(mine, n):
    return trade(jnp.broadcast_to(mine[None], (n,) + mine.shape))


def across(x, bit):
    return lax.ppermute(x, "rows", [(i, i ^ bit) for i in range(lax.axis_size("rows"))])


def along_pairs(x, sign):
    n_rows, n_pairs = lax.axis_size("rows"), lax.axis_size("pairs")
    route = []
    for r in range(n_rows):
        step = sign if r % 2 else -sign
        for p in range(n_pairs):
            route.append((r * n_pairs + p, r * n_pairs + (p + step) % n_pairs))
    return lax.ppermute(x, ("rows", "pairs"), route)


def body(sample, column_scale, inner_order):
    row, col = lax.axis_index("rows"), lax.axis_index("pairs")
    core = row % 2
    n_pairs = lax.axis_size("pairs")
    rows, width = sample.shape
    height = W // lax.axis_size("rows")
    pair = (shape(rows, N), shape(rows, N))
    own, send = call(start_kernel, pair, [], sample, column_scale.reshape(1, width))
    other = across(send, 1)
    near = along_pairs(jnp.concatenate([own, other], axis=0), 1)
    near_col = (col + jnp.where(core == 0, 1, -1)) % n_pairs

    ids = jnp.arange(height, dtype=jnp.int32)
    row_ids = jnp.concatenate([ids + row * height, ids + (row ^ 1) * height])[:, None]
    places = (jnp.arange(N, dtype=jnp.int32)[None, :] + core * BLOCK) % N + core * N
    unit = jnp.where(row_ids == places + 2 * N * col, 1.0, 0.0).astype(jnp.float32)
    near_unit = jnp.where(row_ids == places + 2 * N * near_col, 1.0, 0.0).astype(jnp.float32)

    order = ((inner_order + core * BLOCK) % N).astype(jnp.float32)
    table = np.eye(N)[:, np.concatenate([arrangement(0), arrangement(ROUNDS)])]
    table = jnp.asarray(table.astype(np.float32))
    along = dot(order, table).reshape(2 * STEPS, N)
    down = along.T

    chips = lax.axis_size("rows") // 2
    gram_rows, mixed_rows = 3 * BLOCK // chips, N // chips
    gram = call(gram_kernel, shape(3, BLOCK, BLOCK), [], own, other)
    parts = trade(gram.reshape(chips, -1, BLOCK))
    blocks = shape(2, BLOCK, BLOCK)
    keep, give = call(mixed_kernel, (blocks, blocks), [], own, other, near)
    got = across(give, 2)
    landed = trade(
        call(
            spread_kernel,
            shape(chips, gram_rows + mixed_rows, BLOCK),
            [],
            parts,
            keep,
            got,
        )
    )
    q, ship = call(
        first_kernel,
        (shape(N, N), shape(N + BLOCK, BLOCK)),
        solve_scratch(1),
        landed,
        along,
        down,
    )
    ship = along_pairs(ship, 1)
    mixed = trade(call(share_kernel, shape(chips, N // chips, BLOCK), [], landed, q))
    half, half_basis = shape(2 * rows, BLOCK), shape(2 * height, BLOCK)
    kept, kept_basis = call(
        keep_kernel,
        (shape(2 * rows + BLOCK, BLOCK), half_basis),
        [],
        landed,
        q,
        own,
        other,
        unit,
    )
    x0, x1, gram, q = call(
        second_kernel,
        (half, half, shape(N, N), shape(N, N)),
        [pltpu.VMEM(half.shape, jnp.float32)] + solve_scratch(1),
        mixed,
        ship,
        kept,
        near,
        along,
        down,
    )

    far0, near1 = along_pairs(x0, -1), along_pairs(x1, 1)
    rest = shape(2 * height + BLOCK, BLOCK)
    rest0, rest1, inner = call(
        basis_kernel,
        (rest, rest, shape(BLOCK, BLOCK)),
        [],
        kept_basis,
        near_unit,
        ship,
        q,
        gram,
    )
    far0, near1, rest0, rest1 = lax.optimization_barrier((far0, near1, rest0, rest1))
    far_rest, near_rest = along_pairs(rest0, -1), along_pairs(rest1, 1)
    cross = call(cross_kernel, shape(5, BLOCK, BLOCK), [], far0, x0, x1, near1)
    sums = trade(cross.reshape(chips, -1, BLOCK)).sum(0)
    sums, far_rest, near_rest = lax.optimization_barrier((sums, far_rest, near_rest))
    sums = all_slices(sums, chips).reshape(5, BLOCK, BLOCK)
    tall = shape(2 * (rows + height), BLOCK)
    theirs, ya, yb, q = call(
        last_kernel,
        (shape(rows + height, N), tall, tall, shape(N, N)),
        solve_scratch(2),
        sums,
        inner,
        far0,
        x0,
        x1,
        near1,
        far_rest,
        rest0,
        rest1,
        near_rest,
        along,
        down,
    )
    got = across(theirs, 1)
    mine_data, mine_basis = call(
        mine_kernel, (shape(rows, N), shape(height, N)), [], ya, yb, q
    )
    return call(
        place_kernel,
        (shape(rows, width), shape(height, width)),
        [],
        got,
        mine_data,
        mine_basis,
    )


def solution(mesh):
    return jax.shard_map(
        body,
        mesh=mesh,
        in_specs=(P("rows", "pairs"), P("pairs"), P()),
        out_specs=(P("rows", "pairs"), P("rows", "pairs")),
        check_vma=False,
    )
```

```python
import functools

import jax
import jax.numpy as jnp
import numpy as np
from jax import lax
from jax.experimental import pallas as pl
from jax.experimental.pallas import tpu as pltpu
from jax.sharding import PartitionSpec as P

BLOCK = 128
N = 2 * BLOCK
W = 4096
STEPS = 4
ROUNDS = 8
HIGHEST = lax.Precision.HIGHEST
VMEM = pl.BlockSpec(memory_space=pltpu.VMEM)


def arrangement(r):
    m = N - 1
    first = [m] + [(r + i) % m for i in range(1, BLOCK)]
    second = [r % m] + [(r - i) % m for i in range(1, BLOCK)]
    return np.array(first + second)


def shape(*dims):
    return jax.ShapeDtypeStruct(dims, jnp.float32)


def call(kernel, out_shape, scratch, *operands):
    return pl.pallas_call(
        kernel,
        out_shape=out_shape,
        in_specs=[VMEM] * len(operands),
        out_specs=jax.tree.map(lambda _: VMEM, out_shape),
        scratch_shapes=scratch,
        compiler_params=pltpu.CompilerParams(vmem_limit_bytes=40 * 2**20),
    )(*operands)


def solve_scratch(count):
    block = pltpu.VMEM((2, count, BLOCK + 16, BLOCK), jnp.float32)
    return [block] * 8


def dot(left, right):
    return jnp.dot(left, right, precision=HIGHEST, preferred_element_type=jnp.float32)


def dot_t(left, right):
    return lax.dot_general(
        left,
        right,
        (((0,), (0,)), ((), ())),
        precision=HIGHEST,
        preferred_element_type=jnp.float32,
    )


def beside(*parts):
    return jnp.concatenate(parts, axis=1)


def joined(g00, g01, g11):
    return jnp.concatenate([beside(g00, g01), beside(g01.T, g11)], axis=0)


def thirds(x):
    high = x.astype(jnp.bfloat16)
    rest = x - high.astype(jnp.float32)
    middle = rest.astype(jnp.bfloat16)
    return high, middle, (rest - middle.astype(jnp.float32)).astype(jnp.bfloat16)


def dot_16(left, right):
    return jnp.dot(left, right, preferred_element_type=jnp.float32)


def pick_columns(x, units):
    high, middle, low = thirds(x)
    return dot_16(high, units) + (dot_16(middle, units) + dot_16(low, units))


def pick_rows(units, x):
    high, middle, low = thirds(x)
    return dot_16(units, high) + (dot_16(units, middle) + dot_16(units, low))


def dot_3(left, right):
    l_high, l_low, _ = thirds(left)
    r_high, r_low, _ = thirds(right)
    return dot_16(l_high, r_high) + (dot_16(l_high, r_low) + dot_16(l_low, r_high))


def turn(p, q, c, s):
    return c * p - s * q, s * p + c * q


def advance(p, q):
    at = lax.broadcasted_iota(jnp.int32, p.shape, 1)
    p_back = pltpu.roll(p, BLOCK - 1, 1)
    q_on = pltpu.roll(q, 1, 1)
    new_p = jnp.where(at == 0, p, jnp.where(at == BLOCK - 1, q, p_back))
    new_q = jnp.where(at == 0, p_back, q_on)
    return new_p, new_q


def angles(gpp, cross, gqq):
    d = gqq - gpp
    root = jnp.sqrt(d * d + 4.0 * cross * cross)
    t = 2.0 * cross * d / ((jnp.abs(d) + root) * root + 1e-06 * (gpp + gqq) * (gpp + gqq))
    w = 1.0 + t * t
    c = lax.rsqrt(w)
    c = c * (1.5 - 0.5 * w * c * c)
    return c, t * c


def solves(grams, step, along_ref, down_ref, scratch, beside_rounds=None):
    along = along_ref[2 * step : 2 * step + 1]
    down = down_ref[:, 2 * step : 2 * step + 2]
    ga, gb, gc, gd, qa, qb, qc, qd = scratch
    count = len(grams)
    lane = lax.broadcasted_iota(jnp.int32, (N, N), 1).astype(jnp.float32)
    sub = lax.broadcasted_iota(jnp.int32, (N, N), 0).astype(jnp.float32)
    take = jnp.where(sub == along, 1.0, 0.0).astype(jnp.bfloat16)
    take_t = jnp.where(lane == down[:, 0:1], 1.0, 0.0)
    back_t = jnp.where(lane == down[:, 1:2], 1.0, 0.0).astype(jnp.bfloat16)
    i0 = lax.broadcasted_iota(jnp.int32, (BLOCK, BLOCK), 0)
    i1 = lax.broadcasted_iota(jnp.int32, (BLOCK, BLOCK), 1)
    at = lax.broadcasted_iota(jnp.int32, (1, BLOCK), 1)
    body = pl.ds(8, BLOCK)
    state = []
    for k, gram in enumerate(grams):
        placed = pick_rows(take_t.astype(jnp.bfloat16), pick_columns(gram, take))
        a, b = placed[:BLOCK, :BLOCK], placed[:BLOCK, BLOCK:]
        c_, d_ = placed[BLOCK:, :BLOCK], placed[BLOCK:, BLOCK:]
        ga[0, k, body], gb[0, k, body], gc[0, k, body], gd[0, k, body] = a, b, c_, d_
        qa[0, k, body], qb[0, k, body] = take_t[:BLOCK, :BLOCK], take_t[:BLOCK, BLOCK:]
        qc[0, k, body], qd[0, k, body] = take_t[BLOCK:, :BLOCK], take_t[BLOCK:, BLOCK:]
        on = i0 == i1

        def diagonal(m):
            return jnp.sum(jnp.where(on, m, 0.0), axis=0, keepdims=True)

        state.append((diagonal(a), diagonal(b), diagonal(d_)))

    def one_round(old, new, k, gpp, cross, gqq):
        c, s = angles(gpp, cross, gqq)
        a, b, c_, d_ = ga[old, k, body], gb[old, k, body], gc[old, k, body], gd[old, k, body]
        on = i0 == i1
        if count == 1:
            c_col = jnp.sum(jnp.where(on, c, 0.0), axis=1, keepdims=True)
            s_col = jnp.sum(jnp.where(on, s, 0.0), axis=1, keepdims=True)
        else:
            c_col = jnp.broadcast_to(c, (BLOCK, BLOCK)).T
            s_col = jnp.broadcast_to(s, (BLOCK, BLOCK)).T
        low = c * gpp - s * cross
        new_pp = c * low - s * (c * cross - s * gqq)
        new_qq = s * (s * gpp + c * cross) + c * (s * cross + c * gqq)
        new_pp, new_qq = advance(new_pp, new_qq)
        off = (i0 == i1 + 2) | ((i0 == BLOCK - 1) & (i1 == BLOCK - 2))

        def beyond(m):
            return jnp.sum(jnp.where(off, m, 0.0), axis=0, keepdims=True)

        ea, eb, ec, ed = (pltpu.roll(beyond(m), 1, 1) for m in (a, b, c_, d_))
        ra, rb, rc, rd = (pltpu.roll(m[0:1], BLOCK - 1, 1) for m in (a, b, c_, d_))
        end, start = at == BLOCK - 1, at == 0
        cl, sl = pltpu.roll(c, 1, 1), pltpu.roll(s, 1, 1)
        cr, sr = pltpu.roll(c, BLOCK - 1, 1), pltpu.roll(s, BLOCK - 1, 1)
        cu, su = jnp.where(end, s, cr), jnp.where(end, -c, sr)
        main = cu * (sl * ea + cl * eb) - su * (sl * ec + cl * ed)
        tip = c * (cr * ra - sr * rb) - s * (cr * rc - sr * rd)
        new_cross = jnp.where(start, tip, main)
        a, b = advance(*turn(a, b, c, s))
        c_, d_ = advance(*turn(c_, d_, c, s))
        qs = [x[old, k, body] for x in (qa, qc, qb, qd)]
        for first, second, top, bottom in (
            (a, c_, ga, gc),
            (b, d_, gb, gd),
            (qs[0], qs[1], qa, qc),
            (qs[2], qs[3], qb, qd),
        ):
            up, under = turn(first, second, c_col, s_col)
            top[new, k, pl.ds(7, BLOCK)] = up
            top[new, k, pl.ds(8, 1)] = up[0:1]
            top[new, k, pl.ds(BLOCK + 7, 1)] = under[BLOCK - 1 :]
            bottom[new, k, pl.ds(9, BLOCK)] = under
            bottom[new, k, pl.ds(8, 1)] = up[1:2]
        return new_pp, new_cross, new_qq

    def two_rounds(i, state):
        if beside_rounds is not None:
            beside_rounds(i)
        state = [one_round(0, 1, k, *state[k]) for k in range(count)]
        return [one_round(1, 0, k, *state[k]) for k in range(count)]

    if count == 1:
        lax.fori_loop(0, ROUNDS // 2, two_rounds, state)
    else:
        for pair in range(ROUNDS // 2):
            state = two_rounds(pair, state)
    turned = [
        [jnp.concatenate([top[0, k, body], bottom[0, k, body]], axis=0).T for k in range(count)]
        for top, bottom in ((qa, qc), (qb, qd))
    ]
    return [
        pick_columns(jnp.concatenate([turned[0][k], turned[1][k]], axis=0), back_t)
        for k in range(count)
    ]


def on_core_1():
    return lax.axis_index("rows") % 2 == 1


def start_kernel(sample, own, send):
    blocks = [sample[:, k * BLOCK : (k + 1) * BLOCK] for k in range(4)]
    swap = on_core_1()
    for k, far in ((0, 3), (1, 2)):
        at = slice(k * BLOCK, (k + 1) * BLOCK)
        own[:, at] = jnp.where(swap, blocks[far], blocks[k])
        send[:, at] = jnp.where(swap, blocks[k], blocks[far])


def gram_kernel(x, out):
    high, middle, low = thirds(x[...])

    def dot_16_t(left, right):
        return lax.dot_general(
            left, right, (((0,), (0,)), ((), ())), preferred_element_type=jnp.float32
        )

    wide = dot_16_t(high, beside(high, middle, low))
    mixed = wide[:, N : 2 * N] + wide[:, 2 * N :]
    gram = wide[:, :N] + ((mixed + mixed.T) + dot_16_t(middle, middle))
    out[0], out[1], out[2] = gram[:BLOCK, :BLOCK], gram[:BLOCK, BLOCK:], gram[BLOCK:, BLOCK:]


def mixed_kernel(x, near, keep, give):
    mixed = dot_t(near[...], x[...])
    upper = lax.axis_index("rows") // 2 % 2 == 1
    for half in range(2):
        at = slice(half * BLOCK, (half + 1) * BLOCK)
        top, bottom = mixed[:BLOCK, at], mixed[BLOCK:, at]
        keep[half] = jnp.where(upper, bottom, top)
        give[half] = jnp.where(upper, top, bottom)


def spread_kernel(parts, keep, got, out):
    n, m = parts.shape[0], parts.shape[1]
    size = BLOCK // n
    total = parts[0]
    for k in range(1, n):
        total = total + parts[k]
    mixed = [keep[half] + got[half] for half in range(2)]
    for k in range(n):
        out[k, :m] = total
        for half in range(2):
            out[k, pl.ds(m + half * size, size)] = mixed[half][k * size : (k + 1) * size]


def share_kernel(landed, q, out):
    n, m = landed.shape[0], 3 * BLOCK // landed.shape[0]
    size = BLOCK // n
    rows = []
    for upper in range(2):
        total = landed[upper, m:]
        for k in range(upper + 2, n, 2):
            total = total + landed[k, m:]
        rows.append(beside(total[:size], total[size:]))
    mine = dot(jnp.concatenate(rows, axis=0), q[:, :BLOCK])
    for k in range(n):
        out[k] = mine


def first_gram(landed, m):
    sums = landed[:, :m].reshape(3, BLOCK, BLOCK)
    return joined(sums[0], sums[1], sums[2])


def first_kernel(landed, along, down, q_out, *scratch):
    gram = first_gram(landed, 3 * BLOCK // landed.shape[0])
    (q,) = solves([gram], 0, along, down, scratch)
    q_out[...] = q


def ship_kernel(landed, q, ship):
    q1 = q[:, BLOCK:]
    ship[:N] = q1
    ship[N:] = dot_t(q1, dot(first_gram(landed, 3 * BLOCK // landed.shape[0]), q1))


def keep_kernel(landed, q, x, unit, kept, kept_basis):
    q0 = q[:, :BLOCK]
    rows = kept.shape[0] - BLOCK
    kept[:rows] = dot(x[...], q0)
    kept[rows:] = dot_t(q0, dot(first_gram(landed, 3 * BLOCK // landed.shape[0]), q0))
    kept_basis[...] = dot(unit[...], q0)


def second_kernel(mixed, ship, kept, near, along, down, x0, x1, gram_out, q_out, turned1, *scratch):
    q1 = ship[:N]
    size = mixed.shape[1] // 2
    cross = dot_t(mixed[:, :size].reshape(BLOCK, BLOCK), q1[:BLOCK]) + dot_t(
        mixed[:, size:].reshape(BLOCK, BLOCK), q1[BLOCK:]
    )
    rows = near.shape[0]
    gram = joined(kept[rows:], cross, ship[N:])
    gram_out[...] = gram
    part = rows // (ROUNDS // 2)

    def near_rows(k):
        at = pl.ds(pl.multiple_of(k * part, part), part)
        turned1[at] = dot(near[at], ship[:N])

    (turned,) = solves([gram], 1, along, down, scratch, near_rows)
    q_out[...] = turned
    y = dot(beside(kept[:rows], turned1[...]), turned)
    x0[...] = y[:, :BLOCK]
    x1[...] = y[:, BLOCK:]


def basis_kernel(kept, unit, ship, q, gram, far, near, out):
    y = dot(beside(kept[...], dot(unit[...], ship[:N])), q[...])
    g = dot_t(q[...], dot(gram[...], q[...]))
    rows = y.shape[0]
    far[:rows], near[:rows] = y[:, :BLOCK], y[:, BLOCK:]
    far[rows:], near[rows:] = g[:BLOCK, :BLOCK], g[BLOCK:, BLOCK:]
    out[...] = g[:BLOCK, BLOCK:]


def cross_kernel(far0, x0, x1, near1, out):
    f0, n1 = far0[...], near1[...]
    both = dot_t(beside(f0, n1), beside(x1[...], x0[...]))
    out[0] = both[:BLOCK, :BLOCK]
    out[1] = both[BLOCK:, BLOCK:]
    out[2] = both[:BLOCK, BLOCK:]
    out[3] = dot_t(f0, n1)
    out[4] = both[BLOCK:, :BLOCK]


def last_grams(sums, inner, far_rest, rest0, rest1, near_rest):
    basis_rows = far_rest.shape[0] - BLOCK
    gram_a = joined(far_rest[basis_rows:], sums[0], rest1[basis_rows:])
    gram_b = joined(rest0[basis_rows:], sums[1].T, near_rest[basis_rows:])
    return gram_a, gram_b


def third_kernel(sums, far_rest, rest0, rest1, near_rest, along, down, out, *scratch):
    grams = last_grams(sums, None, far_rest, rest0, rest1, near_rest)
    qa, qb = solves(grams, 2, along, down, scratch)
    out[0], out[1] = qa[:, :BLOCK], qb[:, BLOCK:]


def last_kernel(
    sums,
    inner,
    far0,
    x0,
    x1,
    near1,
    far_rest,
    rest0,
    rest1,
    near_rest,
    along,
    down,
    q_in,
    theirs,
    ya,
    yb,
    q_out,
    *scratch,
):
    basis_rows = far_rest.shape[0] - BLOCK
    gram_a, gram_b = last_grams(sums, inner, far_rest, rest0, rest1, near_rest)
    mixed = jnp.concatenate(
        [beside(sums[2], sums[3]), beside(inner[...].T, sums[4].T)], axis=0
    )
    qa, qb = q_in[0], q_in[1]
    left = dot(qa.T, beside(gram_a, mixed))
    gram = joined(dot(left[:, :N], qa), dot(left[:, N:], qb), dot(dot(qb.T, gram_b), qb))
    data_rows = far0.shape[0]

    def quarter(k):
        for first, count, pairs in (
            (0, data_rows, ((far0, x1, qa, ya), (x0, near1, qb, yb))),
            (data_rows, basis_rows, ((far_rest, rest1, qa, ya), (rest0, near_rest, qb, yb))),
        ):
            part = count // (ROUNDS // 2)
            at = pl.ds(pl.multiple_of(k * part, part), part)
            to = pl.ds(pl.multiple_of(first + k * part, part), part)
            for left, right, q, out in pairs:
                out[to] = dot_3(beside(left[at], right[at]), q)

    (q,) = solves([gram], 3, along, down, scratch, quarter)
    q_out[...] = q
    half = data_rows // 2
    theirs[:half] = turned_rows(ya, yb, q, half, half)
    theirs[half:] = turned_rows(ya, yb, q, data_rows + basis_rows // 2, basis_rows // 2)


def turned_rows(ya, yb, q, first, count):
    at = pl.ds(first, count)
    y = dot_3(beside(ya[at], yb[at]), q)
    swap = on_core_1()
    return beside(
        jnp.where(swap, y[:, BLOCK:], y[:, :BLOCK]), jnp.where(swap, y[:, :BLOCK], y[:, BLOCK:])
    )


def mine_kernel(ya, yb, q, data, basis):
    rows, height = data.shape[0], basis.shape[0]
    data[...] = turned_rows(ya, yb, q[...], 0, rows)
    basis[...] = turned_rows(ya, yb, q[...], 2 * rows, height)


def place_kernel(got, mine_data, mine_basis, data, basis):
    swap = on_core_1()
    rows = mine_data.shape[0]
    for mine, theirs, out in (
        (mine_data[...], got[:rows], data),
        (mine_basis[...], got[rows:], basis),
    ):
        out[:, :N] = jnp.where(swap, mine, theirs)
        out[:, N:] = jnp.where(swap, theirs, mine)


def chip_groups(size):
    return [list(range(core, size, 2)) for core in range(2)]


def trade(parts):
    groups = chip_groups(lax.axis_size("rows"))
    return lax.all_to_all(parts, "rows", 0, 0, axis_index_groups=groups)


def all_slices(mine, n):
    return trade(jnp.broadcast_to(mine[None], (n,) + mine.shape))


def across(x, bit):
    return lax.ppermute(x, "rows", [(i, i ^ bit) for i in range(lax.axis_size("rows"))])


def along_pairs(x, sign):
    n_rows, n_pairs = lax.axis_size("rows"), lax.axis_size("pairs")
    route = []
    for r in range(n_rows):
        step = sign if r % 2 else -sign
        for p in range(n_pairs):
            route.append((r * n_pairs + p, r * n_pairs + (p + step) % n_pairs))
    return lax.ppermute(x, ("rows", "pairs"), route)


def body(sample, column_scale, inner_order):
    row, col = lax.axis_index("rows"), lax.axis_index("pairs")
    core = row % 2
    n_pairs = lax.axis_size("pairs")
    rows, width = sample.shape
    height = W // lax.axis_size("rows")
    pair = (shape(rows, N), shape(rows, N))
    own, send = call(start_kernel, pair, [], sample)
    scale = column_scale.reshape(4, BLOCK)
    scale = jnp.where(core == 0, scale[:2], scale[:1:-1]).reshape(1, N)
    x = jnp.concatenate([own, across(send, 1)], axis=0) * scale
    near = along_pairs(x, 1)
    near_col = (col + jnp.where(core == 0, 1, -1)) % n_pairs

    ids = jnp.arange(height, dtype=jnp.int32)
    row_ids = jnp.concatenate([ids + row * height, ids + (row ^ 1) * height])[:, None]
    places = (jnp.arange(N, dtype=jnp.int32)[None, :] + core * BLOCK) % N + core * N
    unit = jnp.where(row_ids == places + 2 * N * col, 1.0, 0.0).astype(jnp.float32)
    near_unit = jnp.where(row_ids == places + 2 * N * near_col, 1.0, 0.0).astype(jnp.float32)

    order = ((inner_order + core * BLOCK) % N).astype(jnp.float32)
    table = np.eye(N)[:, np.concatenate([arrangement(0), arrangement(ROUNDS)])]
    table = jnp.asarray(table.astype(np.float32))
    along = dot(order, table).reshape(2 * STEPS, N)
    down = along.T

    chips = lax.axis_size("rows") // 2
    gram_rows, mixed_rows = 3 * BLOCK // chips, N // chips
    gram = call(gram_kernel, shape(3, BLOCK, BLOCK), [], x)
    parts = trade(gram.reshape(chips, -1, BLOCK))
    blocks = shape(2, BLOCK, BLOCK)
    keep, give = call(mixed_kernel, (blocks, blocks), [], x, near)
    got = across(give, 2)
    landed = trade(
        call(
            spread_kernel,
            shape(chips, gram_rows + mixed_rows, BLOCK),
            [],
            parts,
            keep,
            got,
        )
    )
    q = call(first_kernel, shape(N, N), solve_scratch(1), landed, along, down)
    ship = call(ship_kernel, shape(N + BLOCK, BLOCK), [], landed, q)
    ship = along_pairs(ship, 1)
    mixed = trade(call(share_kernel, shape(chips, N // chips, BLOCK), [], landed, q))
    half, half_basis = shape(2 * rows, BLOCK), shape(2 * height, BLOCK)
    kept, kept_basis = call(
        keep_kernel,
        (shape(2 * rows + BLOCK, BLOCK), half_basis),
        [],
        landed,
        q,
        x,
        unit,
    )
    x0, x1, gram, q = call(
        second_kernel,
        (half, half, shape(N, N), shape(N, N)),
        [pltpu.VMEM(half.shape, jnp.float32)] + solve_scratch(1),
        mixed,
        ship,
        kept,
        near,
        along,
        down,
    )

    far0, near1 = along_pairs(x0, -1), along_pairs(x1, 1)
    rest = shape(2 * height + BLOCK, BLOCK)
    rest0, rest1, inner = call(
        basis_kernel,
        (rest, rest, shape(BLOCK, BLOCK)),
        [],
        kept_basis,
        near_unit,
        ship,
        q,
        gram,
    )
    far0, near1, rest0, rest1 = lax.optimization_barrier((far0, near1, rest0, rest1))
    far_rest, near_rest = along_pairs(rest0, -1), along_pairs(rest1, 1)
    cross = call(cross_kernel, shape(5, BLOCK, BLOCK), [], far0, x0, x1, near1)
    sums = trade(cross.reshape(chips, -1, BLOCK)).sum(0)
    sums, far_rest, near_rest = lax.optimization_barrier((sums, far_rest, near_rest))
    sums = all_slices(sums, chips).reshape(5, BLOCK, BLOCK)
    q = call(
        third_kernel,
        shape(2, N, BLOCK),
        solve_scratch(2),
        sums,
        far_rest,
        rest0,
        rest1,
        near_rest,
        along,
        down,
    )
    tall = shape(2 * (rows + height), BLOCK)
    theirs, ya, yb, q = call(
        last_kernel,
        (shape(rows + height, N), tall, tall, shape(N, N)),
        solve_scratch(1),
        sums,
        inner,
        far0,
        x0,
        x1,
        near1,
        far_rest,
        rest0,
        rest1,
        near_rest,
        along,
        down,
        q,
    )
    got = across(theirs, 1)
    mine_data, mine_basis = call(
        mine_kernel, (shape(rows, N), shape(height, N)), [], ya, yb, q
    )
    return call(
        place_kernel,
        (shape(rows, width), shape(height, width)),
        [],
        got,
        mine_data,
        mine_basis,
    )


def solution(mesh):
    return jax.shard_map(
        body,
        mesh=mesh,
        in_specs=(P("rows", "pairs"), P("pairs"), P()),
        out_specs=(P("rows", "pairs"), P("rows", "pairs")),
        check_vma=False,
    )
```

```python
import functools

import jax
import jax.numpy as jnp
import numpy as np
from jax import lax
from jax.experimental import pallas as pl
from jax.experimental.pallas import tpu as pltpu
from jax.sharding import PartitionSpec as P

BLOCK = 128
N = 2 * BLOCK
W = 4096
STEPS = 4
ROUNDS = 8
HIGHEST = lax.Precision.HIGHEST
VMEM = pl.BlockSpec(memory_space=pltpu.VMEM)


def arrangement(r):
    m = N - 1
    first = [m] + [(r + i) % m for i in range(1, BLOCK)]
    second = [r % m] + [(r - i) % m for i in range(1, BLOCK)]
    return np.array(first + second)


def shape(*dims):
    return jax.ShapeDtypeStruct(dims, jnp.float32)


def call(kernel, out_shape, scratch, *operands):
    return pl.pallas_call(
        kernel,
        out_shape=out_shape,
        in_specs=[VMEM] * len(operands),
        out_specs=jax.tree.map(lambda _: VMEM, out_shape),
        scratch_shapes=scratch,
        compiler_params=pltpu.CompilerParams(vmem_limit_bytes=40 * 2**20),
    )(*operands)


def solve_scratch(count):
    block = pltpu.VMEM((2, count, BLOCK + 16, BLOCK), jnp.float32)
    return [block] * 8


def dot(left, right):
    return jnp.dot(left, right, precision=HIGHEST, preferred_element_type=jnp.float32)


def dot_t(left, right):
    return lax.dot_general(
        left,
        right,
        (((0,), (0,)), ((), ())),
        precision=HIGHEST,
        preferred_element_type=jnp.float32,
    )


def beside(*parts):
    return jnp.concatenate(parts, axis=1)


def joined(g00, g01, g11):
    return jnp.concatenate([beside(g00, g01), beside(g01.T, g11)], axis=0)


def thirds(x):
    high = x.astype(jnp.bfloat16)
    rest = x - high.astype(jnp.float32)
    middle = rest.astype(jnp.bfloat16)
    return high, middle, (rest - middle.astype(jnp.float32)).astype(jnp.bfloat16)


def dot_16(left, right):
    return jnp.dot(left, right, preferred_element_type=jnp.float32)


def pick_columns(x, units):
    high, middle, low = thirds(x)
    return dot_16(high, units) + (dot_16(middle, units) + dot_16(low, units))


def pick_rows(units, x):
    high, middle, low = thirds(x)
    return dot_16(units, high) + (dot_16(units, middle) + dot_16(units, low))


def dot_3(left, right):
    l_high, l_low, _ = thirds(left)
    r_high, r_low, _ = thirds(right)
    return dot_16(l_high, r_high) + (dot_16(l_high, r_low) + dot_16(l_low, r_high))


def turn(p, q, c, s):
    return c * p - s * q, s * p + c * q


def advance(p, q):
    at = lax.broadcasted_iota(jnp.int32, p.shape, 1)
    p_back = pltpu.roll(p, BLOCK - 1, 1)
    q_on = pltpu.roll(q, 1, 1)
    new_p = jnp.where(at == 0, p, jnp.where(at == BLOCK - 1, q, p_back))
    new_q = jnp.where(at == 0, p_back, q_on)
    return new_p, new_q


def angles(gpp, cross, gqq):
    d = gqq - gpp
    root = jnp.sqrt(d * d + 4.0 * cross * cross)
    t = 2.0 * cross * d / ((jnp.abs(d) + root) * root + 1e-06 * (gpp + gqq) * (gpp + gqq))
    w = 1.0 + t * t
    c = lax.rsqrt(w)
    c = c * (1.5 - 0.5 * w * c * c)
    return c, t * c


def solves(grams, step, along_ref, down_ref, scratch, beside_rounds=None):
    along = along_ref[2 * step : 2 * step + 1]
    down = down_ref[:, 2 * step : 2 * step + 2]
    ga, gb, gc, gd, qa, qb, qc, qd = scratch
    count = len(grams)
    lane = lax.broadcasted_iota(jnp.int32, (N, N), 1).astype(jnp.float32)
    sub = lax.broadcasted_iota(jnp.int32, (N, N), 0).astype(jnp.float32)
    take = jnp.where(sub == along, 1.0, 0.0).astype(jnp.bfloat16)
    take_t = jnp.where(lane == down[:, 0:1], 1.0, 0.0)
    back_t = jnp.where(lane == down[:, 1:2], 1.0, 0.0).astype(jnp.bfloat16)
    i0 = lax.broadcasted_iota(jnp.int32, (BLOCK, BLOCK), 0)
    i1 = lax.broadcasted_iota(jnp.int32, (BLOCK, BLOCK), 1)
    at = lax.broadcasted_iota(jnp.int32, (1, BLOCK), 1)
    body = pl.ds(8, BLOCK)
    state = []
    for k, gram in enumerate(grams):
        placed = pick_rows(take_t.astype(jnp.bfloat16), pick_columns(gram, take))
        a, b = placed[:BLOCK, :BLOCK], placed[:BLOCK, BLOCK:]
        c_, d_ = placed[BLOCK:, :BLOCK], placed[BLOCK:, BLOCK:]
        ga[0, k, body], gb[0, k, body], gc[0, k, body], gd[0, k, body] = a, b, c_, d_
        qa[0, k, body], qb[0, k, body] = take_t[:BLOCK, :BLOCK], take_t[:BLOCK, BLOCK:]
        qc[0, k, body], qd[0, k, body] = take_t[BLOCK:, :BLOCK], take_t[BLOCK:, BLOCK:]
        on = i0 == i1

        def diagonal(m):
            return jnp.sum(jnp.where(on, m, 0.0), axis=0, keepdims=True)

        state.append((diagonal(a), diagonal(b), diagonal(d_)))

    def one_round(old, new, k, gpp, cross, gqq):
        c, s = angles(gpp, cross, gqq)
        a, b, c_, d_ = ga[old, k, body], gb[old, k, body], gc[old, k, body], gd[old, k, body]
        on = i0 == i1
        if count == 1:
            c_col = jnp.sum(jnp.where(on, c, 0.0), axis=1, keepdims=True)
            s_col = jnp.sum(jnp.where(on, s, 0.0), axis=1, keepdims=True)
        else:
            c_col = jnp.broadcast_to(c, (BLOCK, BLOCK)).T
            s_col = jnp.broadcast_to(s, (BLOCK, BLOCK)).T
        low = c * gpp - s * cross
        new_pp = c * low - s * (c * cross - s * gqq)
        new_qq = s * (s * gpp + c * cross) + c * (s * cross + c * gqq)
        new_pp, new_qq = advance(new_pp, new_qq)
        off = (i0 == i1 + 2) | ((i0 == BLOCK - 1) & (i1 == BLOCK - 2))

        def beyond(m):
            return jnp.sum(jnp.where(off, m, 0.0), axis=0, keepdims=True)

        ea, eb, ec, ed = (pltpu.roll(beyond(m), 1, 1) for m in (a, b, c_, d_))
        ra, rb, rc, rd = (pltpu.roll(m[0:1], BLOCK - 1, 1) for m in (a, b, c_, d_))
        end, start = at == BLOCK - 1, at == 0
        cl, sl = pltpu.roll(c, 1, 1), pltpu.roll(s, 1, 1)
        cr, sr = pltpu.roll(c, BLOCK - 1, 1), pltpu.roll(s, BLOCK - 1, 1)
        cu, su = jnp.where(end, s, cr), jnp.where(end, -c, sr)
        main = cu * (sl * ea + cl * eb) - su * (sl * ec + cl * ed)
        tip = c * (cr * ra - sr * rb) - s * (cr * rc - sr * rd)
        new_cross = jnp.where(start, tip, main)
        a, b = advance(*turn(a, b, c, s))
        c_, d_ = advance(*turn(c_, d_, c, s))
        qs = [x[old, k, body] for x in (qa, qc, qb, qd)]
        for first, second, top, bottom in (
            (a, c_, ga, gc),
            (b, d_, gb, gd),
            (qs[0], qs[1], qa, qc),
            (qs[2], qs[3], qb, qd),
        ):
            up, under = turn(first, second, c_col, s_col)
            top[new, k, pl.ds(7, BLOCK)] = up
            top[new, k, pl.ds(8, 1)] = up[0:1]
            top[new, k, pl.ds(BLOCK + 7, 1)] = under[BLOCK - 1 :]
            bottom[new, k, pl.ds(9, BLOCK)] = under
            bottom[new, k, pl.ds(8, 1)] = up[1:2]
        return new_pp, new_cross, new_qq

    def two_rounds(i, state):
        if beside_rounds is not None:
            beside_rounds(i)
        state = [one_round(0, 1, k, *state[k]) for k in range(count)]
        return [one_round(1, 0, k, *state[k]) for k in range(count)]

    if count == 1:
        lax.fori_loop(0, ROUNDS // 2, two_rounds, state)
    else:
        for pair in range(ROUNDS // 2):
            state = two_rounds(pair, state)
    turned = [
        [jnp.concatenate([top[0, k, body], bottom[0, k, body]], axis=0).T for k in range(count)]
        for top, bottom in ((qa, qc), (qb, qd))
    ]
    return [
        pick_columns(jnp.concatenate([turned[0][k], turned[1][k]], axis=0), back_t)
        for k in range(count)
    ]


def on_core_1():
    return lax.axis_index("rows") % 2 == 1


def start_kernel(sample, own, send):
    blocks = [sample[:, k * BLOCK : (k + 1) * BLOCK] for k in range(4)]
    swap = on_core_1()
    for k, far in ((0, 3), (1, 2)):
        at = slice(k * BLOCK, (k + 1) * BLOCK)
        own[:, at] = jnp.where(swap, blocks[far], blocks[k])
        send[:, at] = jnp.where(swap, blocks[k], blocks[far])


def gram_kernel(x, out):
    high, middle, low = thirds(x[...])

    def dot_16_t(left, right):
        return lax.dot_general(
            left, right, (((0,), (0,)), ((), ())), preferred_element_type=jnp.float32
        )

    wide = dot_16_t(high, beside(high, middle, low))
    mixed = wide[:, N : 2 * N] + wide[:, 2 * N :]
    gram = wide[:, :N] + ((mixed + mixed.T) + dot_16_t(middle, middle))
    out[0], out[1], out[2] = gram[:BLOCK, :BLOCK], gram[:BLOCK, BLOCK:], gram[BLOCK:, BLOCK:]


def mixed_kernel(x, near, keep, give):
    mixed = dot_t(near[...], x[...])
    upper = lax.axis_index("rows") // 2 % 2 == 1
    for half in range(2):
        at = slice(half * BLOCK, (half + 1) * BLOCK)
        top, bottom = mixed[:BLOCK, at], mixed[BLOCK:, at]
        keep[half] = jnp.where(upper, bottom, top)
        give[half] = jnp.where(upper, top, bottom)


def spread_kernel(parts, keep, got, out):
    n, m = parts.shape[0], parts.shape[1]
    size = BLOCK // n
    total = parts[0]
    for k in range(1, n):
        total = total + parts[k]
    mixed = [keep[half] + got[half] for half in range(2)]
    for k in range(n):
        out[k, :m] = total
        for half in range(2):
            out[k, pl.ds(m + half * size, size)] = mixed[half][k * size : (k + 1) * size]


def share_kernel(landed, q, out):
    n, m = landed.shape[0], 3 * BLOCK // landed.shape[0]
    size = BLOCK // n
    rows = []
    for upper in range(2):
        total = landed[upper, m:]
        for k in range(upper + 2, n, 2):
            total = total + landed[k, m:]
        rows.append(beside(total[:size], total[size:]))
    mine = dot(jnp.concatenate(rows, axis=0), q[:, :BLOCK])
    for k in range(n):
        out[k] = mine


def first_gram(landed, m):
    sums = landed[:, :m].reshape(3, BLOCK, BLOCK)
    return joined(sums[0], sums[1], sums[2])


def first_kernel(landed, along, down, q_out, *scratch):
    gram = first_gram(landed, 3 * BLOCK // landed.shape[0])
    (q,) = solves([gram], 0, along, down, scratch)
    q_out[...] = q


def ship_kernel(landed, q, ship):
    q1 = q[:, BLOCK:]
    ship[:N] = q1
    ship[N:] = dot_t(q1, dot(first_gram(landed, 3 * BLOCK // landed.shape[0]), q1))


def keep_kernel(landed, q, x, unit, kept, kept_basis):
    q0 = q[:, :BLOCK]
    rows = kept.shape[0] - BLOCK
    kept[:rows] = dot(x[...], q0)
    kept[rows:] = dot_t(q0, dot(first_gram(landed, 3 * BLOCK // landed.shape[0]), q0))
    kept_basis[...] = dot(unit[...], q0)


def second_kernel(mixed, ship, kept, near, along, down, x0, x1, gram_out, q_out, turned1, *scratch):
    q1 = ship[:N]
    size = mixed.shape[1] // 2
    cross = dot_t(mixed[:, :size].reshape(BLOCK, BLOCK), q1[:BLOCK]) + dot_t(
        mixed[:, size:].reshape(BLOCK, BLOCK), q1[BLOCK:]
    )
    rows = near.shape[0]
    gram = joined(kept[rows:], cross, ship[N:])
    gram_out[...] = gram
    part = rows // (ROUNDS // 2)

    def near_rows(k):
        at = pl.ds(pl.multiple_of(k * part, part), part)
        turned1[at] = dot(near[at], ship[:N])

    (turned,) = solves([gram], 1, along, down, scratch, near_rows)
    q_out[...] = turned
    y = dot(beside(kept[:rows], turned1[...]), turned)
    x0[...] = y[:, :BLOCK]
    x1[...] = y[:, BLOCK:]


def basis_kernel(kept, unit, ship, q, gram, far, near, out):
    y = dot(beside(kept[...], dot(unit[...], ship[:N])), q[...])
    g = dot_t(q[...], dot(gram[...], q[...]))
    rows = y.shape[0]
    far[:rows], near[:rows] = y[:, :BLOCK], y[:, BLOCK:]
    far[rows:], near[rows:] = g[:BLOCK, :BLOCK], g[BLOCK:, BLOCK:]
    out[...] = g[:BLOCK, BLOCK:]


def cross_kernel(far0, x0, x1, near1, out):
    f0, n1 = far0[...], near1[...]
    both = dot_t(beside(f0, n1), beside(x1[...], x0[...]))
    out[0] = both[:BLOCK, :BLOCK]
    out[1] = both[BLOCK:, BLOCK:]
    out[2] = both[:BLOCK, BLOCK:]
    out[3] = dot_t(f0, n1)
    out[4] = both[BLOCK:, :BLOCK]


def last_grams(sums, inner, far_rest, rest0, rest1, near_rest):
    basis_rows = far_rest.shape[0] - BLOCK
    gram_a = joined(far_rest[basis_rows:], sums[0], rest1[basis_rows:])
    gram_b = joined(rest0[basis_rows:], sums[1].T, near_rest[basis_rows:])
    return gram_a, gram_b


def third_kernel(sums, far_rest, rest0, rest1, near_rest, along, down, out, *scratch):
    grams = last_grams(sums, None, far_rest, rest0, rest1, near_rest)
    qa, qb = solves(grams, 2, along, down, scratch)
    out[0], out[1] = qa[:, :BLOCK], qb[:, BLOCK:]


def last_kernel(
    sums,
    inner,
    far0,
    x0,
    x1,
    near1,
    far_rest,
    rest0,
    rest1,
    near_rest,
    along,
    down,
    q_in,
    theirs,
    ya,
    yb,
    q_out,
    *scratch,
):
    basis_rows = far_rest.shape[0] - BLOCK
    gram_a, gram_b = last_grams(sums, inner, far_rest, rest0, rest1, near_rest)
    mixed = jnp.concatenate(
        [beside(sums[2], sums[3]), beside(inner[...].T, sums[4].T)], axis=0
    )
    qa, qb = q_in[0], q_in[1]
    left = dot(qa.T, beside(gram_a, mixed))
    gram = joined(dot(left[:, :N], qa), dot(left[:, N:], qb), dot(dot(qb.T, gram_b), qb))
    data_rows = far0.shape[0]

    def quarter(k):
        for first, count, pairs in (
            (0, data_rows, ((far0, x1, qa, ya), (x0, near1, qb, yb))),
            (data_rows, basis_rows, ((far_rest, rest1, qa, ya), (rest0, near_rest, qb, yb))),
        ):
            part = count // (ROUNDS // 2)
            at = pl.ds(pl.multiple_of(k * part, part), part)
            to = pl.ds(pl.multiple_of(first + k * part, part), part)
            for left, right, q, out in pairs:
                out[to] = dot_3(beside(left[at], right[at]), q)

    (q,) = solves([gram], 3, along, down, scratch, quarter)
    q_out[...] = q
    half = data_rows // 2
    theirs[:half] = turned_rows(ya, yb, q, half, half)
    theirs[half:] = turned_rows(ya, yb, q, data_rows + basis_rows // 2, basis_rows // 2)


def turned_rows(ya, yb, q, first, count):
    at = pl.ds(first, count)
    y = dot_3(beside(ya[at], yb[at]), q)
    swap = on_core_1()
    return beside(
        jnp.where(swap, y[:, BLOCK:], y[:, :BLOCK]), jnp.where(swap, y[:, :BLOCK], y[:, BLOCK:])
    )


def mine_kernel(ya, yb, q, data, basis):
    rows, height = data.shape[0], basis.shape[0]
    data[...] = turned_rows(ya, yb, q[...], 0, rows)
    basis[...] = turned_rows(ya, yb, q[...], 2 * rows, height)


def place_kernel(got, mine_data, mine_basis, data, basis):
    swap = on_core_1()
    rows = mine_data.shape[0]
    for mine, theirs, out in (
        (mine_data[...], got[:rows], data),
        (mine_basis[...], got[rows:], basis),
    ):
        out[:, :N] = jnp.where(swap, mine, theirs)
        out[:, N:] = jnp.where(swap, theirs, mine)


def chip_groups(size):
    return [list(range(core, size, 2)) for core in range(2)]


def trade(parts):
    groups = chip_groups(lax.axis_size("rows"))
    return lax.all_to_all(parts, "rows", 0, 0, axis_index_groups=groups)


def all_slices(mine, n):
    return trade(jnp.broadcast_to(mine[None], (n,) + mine.shape))


def across(x, bit):
    return lax.ppermute(x, "rows", [(i, i ^ bit) for i in range(lax.axis_size("rows"))])


def along_pairs(x, sign):
    n_rows, n_pairs = lax.axis_size("rows"), lax.axis_size("pairs")
    route = []
    for r in range(n_rows):
        step = sign if r % 2 else -sign
        for p in range(n_pairs):
            route.append((r * n_pairs + p, r * n_pairs + (p + step) % n_pairs))
    return lax.ppermute(x, ("rows", "pairs"), route)


def body(sample, column_scale, inner_order):
    row, col = lax.axis_index("rows"), lax.axis_index("pairs")
    core = row % 2
    n_pairs = lax.axis_size("pairs")
    rows, width = sample.shape
    height = W // lax.axis_size("rows")
    pair = (shape(rows, N), shape(rows, N))
    own, send = call(start_kernel, pair, [], sample)
    scale = column_scale.reshape(4, BLOCK)
    scale = jnp.where(core == 0, scale[:2], scale[:1:-1]).reshape(1, N)
    x = jnp.concatenate([own, across(send, 1)], axis=0) * scale
    near = along_pairs(x, 1)
    near_col = (col + jnp.where(core == 0, 1, -1)) % n_pairs

    ids = jnp.arange(height, dtype=jnp.int32)
    row_ids = jnp.concatenate([ids + row * height, ids + (row ^ 1) * height])[:, None]
    places = (jnp.arange(N, dtype=jnp.int32)[None, :] + core * BLOCK) % N + core * N
    unit = jnp.where(row_ids == places + 2 * N * col, 1.0, 0.0).astype(jnp.float32)
    near_unit = jnp.where(row_ids == places + 2 * N * near_col, 1.0, 0.0).astype(jnp.float32)

    near, inner_order = lax.optimization_barrier((near, inner_order))
    order = ((inner_order + core * BLOCK) % N).astype(jnp.float32)
    table = np.eye(N)[:, np.concatenate([arrangement(0), arrangement(ROUNDS)])]
    table = jnp.asarray(table.astype(np.float32))
    along = dot(order, table).reshape(2 * STEPS, N)
    down = along.T

    chips = lax.axis_size("rows") // 2
    gram_rows, mixed_rows = 3 * BLOCK // chips, N // chips
    gram = call(gram_kernel, shape(3, BLOCK, BLOCK), [], x)
    parts = trade(gram.reshape(chips, -1, BLOCK))
    blocks = shape(2, BLOCK, BLOCK)
    keep, give = call(mixed_kernel, (blocks, blocks), [], x, near)
    got = across(give, 2)
    keep, got, along, down, unit, near_unit = lax.optimization_barrier(
        (keep, got, along, down, unit, near_unit)
    )
    landed = trade(
        call(
            spread_kernel,
            shape(chips, gram_rows + mixed_rows, BLOCK),
            [],
            parts,
            keep,
            got,
        )
    )
    q = call(first_kernel, shape(N, N), solve_scratch(1), landed, along, down)
    ship = call(ship_kernel, shape(N + BLOCK, BLOCK), [], landed, q)
    ship = along_pairs(ship, 1)
    mixed = trade(call(share_kernel, shape(chips, N // chips, BLOCK), [], landed, q))
    half, half_basis = shape(2 * rows, BLOCK), shape(2 * height, BLOCK)
    kept, kept_basis = call(
        keep_kernel,
        (shape(2 * rows + BLOCK, BLOCK), half_basis),
        [],
        landed,
        q,
        x,
        unit,
    )
    x0, x1, gram, q = call(
        second_kernel,
        (half, half, shape(N, N), shape(N, N)),
        [pltpu.VMEM(half.shape, jnp.float32)] + solve_scratch(1),
        mixed,
        ship,
        kept,
        near,
        along,
        down,
    )

    far0, near1 = along_pairs(x0, -1), along_pairs(x1, 1)
    rest = shape(2 * height + BLOCK, BLOCK)
    rest0, rest1, inner = call(
        basis_kernel,
        (rest, rest, shape(BLOCK, BLOCK)),
        [],
        kept_basis,
        near_unit,
        ship,
        q,
        gram,
    )
    far0, near1, rest0, rest1 = lax.optimization_barrier((far0, near1, rest0, rest1))
    cross = call(cross_kernel, shape(5, BLOCK, BLOCK), [], far0, x0, x1, near1)
    sums = trade(cross.reshape(chips, -1, BLOCK)).sum(0)
    sums, rest0, rest1, inner = lax.optimization_barrier((sums, rest0, rest1, inner))
    far_rest, near_rest = along_pairs(rest0, -1), along_pairs(rest1, 1)
    sums = all_slices(sums, chips).reshape(5, BLOCK, BLOCK)
    q = call(
        third_kernel,
        shape(2, N, BLOCK),
        solve_scratch(2),
        sums,
        far_rest,
        rest0,
        rest1,
        near_rest,
        along,
        down,
    )
    tall = shape(2 * (rows + height), BLOCK)
    theirs, ya, yb, q = call(
        last_kernel,
        (shape(rows + height, N), tall, tall, shape(N, N)),
        solve_scratch(1),
        sums,
        inner,
        far0,
        x0,
        x1,
        near1,
        far_rest,
        rest0,
        rest1,
        near_rest,
        along,
        down,
        q,
    )
    got = across(theirs, 1)
    mine_data, mine_basis = call(
        mine_kernel, (shape(rows, N), shape(height, N)), [], ya, yb, q
    )
    return call(
        place_kernel,
        (shape(rows, width), shape(height, width)),
        [],
        got,
        mine_data,
        mine_basis,
    )


def solution(mesh):
    return jax.shard_map(
        body,
        mesh=mesh,
        in_specs=(P("rows", "pairs"), P("pairs"), P()),
        out_specs=(P("rows", "pairs"), P("rows", "pairs")),
        check_vma=False,
    )
```

```python
import functools

import jax
import jax.numpy as jnp
import numpy as np
from jax import lax
from jax.experimental import pallas as pl
from jax.experimental.pallas import tpu as pltpu
from jax.sharding import PartitionSpec as P

BLOCK = 128
N = 2 * BLOCK
W = 4096
STEPS = 4
ROUNDS = 8
HIGHEST = lax.Precision.HIGHEST
VMEM = pl.BlockSpec(memory_space=pltpu.VMEM)


def arrangement(r):
    m = N - 1
    first = [m] + [(r + i) % m for i in range(1, BLOCK)]
    second = [r % m] + [(r - i) % m for i in range(1, BLOCK)]
    return np.array(first + second)


def shape(*dims):
    return jax.ShapeDtypeStruct(dims, jnp.float32)


def call(kernel, out_shape, scratch, *operands):
    return pl.pallas_call(
        kernel,
        out_shape=out_shape,
        in_specs=[VMEM] * len(operands),
        out_specs=jax.tree.map(lambda _: VMEM, out_shape),
        scratch_shapes=scratch,
        compiler_params=pltpu.CompilerParams(vmem_limit_bytes=40 * 2**20),
    )(*operands)


def solve_scratch(count):
    block = pltpu.VMEM((2, count, BLOCK + 16, BLOCK), jnp.float32)
    return [block] * 8


def dot(left, right):
    return jnp.dot(left, right, precision=HIGHEST, preferred_element_type=jnp.float32)


def dot_t(left, right):
    return lax.dot_general(
        left,
        right,
        (((0,), (0,)), ((), ())),
        precision=HIGHEST,
        preferred_element_type=jnp.float32,
    )


def beside(*parts):
    return jnp.concatenate(parts, axis=1)


def joined(g00, g01, g11):
    return jnp.concatenate([beside(g00, g01), beside(g01.T, g11)], axis=0)


def thirds(x):
    high = x.astype(jnp.bfloat16)
    rest = x - high.astype(jnp.float32)
    middle = rest.astype(jnp.bfloat16)
    return high, middle, (rest - middle.astype(jnp.float32)).astype(jnp.bfloat16)


def dot_16(left, right):
    return jnp.dot(left, right, preferred_element_type=jnp.float32)


def pick_columns(x, units):
    high, middle, low = thirds(x)
    return dot_16(high, units) + (dot_16(middle, units) + dot_16(low, units))


def pick_rows(units, x):
    high, middle, low = thirds(x)
    return dot_16(units, high) + (dot_16(units, middle) + dot_16(units, low))


def dot_3(left, right):
    l_high, l_low, _ = thirds(left)
    r_high, r_low, _ = thirds(right)
    return dot_16(l_high, r_high) + (dot_16(l_high, r_low) + dot_16(l_low, r_high))


def turn(p, q, c, s):
    return c * p - s * q, s * p + c * q


def advance(p, q):
    at = lax.broadcasted_iota(jnp.int32, p.shape, 1)
    p_back = pltpu.roll(p, BLOCK - 1, 1)
    q_on = pltpu.roll(q, 1, 1)
    new_p = jnp.where(at == 0, p, jnp.where(at == BLOCK - 1, q, p_back))
    new_q = jnp.where(at == 0, p_back, q_on)
    return new_p, new_q


def angles(gpp, cross, gqq):
    d = gqq - gpp
    root = jnp.sqrt(d * d + 4.0 * cross * cross)
    t = 2.0 * cross * d / ((jnp.abs(d) + root) * root + 1e-06 * (gpp + gqq) * (gpp + gqq))
    w = 1.0 + t * t
    c = lax.rsqrt(w)
    c = c * (1.5 - 0.5 * w * c * c)
    return c, t * c


def solves(grams, step, along_ref, down_ref, scratch, beside_rounds=None):
    along = along_ref[2 * step : 2 * step + 1]
    down = down_ref[:, 2 * step : 2 * step + 2]
    ga, gb, gc, gd, qa, qb, qc, qd = scratch
    count = len(grams)
    lane = lax.broadcasted_iota(jnp.int32, (N, N), 1).astype(jnp.float32)
    sub = lax.broadcasted_iota(jnp.int32, (N, N), 0).astype(jnp.float32)
    take = jnp.where(sub == along, 1.0, 0.0).astype(jnp.bfloat16)
    take_t = jnp.where(lane == down[:, 0:1], 1.0, 0.0)
    back_t = jnp.where(lane == down[:, 1:2], 1.0, 0.0).astype(jnp.bfloat16)
    i0 = lax.broadcasted_iota(jnp.int32, (BLOCK, BLOCK), 0)
    i1 = lax.broadcasted_iota(jnp.int32, (BLOCK, BLOCK), 1)
    at = lax.broadcasted_iota(jnp.int32, (1, BLOCK), 1)
    body = pl.ds(8, BLOCK)
    state = []
    for k, gram in enumerate(grams):
        placed = pick_rows(take_t.astype(jnp.bfloat16), pick_columns(gram, take))
        a, b = placed[:BLOCK, :BLOCK], placed[:BLOCK, BLOCK:]
        c_, d_ = placed[BLOCK:, :BLOCK], placed[BLOCK:, BLOCK:]
        ga[0, k, body], gb[0, k, body], gc[0, k, body], gd[0, k, body] = a, b, c_, d_
        qa[0, k, body], qb[0, k, body] = take_t[:BLOCK, :BLOCK], take_t[:BLOCK, BLOCK:]
        qc[0, k, body], qd[0, k, body] = take_t[BLOCK:, :BLOCK], take_t[BLOCK:, BLOCK:]
        on = i0 == i1

        def diagonal(m):
            return jnp.sum(jnp.where(on, m, 0.0), axis=0, keepdims=True)

        state.append((diagonal(a), diagonal(b), diagonal(d_)))

    def one_round(old, new, k, gpp, cross, gqq):
        c, s = angles(gpp, cross, gqq)
        a, b, c_, d_ = ga[old, k, body], gb[old, k, body], gc[old, k, body], gd[old, k, body]
        on = i0 == i1
        if count == 1:
            c_col = jnp.sum(jnp.where(on, c, 0.0), axis=1, keepdims=True)
            s_col = jnp.sum(jnp.where(on, s, 0.0), axis=1, keepdims=True)
        else:
            c_col = jnp.broadcast_to(c, (BLOCK, BLOCK)).T
            s_col = jnp.broadcast_to(s, (BLOCK, BLOCK)).T
        low = c * gpp - s * cross
        new_pp = c * low - s * (c * cross - s * gqq)
        new_qq = s * (s * gpp + c * cross) + c * (s * cross + c * gqq)
        new_pp, new_qq = advance(new_pp, new_qq)
        off = (i0 == i1 + 2) | ((i0 == BLOCK - 1) & (i1 == BLOCK - 2))

        def beyond(m):
            return jnp.sum(jnp.where(off, m, 0.0), axis=0, keepdims=True)

        ea, eb, ec, ed = (pltpu.roll(beyond(m), 1, 1) for m in (a, b, c_, d_))
        ra, rb, rc, rd = (pltpu.roll(m[0:1], BLOCK - 1, 1) for m in (a, b, c_, d_))
        end, start = at == BLOCK - 1, at == 0
        cl, sl = pltpu.roll(c, 1, 1), pltpu.roll(s, 1, 1)
        cr, sr = pltpu.roll(c, BLOCK - 1, 1), pltpu.roll(s, BLOCK - 1, 1)
        cu, su = jnp.where(end, s, cr), jnp.where(end, -c, sr)
        main = cu * (sl * ea + cl * eb) - su * (sl * ec + cl * ed)
        tip = c * (cr * ra - sr * rb) - s * (cr * rc - sr * rd)
        new_cross = jnp.where(start, tip, main)
        a, b = advance(*turn(a, b, c, s))
        c_, d_ = advance(*turn(c_, d_, c, s))
        qs = [x[old, k, body] for x in (qa, qc, qb, qd)]
        for first, second, top, bottom in (
            (a, c_, ga, gc),
            (b, d_, gb, gd),
            (qs[0], qs[1], qa, qc),
            (qs[2], qs[3], qb, qd),
        ):
            up, under = turn(first, second, c_col, s_col)
            top[new, k, pl.ds(7, BLOCK)] = up
            top[new, k, pl.ds(8, 1)] = up[0:1]
            top[new, k, pl.ds(BLOCK + 7, 1)] = under[BLOCK - 1 :]
            bottom[new, k, pl.ds(9, BLOCK)] = under
            bottom[new, k, pl.ds(8, 1)] = up[1:2]
        return new_pp, new_cross, new_qq

    def two_rounds(i, state):
        if beside_rounds is not None:
            beside_rounds(i)
        state = [one_round(0, 1, k, *state[k]) for k in range(count)]
        return [one_round(1, 0, k, *state[k]) for k in range(count)]

    if count == 1:
        def four_rounds(i, held):
            return two_rounds(2 * i + 1, two_rounds(2 * i, held))

        lax.fori_loop(0, ROUNDS // 4, four_rounds, state)
    else:
        for pair in range(ROUNDS // 2):
            state = two_rounds(pair, state)
    turned = [
        [jnp.concatenate([top[0, k, body], bottom[0, k, body]], axis=0).T for k in range(count)]
        for top, bottom in ((qa, qc), (qb, qd))
    ]
    return [
        pick_columns(jnp.concatenate([turned[0][k], turned[1][k]], axis=0), back_t)
        for k in range(count)
    ]


def on_core_1():
    return lax.axis_index("rows") % 2 == 1


def start_kernel(sample, own, send):
    blocks = [sample[:, k * BLOCK : (k + 1) * BLOCK] for k in range(4)]
    swap = on_core_1()
    for k, far in ((0, 3), (1, 2)):
        at = slice(k * BLOCK, (k + 1) * BLOCK)
        own[:, at] = jnp.where(swap, blocks[far], blocks[k])
        send[:, at] = jnp.where(swap, blocks[k], blocks[far])


def gram_kernel(x, out):
    high, middle, low = thirds(x[...])

    def dot_16_t(left, right):
        return lax.dot_general(
            left, right, (((0,), (0,)), ((), ())), preferred_element_type=jnp.float32
        )

    wide = dot_16_t(high, beside(high, middle, low))
    mixed = wide[:, N : 2 * N] + wide[:, 2 * N :]
    gram = wide[:, :N] + ((mixed + mixed.T) + dot_16_t(middle, middle))
    out[0], out[1], out[2] = gram[:BLOCK, :BLOCK], gram[:BLOCK, BLOCK:], gram[BLOCK:, BLOCK:]


def mixed_kernel(x, near, keep, give):
    mixed = dot_t(near[...], x[...])
    upper = lax.axis_index("rows") // 2 % 2 == 1
    for half in range(2):
        at = slice(half * BLOCK, (half + 1) * BLOCK)
        top, bottom = mixed[:BLOCK, at], mixed[BLOCK:, at]
        keep[half] = jnp.where(upper, bottom, top)
        give[half] = jnp.where(upper, top, bottom)


def spread_kernel(parts, keep, got, out):
    n, m = parts.shape[0], parts.shape[1]
    size = BLOCK // n
    total = parts[0]
    for k in range(1, n):
        total = total + parts[k]
    mixed = [keep[half] + got[half] for half in range(2)]
    for k in range(n):
        out[k, :m] = total
        for half in range(2):
            out[k, pl.ds(m + half * size, size)] = mixed[half][k * size : (k + 1) * size]


def share_kernel(landed, q, out):
    n, m = landed.shape[0], 3 * BLOCK // landed.shape[0]
    size = BLOCK // n
    rows = []
    for upper in range(2):
        total = landed[upper, m:]
        for k in range(upper + 2, n, 2):
            total = total + landed[k, m:]
        rows.append(beside(total[:size], total[size:]))
    mine = dot(jnp.concatenate(rows, axis=0), q[:, :BLOCK])
    for k in range(n):
        out[k] = mine


def first_gram(landed, m):
    sums = landed[:, :m].reshape(3, BLOCK, BLOCK)
    return joined(sums[0], sums[1], sums[2])


def first_kernel(landed, along, down, q_out, *scratch):
    gram = first_gram(landed, 3 * BLOCK // landed.shape[0])
    (q,) = solves([gram], 0, along, down, scratch)
    q_out[...] = q


def ship_kernel(landed, q, ship):
    q1 = q[:, BLOCK:]
    ship[:N] = q1
    ship[N:] = dot(dot(q1.T, first_gram(landed, 3 * BLOCK // landed.shape[0])), q1)


def keep_kernel(landed, q, x, unit, kept, kept_basis):
    q0 = q[:, :BLOCK]
    rows = kept.shape[0] - BLOCK
    kept[:rows] = dot(x[...], q0)
    kept[rows:] = dot_t(q0, dot(first_gram(landed, 3 * BLOCK // landed.shape[0]), q0))
    kept_basis[...] = dot(unit[...], q0)


def second_kernel(mixed, ship, kept, near, along, down, x0, x1, gram_out, q_out, turned1, *scratch):
    q1 = ship[:N]
    size = mixed.shape[1] // 2
    halves = [mixed[:, :size].reshape(BLOCK, BLOCK), mixed[:, size:].reshape(BLOCK, BLOCK)]
    cross = dot(jnp.concatenate(halves, axis=0).T, q1)
    rows = near.shape[0]
    gram = joined(kept[rows:], cross, ship[N:])
    gram_out[...] = gram
    part = rows // (ROUNDS // 2)

    def near_rows(k):
        at = pl.ds(pl.multiple_of(k * part, part), part)
        turned1[at] = dot(near[at], ship[:N])

    (turned,) = solves([gram], 1, along, down, scratch, near_rows)
    q_out[...] = turned
    y = dot(beside(kept[:rows], turned1[...]), turned)
    x0[...] = y[:, :BLOCK]
    x1[...] = y[:, BLOCK:]


def basis_kernel(kept, unit, ship, q, gram, far, near, out):
    y = dot(beside(kept[...], dot(unit[...], ship[:N])), q[...])
    g = dot_t(q[...], dot(gram[...], q[...]))
    rows = y.shape[0]
    far[:rows], near[:rows] = y[:, :BLOCK], y[:, BLOCK:]
    far[rows:], near[rows:] = g[:BLOCK, :BLOCK], g[BLOCK:, BLOCK:]
    out[...] = g[:BLOCK, BLOCK:]


def cross_kernel(far0, x0, x1, near1, out):
    f0, n1 = far0[...], near1[...]
    both = dot_t(beside(f0, n1), beside(x1[...], x0[...]))
    out[0] = both[:BLOCK, :BLOCK]
    out[1] = both[BLOCK:, BLOCK:]
    out[2] = both[:BLOCK, BLOCK:]
    out[3] = dot_t(f0, n1)
    out[4] = both[BLOCK:, :BLOCK]


def last_grams(sums, inner, far_rest, rest0, rest1, near_rest):
    basis_rows = far_rest.shape[0] - BLOCK
    gram_a = joined(far_rest[basis_rows:], sums[0], rest1[basis_rows:])
    gram_b = joined(rest0[basis_rows:], sums[1].T, near_rest[basis_rows:])
    return gram_a, gram_b


def third_kernel(sums, far_rest, rest0, rest1, near_rest, along, down, out, *scratch):
    grams = last_grams(sums, None, far_rest, rest0, rest1, near_rest)
    qa, qb = solves(grams, 2, along, down, scratch)
    out[0], out[1] = qa[:, :BLOCK], qb[:, BLOCK:]


def last_kernel(
    sums,
    inner,
    far0,
    x0,
    x1,
    near1,
    far_rest,
    rest0,
    rest1,
    near_rest,
    along,
    down,
    q_in,
    theirs,
    ya,
    yb,
    q_out,
    *scratch,
):
    basis_rows = far_rest.shape[0] - BLOCK
    gram_a, gram_b = last_grams(sums, inner, far_rest, rest0, rest1, near_rest)
    mixed = jnp.concatenate(
        [beside(sums[2], sums[3]), beside(inner[...].T, sums[4].T)], axis=0
    )
    qa, qb = q_in[0], q_in[1]
    left = dot(qa.T, beside(gram_a, mixed))
    gram = joined(dot(left[:, :N], qa), dot(left[:, N:], qb), dot(dot(qb.T, gram_b), qb))
    data_rows = far0.shape[0]

    def quarter(k):
        for first, count, pairs in (
            (0, data_rows, ((far0, x1, qa, ya), (x0, near1, qb, yb))),
            (data_rows, basis_rows, ((far_rest, rest1, qa, ya), (rest0, near_rest, qb, yb))),
        ):
            part = count // (ROUNDS // 2)
            at = pl.ds(pl.multiple_of(k * part, part), part)
            to = pl.ds(pl.multiple_of(first + k * part, part), part)
            for left, right, q, out in pairs:
                out[to] = dot_3(beside(left[at], right[at]), q)

    (q,) = solves([gram], 3, along, down, scratch, quarter)
    q_out[...] = q
    half = data_rows // 2
    theirs[:half] = turned_rows(ya, yb, q, half, half)
    theirs[half:] = turned_rows(ya, yb, q, data_rows + basis_rows // 2, basis_rows // 2)


def turned_rows(ya, yb, q, first, count):
    at = pl.ds(first, count)
    y = dot_3(beside(ya[at], yb[at]), q)
    swap = on_core_1()
    return beside(
        jnp.where(swap, y[:, BLOCK:], y[:, :BLOCK]), jnp.where(swap, y[:, :BLOCK], y[:, BLOCK:])
    )


def mine_kernel(ya, yb, q, data, basis):
    rows, height = data.shape[0], basis.shape[0]
    data[...] = turned_rows(ya, yb, q[...], 0, rows)
    basis[...] = turned_rows(ya, yb, q[...], 2 * rows, height)


def place_kernel(got, mine_data, mine_basis, data, basis):
    swap = on_core_1()
    rows = mine_data.shape[0]
    for mine, theirs, out in (
        (mine_data[...], got[:rows], data),
        (mine_basis[...], got[rows:], basis),
    ):
        out[:, :N] = jnp.where(swap, mine, theirs)
        out[:, N:] = jnp.where(swap, theirs, mine)


def chip_groups(size):
    return [list(range(core, size, 2)) for core in range(2)]


def trade(parts):
    groups = chip_groups(lax.axis_size("rows"))
    return lax.all_to_all(parts, "rows", 0, 0, axis_index_groups=groups)


def all_slices(mine, n):
    return trade(jnp.broadcast_to(mine[None], (n,) + mine.shape))


def across(x, bit):
    return lax.ppermute(x, "rows", [(i, i ^ bit) for i in range(lax.axis_size("rows"))])


def along_pairs(x, sign):
    n_rows, n_pairs = lax.axis_size("rows"), lax.axis_size("pairs")
    route = []
    for r in range(n_rows):
        step = sign if r % 2 else -sign
        for p in range(n_pairs):
            route.append((r * n_pairs + p, r * n_pairs + (p + step) % n_pairs))
    return lax.ppermute(x, ("rows", "pairs"), route)


def body(sample, column_scale, inner_order):
    row, col = lax.axis_index("rows"), lax.axis_index("pairs")
    core = row % 2
    n_pairs = lax.axis_size("pairs")
    rows, width = sample.shape
    height = W // lax.axis_size("rows")
    pair = (shape(rows, N), shape(rows, N))
    own, send = call(start_kernel, pair, [], sample)
    scale = column_scale.reshape(4, BLOCK)
    scale = jnp.where(core == 0, scale[:2], scale[:1:-1]).reshape(1, N)
    x = jnp.concatenate([own, across(send, 1)], axis=0) * scale
    near = along_pairs(x, 1)
    near_col = (col + jnp.where(core == 0, 1, -1)) % n_pairs

    ids = jnp.arange(height, dtype=jnp.int32)
    row_ids = jnp.concatenate([ids + row * height, ids + (row ^ 1) * height])[:, None]
    places = (jnp.arange(N, dtype=jnp.int32)[None, :] + core * BLOCK) % N + core * N
    unit = jnp.where(row_ids == places + 2 * N * col, 1.0, 0.0).astype(jnp.float32)
    near_unit = jnp.where(row_ids == places + 2 * N * near_col, 1.0, 0.0).astype(jnp.float32)

    near, inner_order = lax.optimization_barrier((near, inner_order))
    order = ((inner_order + core * BLOCK) % N).astype(jnp.float32)
    table = np.eye(N)[:, np.concatenate([arrangement(0), arrangement(ROUNDS)])]
    table = jnp.asarray(table.astype(np.float32))
    along = dot(order, table).reshape(2 * STEPS, N)
    down = along.T

    chips = lax.axis_size("rows") // 2
    gram_rows, mixed_rows = 3 * BLOCK // chips, N // chips
    gram = call(gram_kernel, shape(3, BLOCK, BLOCK), [], x)
    parts = trade(gram.reshape(chips, -1, BLOCK))
    blocks = shape(2, BLOCK, BLOCK)
    keep, give = call(mixed_kernel, (blocks, blocks), [], x, near)
    got = across(give, 2)
    keep, got, along, down, unit, near_unit = lax.optimization_barrier(
        (keep, got, along, down, unit, near_unit)
    )
    landed = trade(
        call(
            spread_kernel,
            shape(chips, gram_rows + mixed_rows, BLOCK),
            [],
            parts,
            keep,
            got,
        )
    )
    q = call(first_kernel, shape(N, N), solve_scratch(1), landed, along, down)
    ship = call(ship_kernel, shape(N + BLOCK, BLOCK), [], landed, q)
    ship = along_pairs(ship, 1)
    mixed = trade(call(share_kernel, shape(chips, N // chips, BLOCK), [], landed, q))
    half, half_basis = shape(2 * rows, BLOCK), shape(2 * height, BLOCK)
    kept, kept_basis = call(
        keep_kernel,
        (shape(2 * rows + BLOCK, BLOCK), half_basis),
        [],
        landed,
        q,
        x,
        unit,
    )
    x0, x1, gram, q = call(
        second_kernel,
        (half, half, shape(N, N), shape(N, N)),
        [pltpu.VMEM(half.shape, jnp.float32)] + solve_scratch(1),
        mixed,
        ship,
        kept,
        near,
        along,
        down,
    )

    near1 = along_pairs(x1, 1)
    far0 = along_pairs(x0, -1)
    rest = shape(2 * height + BLOCK, BLOCK)
    rest0, rest1, inner = call(
        basis_kernel,
        (rest, rest, shape(BLOCK, BLOCK)),
        [],
        kept_basis,
        near_unit,
        ship,
        q,
        gram,
    )
    far0, near1, rest0, rest1 = lax.optimization_barrier((far0, near1, rest0, rest1))
    cross = call(cross_kernel, shape(5, BLOCK, BLOCK), [], far0, x0, x1, near1)
    sums = trade(cross.reshape(chips, -1, BLOCK)).sum(0)
    sums, rest0, rest1, inner = lax.optimization_barrier((sums, rest0, rest1, inner))
    far_rest, near_rest = along_pairs(rest0, -1), along_pairs(rest1, 1)
    sums = all_slices(sums, chips).reshape(5, BLOCK, BLOCK)
    q = call(
        third_kernel,
        shape(2, N, BLOCK),
        solve_scratch(2),
        sums,
        far_rest,
        rest0,
        rest1,
        near_rest,
        along,
        down,
    )
    tall = shape(2 * (rows + height), BLOCK)
    theirs, ya, yb, q = call(
        last_kernel,
        (shape(rows + height, N), tall, tall, shape(N, N)),
        solve_scratch(1),
        sums,
        inner,
        far0,
        x0,
        x1,
        near1,
        far_rest,
        rest0,
        rest1,
        near_rest,
        along,
        down,
        q,
    )
    got = across(theirs, 1)
    mine_data, mine_basis = call(
        mine_kernel, (shape(rows, N), shape(height, N)), [], ya, yb, q
    )
    return call(
        place_kernel,
        (shape(rows, width), shape(height, width)),
        [],
        got,
        mine_data,
        mine_basis,
    )


def solution(mesh):
    return jax.shard_map(
        body,
        mesh=mesh,
        in_specs=(P("rows", "pairs"), P("pairs"), P()),
        out_specs=(P("rows", "pairs"), P("rows", "pairs")),
        check_vma=False,
    )
```

```python
import functools

import jax
import jax.numpy as jnp
import numpy as np
from jax import lax
from jax.experimental import pallas as pl
from jax.experimental.pallas import tpu as pltpu
from jax.sharding import PartitionSpec as P

BLOCK = 128
N = 2 * BLOCK
W = 4096
STEPS = 4
ROUNDS = 8
HIGHEST = lax.Precision.HIGHEST
VMEM = pl.BlockSpec(memory_space=pltpu.VMEM)


def arrangement(r):
    m = N - 1
    first = [m] + [(r + i) % m for i in range(1, BLOCK)]
    second = [r % m] + [(r - i) % m for i in range(1, BLOCK)]
    return np.array(first + second)


def shape(*dims):
    return jax.ShapeDtypeStruct(dims, jnp.float32)


def call(kernel, out_shape, scratch, *operands):
    return pl.pallas_call(
        kernel,
        out_shape=out_shape,
        in_specs=[VMEM] * len(operands),
        out_specs=jax.tree.map(lambda _: VMEM, out_shape),
        scratch_shapes=scratch,
        compiler_params=pltpu.CompilerParams(vmem_limit_bytes=40 * 2**20),
    )(*operands)


def solve_scratch(count):
    block = pltpu.VMEM((2, count, BLOCK + 16, BLOCK), jnp.float32)
    return [block] * 8


def dot(left, right):
    return jnp.dot(left, right, precision=HIGHEST, preferred_element_type=jnp.float32)


def dot_t(left, right):
    return lax.dot_general(
        left,
        right,
        (((0,), (0,)), ((), ())),
        precision=HIGHEST,
        preferred_element_type=jnp.float32,
    )


def beside(*parts):
    return jnp.concatenate(parts, axis=1)


def joined(g00, g01, g11):
    return jnp.concatenate([beside(g00, g01), beside(g01.T, g11)], axis=0)


def thirds(x):
    high = x.astype(jnp.bfloat16)
    rest = x - high.astype(jnp.float32)
    middle = rest.astype(jnp.bfloat16)
    return high, middle, (rest - middle.astype(jnp.float32)).astype(jnp.bfloat16)


def dot_16(left, right):
    return jnp.dot(left, right, preferred_element_type=jnp.float32)


def pick_columns(x, units):
    high, middle, low = thirds(x)
    return dot_16(high, units) + (dot_16(middle, units) + dot_16(low, units))


def pick_rows(units, x):
    high, middle, low = thirds(x)
    return dot_16(units, high) + (dot_16(units, middle) + dot_16(units, low))


def dot_3(left, right):
    l_high, l_low, _ = thirds(left)
    r_high, r_low, _ = thirds(right)
    return dot_16(l_high, r_high) + (dot_16(l_high, r_low) + dot_16(l_low, r_high))


def turn(p, q, c, s):
    return c * p - s * q, s * p + c * q


def advance(p, q):
    at = lax.broadcasted_iota(jnp.int32, p.shape, 1)
    p_back = pltpu.roll(p, BLOCK - 1, 1)
    q_on = pltpu.roll(q, 1, 1)
    new_p = jnp.where(at == 0, p, jnp.where(at == BLOCK - 1, q, p_back))
    new_q = jnp.where(at == 0, p_back, q_on)
    return new_p, new_q


def angles(gpp, cross, gqq):
    d = gqq - gpp
    root = jnp.sqrt(d * d + 4.0 * cross * cross)
    t = 2.0 * cross * d / ((jnp.abs(d) + root) * root + 1e-06 * (gpp + gqq) * (gpp + gqq))
    w = 1.0 + t * t
    c = lax.rsqrt(w)
    c = c * (1.5 - 0.5 * w * c * c)
    return c, t * c


def solves(grams, step, along_ref, down_ref, scratch, beside_rounds=None):
    along = along_ref[2 * step : 2 * step + 1]
    down = down_ref[:, 2 * step : 2 * step + 2]
    ga, gb, gc, gd, qa, qb, qc, qd = scratch
    count = len(grams)
    lane = lax.broadcasted_iota(jnp.int32, (N, N), 1).astype(jnp.float32)
    sub = lax.broadcasted_iota(jnp.int32, (N, N), 0).astype(jnp.float32)
    take = jnp.where(sub == along, 1.0, 0.0).astype(jnp.bfloat16)
    take_t = jnp.where(lane == down[:, 0:1], 1.0, 0.0)
    back_t = jnp.where(lane == down[:, 1:2], 1.0, 0.0).astype(jnp.bfloat16)
    i0 = lax.broadcasted_iota(jnp.int32, (BLOCK, BLOCK), 0)
    i1 = lax.broadcasted_iota(jnp.int32, (BLOCK, BLOCK), 1)
    at = lax.broadcasted_iota(jnp.int32, (1, BLOCK), 1)
    body = pl.ds(8, BLOCK)
    state = []
    for k, gram in enumerate(grams):
        placed = pick_rows(take_t.astype(jnp.bfloat16), pick_columns(gram, take))
        a, b = placed[:BLOCK, :BLOCK], placed[:BLOCK, BLOCK:]
        c_, d_ = placed[BLOCK:, :BLOCK], placed[BLOCK:, BLOCK:]
        ga[0, k, body], gb[0, k, body], gc[0, k, body], gd[0, k, body] = a, b, c_, d_
        qa[0, k, body], qb[0, k, body] = take_t[:BLOCK, :BLOCK], take_t[:BLOCK, BLOCK:]
        qc[0, k, body], qd[0, k, body] = take_t[BLOCK:, :BLOCK], take_t[BLOCK:, BLOCK:]
        on = i0 == i1

        def diagonal(m):
            return jnp.sum(jnp.where(on, m, 0.0), axis=0, keepdims=True)

        state.append((diagonal(a), diagonal(b), diagonal(d_)))

    def one_round(old, new, k, gpp, cross, gqq):
        c, s = angles(gpp, cross, gqq)
        a, b, c_, d_ = ga[old, k, body], gb[old, k, body], gc[old, k, body], gd[old, k, body]
        on = i0 == i1
        if count == 1:
            c_col = jnp.sum(jnp.where(on, c, 0.0), axis=1, keepdims=True)
            s_col = jnp.sum(jnp.where(on, s, 0.0), axis=1, keepdims=True)
        else:
            c_col = jnp.broadcast_to(c, (BLOCK, BLOCK)).T
            s_col = jnp.broadcast_to(s, (BLOCK, BLOCK)).T
        low = c * gpp - s * cross
        new_pp = c * low - s * (c * cross - s * gqq)
        new_qq = s * (s * gpp + c * cross) + c * (s * cross + c * gqq)
        new_pp, new_qq = advance(new_pp, new_qq)
        off = (i0 == i1 + 2) | ((i0 == BLOCK - 1) & (i1 == BLOCK - 2))

        def beyond(m):
            return jnp.sum(jnp.where(off, m, 0.0), axis=0, keepdims=True)

        ea, eb, ec, ed = (pltpu.roll(beyond(m), 1, 1) for m in (a, b, c_, d_))
        ra, rb, rc, rd = (pltpu.roll(m[0:1], BLOCK - 1, 1) for m in (a, b, c_, d_))
        end, start = at == BLOCK - 1, at == 0
        cl, sl = pltpu.roll(c, 1, 1), pltpu.roll(s, 1, 1)
        cr, sr = pltpu.roll(c, BLOCK - 1, 1), pltpu.roll(s, BLOCK - 1, 1)
        cu, su = jnp.where(end, s, cr), jnp.where(end, -c, sr)
        main = cu * (sl * ea + cl * eb) - su * (sl * ec + cl * ed)
        tip = c * (cr * ra - sr * rb) - s * (cr * rc - sr * rd)
        new_cross = jnp.where(start, tip, main)
        a, b = advance(*turn(a, b, c, s))
        c_, d_ = advance(*turn(c_, d_, c, s))
        qs = [x[old, k, body] for x in (qa, qc, qb, qd)]
        for first, second, top, bottom in (
            (a, c_, ga, gc),
            (b, d_, gb, gd),
            (qs[0], qs[1], qa, qc),
            (qs[2], qs[3], qb, qd),
        ):
            up, under = turn(first, second, c_col, s_col)
            top[new, k, pl.ds(7, BLOCK)] = up
            top[new, k, pl.ds(8, 1)] = up[0:1]
            top[new, k, pl.ds(BLOCK + 7, 1)] = under[BLOCK - 1 :]
            bottom[new, k, pl.ds(9, BLOCK)] = under
            bottom[new, k, pl.ds(8, 1)] = up[1:2]
        return new_pp, new_cross, new_qq

    def two_rounds(i, state):
        if beside_rounds is not None:
            beside_rounds(i)
        state = [one_round(0, 1, k, *state[k]) for k in range(count)]
        return [one_round(1, 0, k, *state[k]) for k in range(count)]

    if count == 1:
        def four_rounds(i, held):
            return two_rounds(2 * i + 1, two_rounds(2 * i, held))

        lax.fori_loop(0, ROUNDS // 4, four_rounds, state)
    else:
        for pair in range(ROUNDS // 2):
            state = two_rounds(pair, state)
    turned = [
        [jnp.concatenate([top[0, k, body], bottom[0, k, body]], axis=0).T for k in range(count)]
        for top, bottom in ((qa, qc), (qb, qd))
    ]
    return [
        pick_columns(jnp.concatenate([turned[0][k], turned[1][k]], axis=0), back_t)
        for k in range(count)
    ]


def on_core_1():
    return lax.axis_index("rows") % 2 == 1


def start_kernel(sample, own, send):
    blocks = [sample[:, k * BLOCK : (k + 1) * BLOCK] for k in range(4)]
    swap = on_core_1()
    for k, far in ((0, 3), (1, 2)):
        at = slice(k * BLOCK, (k + 1) * BLOCK)
        own[:, at] = jnp.where(swap, blocks[far], blocks[k])
        send[:, at] = jnp.where(swap, blocks[k], blocks[far])


def gram_kernel(x, out):
    high, middle, low = thirds(x[...])

    def dot_16_t(left, right):
        return lax.dot_general(
            left, right, (((0,), (0,)), ((), ())), preferred_element_type=jnp.float32
        )

    wide = dot_16_t(high, beside(high, middle, low))
    mixed = wide[:, N : 2 * N] + wide[:, 2 * N :]
    gram = wide[:, :N] + ((mixed + mixed.T) + dot_16_t(middle, middle))
    out[0], out[1], out[2] = gram[:BLOCK, :BLOCK], gram[:BLOCK, BLOCK:], gram[BLOCK:, BLOCK:]


def mixed_kernel(x, near, keep, give):
    mixed = dot_t(near[...], x[...])
    upper = lax.axis_index("rows") // 2 % 2 == 1
    for half in range(2):
        at = slice(half * BLOCK, (half + 1) * BLOCK)
        top, bottom = mixed[:BLOCK, at], mixed[BLOCK:, at]
        keep[half] = jnp.where(upper, bottom, top)
        give[half] = jnp.where(upper, top, bottom)


def spread_kernel(parts, keep, got, out):
    n, m = parts.shape[0], parts.shape[1]
    size = BLOCK // n
    total = parts[0]
    for k in range(1, n):
        total = total + parts[k]
    mixed = [keep[half] + got[half] for half in range(2)]
    for k in range(n):
        out[k, :m] = total
        for half in range(2):
            out[k, pl.ds(m + half * size, size)] = mixed[half][k * size : (k + 1) * size]


def share_kernel(landed, q, out):
    n, m = landed.shape[0], 3 * BLOCK // landed.shape[0]
    size = BLOCK // n
    rows = []
    for upper in range(2):
        total = landed[upper, m:]
        for k in range(upper + 2, n, 2):
            total = total + landed[k, m:]
        rows.append(beside(total[:size], total[size:]))
    mine = dot(jnp.concatenate(rows, axis=0), q[:, :BLOCK])
    for k in range(n):
        out[k] = mine


def first_gram(landed, m):
    sums = landed[:, :m].reshape(3, BLOCK, BLOCK)
    return joined(sums[0], sums[1], sums[2])


def first_kernel(landed, along, down, q_out, *scratch):
    gram = first_gram(landed, 3 * BLOCK // landed.shape[0])
    (q,) = solves([gram], 0, along, down, scratch)
    q_out[...] = q


def ship_kernel(landed, q, ship):
    q1 = q[:, BLOCK:]
    ship[:N] = q1
    ship[N:] = dot(dot(q1.T, first_gram(landed, 3 * BLOCK // landed.shape[0])), q1)


def keep_kernel(landed, q, x, unit, kept, kept_basis):
    q0 = q[:, :BLOCK]
    rows = kept.shape[0] - BLOCK
    kept[:rows] = dot(x[...], q0)
    kept[rows:] = dot_t(q0, dot(first_gram(landed, 3 * BLOCK // landed.shape[0]), q0))
    kept_basis[...] = dot(unit[...], q0)


def second_kernel(mixed, ship, kept, near, along, down, x0, x1, gram_out, q_out, turned1, *scratch):
    q1 = ship[:N]
    size = mixed.shape[1] // 2
    halves = [mixed[:, :size].reshape(BLOCK, BLOCK), mixed[:, size:].reshape(BLOCK, BLOCK)]
    cross = dot(jnp.concatenate(halves, axis=0).T, q1)
    rows = near.shape[0]
    gram = joined(kept[rows:], cross, ship[N:])
    gram_out[...] = gram
    part = rows // (ROUNDS // 2)

    def near_rows(k):
        at = pl.ds(pl.multiple_of(k * part, part), part)
        turned1[at] = dot(near[at], ship[:N])

    (turned,) = solves([gram], 1, along, down, scratch, near_rows)
    q_out[...] = turned
    y = dot(beside(kept[:rows], turned1[...]), turned)
    x0[...] = y[:, :BLOCK]
    x1[...] = y[:, BLOCK:]


def basis_kernel(kept, unit, ship, q, gram, far, near, out):
    y = dot(beside(kept[...], dot(unit[...], ship[:N])), q[...])
    g = dot_t(q[...], dot(gram[...], q[...]))
    rows = y.shape[0]
    far[:rows], near[:rows] = y[:, :BLOCK], y[:, BLOCK:]
    far[rows:], near[rows:] = g[:BLOCK, :BLOCK], g[BLOCK:, BLOCK:]
    out[...] = g[:BLOCK, BLOCK:]


def cross_kernel(far0, x0, x1, near1, out):
    f0, n1 = far0[...], near1[...]
    both = dot_t(beside(f0, n1), beside(x1[...], x0[...]))
    out[0] = both[:BLOCK, :BLOCK]
    out[1] = both[BLOCK:, BLOCK:]
    out[2] = both[:BLOCK, BLOCK:]
    out[3] = dot_t(f0, n1)
    out[4] = both[BLOCK:, :BLOCK]


def last_grams(sums, inner, far_rest, rest0, rest1, near_rest):
    basis_rows = far_rest.shape[0] - BLOCK
    gram_a = joined(far_rest[basis_rows:], sums[0], rest1[basis_rows:])
    gram_b = joined(rest0[basis_rows:], sums[1].T, near_rest[basis_rows:])
    return gram_a, gram_b


def third_kernel(sums, far_rest, rest0, rest1, near_rest, along, down, out, *scratch):
    grams = last_grams(sums, None, far_rest, rest0, rest1, near_rest)
    qa, qb = solves(grams, 2, along, down, scratch)
    out[0], out[1] = qa[:, :BLOCK], qb[:, BLOCK:]


def last_kernel(
    sums,
    inner,
    far0,
    x0,
    x1,
    near1,
    far_rest,
    rest0,
    rest1,
    near_rest,
    along,
    down,
    q_in,
    theirs,
    ya,
    yb,
    q_out,
    *scratch,
):
    basis_rows = far_rest.shape[0] - BLOCK
    gram_a, gram_b = last_grams(sums, inner, far_rest, rest0, rest1, near_rest)
    mixed = jnp.concatenate(
        [beside(sums[2], sums[3]), beside(inner[...].T, sums[4].T)], axis=0
    )
    qa, qb = q_in[0], q_in[1]
    left = dot(qa.T, beside(gram_a, mixed))
    gram = joined(dot(left[:, :N], qa), dot(left[:, N:], qb), dot(dot(qb.T, gram_b), qb))
    data_rows = far0.shape[0]

    def quarter(k):
        for first, count, pairs in (
            (0, data_rows, ((far0, x1, qa, ya), (x0, near1, qb, yb))),
            (data_rows, basis_rows, ((far_rest, rest1, qa, ya), (rest0, near_rest, qb, yb))),
        ):
            part = count // (ROUNDS // 2)
            at = pl.ds(pl.multiple_of(k * part, part), part)
            to = pl.ds(pl.multiple_of(first + k * part, part), part)
            for left, right, q, out in pairs:
                out[to] = dot_3(beside(left[at], right[at]), q)

    (q,) = solves([gram], 3, along, down, scratch, quarter)
    q_out[...] = q
    half = data_rows // 2
    theirs[:half] = turned_rows(ya, yb, q, half, half)
    theirs[half:] = turned_rows(ya, yb, q, data_rows + basis_rows // 2, basis_rows // 2)


def turned_rows(ya, yb, q, first, count):
    at = pl.ds(first, count)
    y = dot_3(beside(ya[at], yb[at]), q)
    swap = on_core_1()
    return beside(
        jnp.where(swap, y[:, BLOCK:], y[:, :BLOCK]), jnp.where(swap, y[:, :BLOCK], y[:, BLOCK:])
    )


def mine_kernel(ya, yb, q, data, basis):
    rows, height = data.shape[0], basis.shape[0]
    data[...] = turned_rows(ya, yb, q[...], 0, rows)
    basis[...] = turned_rows(ya, yb, q[...], 2 * rows, height)


def place_kernel(got, mine_data, mine_basis, data, basis, sems):
    core = lax.axis_index("rows") % 2
    mine_at = pl.ds(pl.multiple_of((1 - core) * N, N), N)
    got_at = pl.ds(pl.multiple_of(core * N, N), N)
    rows, height = mine_data.shape[0], mine_basis.shape[0]
    pairs = (
        (mine_data, data.at[:, mine_at]),
        (got.at[pl.ds(0, rows)], data.at[:, got_at]),
        (mine_basis, basis.at[:, mine_at]),
        (got.at[pl.ds(rows, height)], basis.at[:, got_at]),
    )
    copies = [
        pltpu.make_async_copy(source, target, sems.at[k])
        for k, (source, target) in enumerate(pairs)
    ]
    for copy in copies:
        copy.start()
    for copy in copies:
        copy.wait()


def place(got, mine_data, mine_basis, width):
    rows, height = mine_data.shape[0], mine_basis.shape[0]
    out = pl.BlockSpec(memory_space=pl.ANY)
    return pl.pallas_call(
        place_kernel,
        out_shape=(shape(rows, width), shape(height, width)),
        in_specs=[VMEM] * 3,
        out_specs=(out, out),
        scratch_shapes=[pltpu.SemaphoreType.DMA((4,))],
        compiler_params=pltpu.CompilerParams(vmem_limit_bytes=40 * 2**20),
    )(got, mine_data, mine_basis)


def chip_groups(size):
    return [list(range(core, size, 2)) for core in range(2)]


def trade(parts):
    groups = chip_groups(lax.axis_size("rows"))
    return lax.all_to_all(parts, "rows", 0, 0, axis_index_groups=groups)


def all_slices(mine, n):
    return trade(jnp.broadcast_to(mine[None], (n,) + mine.shape))


def across(x, bit):
    return lax.ppermute(x, "rows", [(i, i ^ bit) for i in range(lax.axis_size("rows"))])


def along_pairs(x, sign):
    n_rows, n_pairs = lax.axis_size("rows"), lax.axis_size("pairs")
    route = []
    for r in range(n_rows):
        step = sign if r % 2 else -sign
        for p in range(n_pairs):
            route.append((r * n_pairs + p, r * n_pairs + (p + step) % n_pairs))
    return lax.ppermute(x, ("rows", "pairs"), route)


def body(sample, column_scale, inner_order):
    row, col = lax.axis_index("rows"), lax.axis_index("pairs")
    core = row % 2
    n_pairs = lax.axis_size("pairs")
    rows, width = sample.shape
    height = W // lax.axis_size("rows")
    pair = (shape(rows, N), shape(rows, N))
    own, send = call(start_kernel, pair, [], sample)
    scale = column_scale.reshape(4, BLOCK)
    scale = jnp.where(core == 0, scale[:2], scale[:1:-1]).reshape(1, N)
    x = jnp.concatenate([own, across(send, 1)], axis=0) * scale
    near = along_pairs(x, 1)
    near_col = (col + jnp.where(core == 0, 1, -1)) % n_pairs

    ids = jnp.arange(height, dtype=jnp.int32)
    row_ids = jnp.concatenate([ids + row * height, ids + (row ^ 1) * height])[:, None]
    places = (jnp.arange(N, dtype=jnp.int32)[None, :] + core * BLOCK) % N + core * N
    unit = jnp.where(row_ids == places + 2 * N * col, 1.0, 0.0).astype(jnp.float32)
    near_unit = jnp.where(row_ids == places + 2 * N * near_col, 1.0, 0.0).astype(jnp.float32)

    near, inner_order = lax.optimization_barrier((near, inner_order))
    order = ((inner_order + core * BLOCK) % N).astype(jnp.float32)
    table = np.eye(N)[:, np.concatenate([arrangement(0), arrangement(ROUNDS)])]
    table = jnp.asarray(table.astype(np.float32))
    along = dot(order, table).reshape(2 * STEPS, N)
    down = along.T

    chips = lax.axis_size("rows") // 2
    gram_rows, mixed_rows = 3 * BLOCK // chips, N // chips
    gram = call(gram_kernel, shape(3, BLOCK, BLOCK), [], x)
    parts = trade(gram.reshape(chips, -1, BLOCK))
    blocks = shape(2, BLOCK, BLOCK)
    keep, give = call(mixed_kernel, (blocks, blocks), [], x, near)
    got = across(give, 2)
    keep, got, along, down, unit, near_unit = lax.optimization_barrier(
        (keep, got, along, down, unit, near_unit)
    )
    landed = trade(
        call(
            spread_kernel,
            shape(chips, gram_rows + mixed_rows, BLOCK),
            [],
            parts,
            keep,
            got,
        )
    )
    q = call(first_kernel, shape(N, N), solve_scratch(1), landed, along, down)
    ship = call(ship_kernel, shape(N + BLOCK, BLOCK), [], landed, q)
    ship = along_pairs(ship, 1)
    mixed = trade(call(share_kernel, shape(chips, N // chips, BLOCK), [], landed, q))
    half, half_basis = shape(2 * rows, BLOCK), shape(2 * height, BLOCK)
    kept, kept_basis = call(
        keep_kernel,
        (shape(2 * rows + BLOCK, BLOCK), half_basis),
        [],
        landed,
        q,
        x,
        unit,
    )
    x0, x1, gram, q = call(
        second_kernel,
        (half, half, shape(N, N), shape(N, N)),
        [pltpu.VMEM(half.shape, jnp.float32)] + solve_scratch(1),
        mixed,
        ship,
        kept,
        near,
        along,
        down,
    )

    near1 = along_pairs(x1, 1)
    far0 = along_pairs(x0, -1)
    rest = shape(2 * height + BLOCK, BLOCK)
    rest0, rest1, inner = call(
        basis_kernel,
        (rest, rest, shape(BLOCK, BLOCK)),
        [],
        kept_basis,
        near_unit,
        ship,
        q,
        gram,
    )
    far0, near1, rest0, rest1 = lax.optimization_barrier((far0, near1, rest0, rest1))
    cross = call(cross_kernel, shape(5, BLOCK, BLOCK), [], far0, x0, x1, near1)
    sums = trade(cross.reshape(chips, -1, BLOCK)).sum(0)
    sums, rest0, rest1, inner = lax.optimization_barrier((sums, rest0, rest1, inner))
    far_rest, near_rest = along_pairs(rest0, -1), along_pairs(rest1, 1)
    sums = all_slices(sums, chips).reshape(5, BLOCK, BLOCK)
    q = call(
        third_kernel,
        shape(2, N, BLOCK),
        solve_scratch(2),
        sums,
        far_rest,
        rest0,
        rest1,
        near_rest,
        along,
        down,
    )
    tall = shape(2 * (rows + height), BLOCK)
    theirs, ya, yb, q = call(
        last_kernel,
        (shape(rows + height, N), tall, tall, shape(N, N)),
        solve_scratch(1),
        sums,
        inner,
        far0,
        x0,
        x1,
        near1,
        far_rest,
        rest0,
        rest1,
        near_rest,
        along,
        down,
        q,
    )
    got = across(theirs, 1)
    mine_data, mine_basis = call(
        mine_kernel, (shape(rows, N), shape(height, N)), [], ya, yb, q
    )
    return place(got, mine_data, mine_basis, width)


def solution(mesh):
    return jax.shard_map(
        body,
        mesh=mesh,
        in_specs=(P("rows", "pairs"), P("pairs"), P()),
        out_specs=(P("rows", "pairs"), P("rows", "pairs")),
        check_vma=False,
    )
```
